128 devices in a mesh: ctx: 16 (over x, z), fsdp: 8 (over y, core).
Axes of the slice: x: 4, y: 4, z: 4, core: 2. Of those that a mesh axis runs over, the one named last changes fastest.
Arguments:
- tokens: bfloat16 [8, 4096, 1024], P('fsdp', 'ctx'), may hold values from -6 to 6
- cotangent: bfloat16 [8, 4096, 1024], P('fsdp', 'ctx'), may hold values from -6 to 6
- lengths: int32 [8, 4], P('fsdp'), may hold values from 1 to 2048, as said below
- input_gain: bfloat16 [1024], P('fsdp'), may hold values from 0.5 to 1.5
- query_weight: bfloat16 [1024, 512], P('fsdp'), may hold values from -0.1875 to 0.1875
- key_weight: bfloat16 [1024, 128], P('fsdp'), may hold values from -0.1875 to 0.1875
- value_weight: bfloat16 [1024, 128], P('fsdp'), may hold values from -0.1875 to 0.1875
- attention_out: bfloat16 [512, 1024], P('fsdp'), may hold values from -1 to 1
- mixer_in: bfloat16 [1024, 3072], P('fsdp'), may hold values from -0.1875 to 0.1875
- state_in: bfloat16 [1024, 256], P('fsdp'), may hold values from -0.046875 to 0.046875
- step_in: bfloat16 [1024, 24], P('fsdp'), may hold values from -0.1875 to 0.1875
- conv_weight: bfloat16 [4, 1792], P(None, 'fsdp'), may hold values from -3 to 3
- conv_bias: bfloat16 [1792], P('fsdp'), may hold values from -2 to 2
- step_bias: bfloat16 [24], P('fsdp'), may hold values from -3 to -0.5
- decay_log: bfloat16 [24], P('fsdp'), may hold values from -4 to -0.5
- skip_gain: bfloat16 [24], P('fsdp'), may hold values from 0.5 to 1.5
- mixer_out: bfloat16 [1536, 1024], P('fsdp'), may hold values from -0.0390625 to 0.0390625
- feed_gain: bfloat16 [1024], P('fsdp'), may hold values from 0.5 to 1.5
- gate_weight: bfloat16 [1024, 2048], P('fsdp'), may hold values from -0.1875 to 0.1875
- up_weight: bfloat16 [1024, 2048], P('fsdp'), may hold values from -0.1875 to 0.1875
- down_weight: bfloat16 [2048, 1024], P('fsdp'), may hold values from -0.125 to 0.125
Outputs:
- output: bfloat16 [8, 4096, 1024], P('fsdp', 'ctx')
- input_grad: float32 [8, 4096, 1024], P('fsdp', 'ctx')
- input_gain_gradient: float32 [1024], P('fsdp')
- query_weight_gradient: float32 [1024, 512], P('fsdp')
- key_weight_gradient: float32 [1024, 128], P('fsdp')
- value_weight_gradient: float32 [1024, 128], P('fsdp')
- attention_out_gradient: float32 [512, 1024], P('fsdp')
- mixer_in_gradient: float32 [1024, 3072], P('fsdp')
- state_in_gradient: float32 [1024, 256], P('fsdp')
- step_in_gradient: float32 [1024, 24], P('fsdp')
- conv_weight_gradient: float32 [4, 1792], P(None, 'fsdp')
- conv_bias_gradient: float32 [1792], P('fsdp')
- step_bias_gradient: float32 [24], P('fsdp')
- decay_log_gradient: float32 [24], P('fsdp')
- skip_gain_gradient: float32 [24], P('fsdp')
- mixer_out_gradient: float32 [1536, 1024], P('fsdp')
- feed_gain_gradient: float32 [1024], P('fsdp')
- gate_weight_gradient: float32 [1024, 2048], P('fsdp')
- up_weight_gradient: float32 [1024, 2048], P('fsdp')
- down_weight_gradient: float32 [2048, 1024], P('fsdp')
The draws below stay inside these ranges and needn't reach their ends.
Inputs may be any that keep to these rules, and one draw needn't show every extreme that they name: In each sequence one document has exactly 2048 positions and is either the first or the last; the lengths of a sequence sum to 4096.
All inputs are finite; a program needn't handle non-finite values.
Results may differ from the reference program's by a relative error of at most 0.019.
The reference program's roundings to bfloat16 on the way count: a program that leaves them out, or rounds other values in their place, can miss the bound.
Values may be sent and summed in bfloat16 or wider, within the bound.
No kernel may reach another device: no remote copies, remote signals or barrier semaphores. Data moves between devices by JAX's collectives and lax.ppermute only.
A program may use at most 256 MiB of HBM per device.

```python
import math
import jax
import jax.numpy as jnp
from jax import lax

D = 1024
HEADS = 8
KV_HEADS = 2
HEAD_DIM = 64
MIX_HEADS = 24
MIX_DIM = 64
STATE = 128
FF = 2048
CONV = 4
DOCS = 4
LB = 128
SEQ_LEN = 4096
SEQS = 8
QW = 512
KW = 128
MIX = 1536
CH = 1792
N_CTX = 16


def draw_lengths(key, part):
    key = jax.random.fold_in(key, 11)
    half_len = SEQ_LEN // 2

    def one_row(row_key):
        cut_key, side_key = jax.random.split(row_key)
        cuts = jnp.sort(jax.random.permutation(cut_key, half_len - 1)[:DOCS - 2] + 1).astype(jnp.int32)
        edges = jnp.concatenate([jnp.zeros((1,), jnp.int32), cuts, jnp.full((1,), half_len, jnp.int32)])
        shorter = edges[1:] - edges[:-1]
        side = jax.random.randint(side_key, (), 0, 2)
        leading = jnp.concatenate([jnp.full((1,), half_len, jnp.int32), shorter])
        trailing = jnp.concatenate([shorter, jnp.full((1,), half_len, jnp.int32)])
        return jnp.where(side == 1, leading, trailing).astype(jnp.int32)
    return jax.vmap(one_row)(jax.random.split(key, SEQS))


def levels(stream_key, shape, shards, least, high):
    def one(axis_at, shards_of):
        steps = jax.random.uniform(jax.random.fold_in(jax.random.fold_in(stream_key, 6), axis_at), (shards_of,), jnp.float32, least / len(shards), high / len(shards))
        return jnp.repeat(jnp.exp(steps), shape[axis_at] // shards_of).reshape((-1,) + (1,) * (len(shape) - axis_at - 1))

    gain = one(*shards[0])
    for cut in shards[1:]:
        gain = gain * one(*cut)
    return gain


def gaussian(key, dims, width, limit, cuts=(), held_as=jnp.bfloat16):
    array = width * jax.random.normal(key, dims, jnp.float32)
    if cuts:
        array = array * levels(key, dims, cuts, -0.22, 0.18)
    return jnp.clip(array, -limit, limit).astype(held_as)


def setup_inputs(seed: int = 0) -> dict:
    key_list = jax.random.split(jax.random.key(seed), 22)
    tokens = gaussian(key_list[0], (SEQS, SEQ_LEN, D), 1.0, 6.0, ((0, 8), (1, 16)))
    cotangent = gaussian(key_list[1], (SEQS, SEQ_LEN, D), 1.0, 6.0, ((0, 8), (1, 16)))
    lengths = draw_lengths(jax.random.fold_in(key_list[21], 71), 0)
    input_gain = jnp.clip(1.0 + 0.1 * jax.random.normal(key_list[3], (D,), jnp.float32), 0.5, 1.5).astype(jnp.bfloat16)
    query_weight = gaussian(key_list[4], (D, QW), D ** -0.5, 0.1875, ((0, 8),))
    key_weight = gaussian(key_list[5], (D, KW), D ** -0.5, 0.1875, ((0, 8),))
    value_weight = gaussian(key_list[6], (D, KW), D ** -0.5, 0.1875, ((0, 8),))
    attention_out = gaussian(key_list[7], (QW, D), 32 ** -0.5, 1.0, ((0, 8),))
    mixer_in = gaussian(key_list[8], (D, 2 * MIX), D ** -0.5, 0.1875, ((0, 8),))
    state_in = gaussian(key_list[9], (D, 2 * STATE), (16 * D) ** -0.5, 0.046875, ((0, 8),))
    step_in = gaussian(key_list[10], (D, MIX_HEADS), D ** -0.5, 0.1875, ((0, 8),))
    conv_weight = gaussian(key_list[11], (CONV, CH), 0.5, 3.0, ((1, 8),))
    conv_bias = gaussian(key_list[12], (CH,), 0.3, 2.0, ((0, 8),))
    step_bias = jnp.clip(-3.0 + 2.5 * jax.random.uniform(key_list[13], (MIX_HEADS,), jnp.float32) ** levels(key_list[13], (MIX_HEADS,), ((0, 8),), -0.2, 0.2), -3.0, -0.5).astype(jnp.bfloat16)
    decay_log = jnp.clip(-4.0 + 3.5 * jax.random.uniform(key_list[14], (MIX_HEADS,), jnp.float32) ** levels(key_list[14], (MIX_HEADS,), ((0, 8),), -0.2, 0.2), -4.0, -0.5).astype(jnp.bfloat16)
    skip_gain = jnp.clip(0.5 + 1.0 * jax.random.uniform(key_list[15], (MIX_HEADS,), jnp.float32) ** levels(key_list[15], (MIX_HEADS,), ((0, 8),), -0.2, 0.2), 0.5, 1.5).astype(jnp.bfloat16)
    mixer_out = gaussian(key_list[16], (MIX, D), (16 * MIX) ** -0.5, 0.0390625, ((0, 8),))
    feed_gain = jnp.clip(1.0 + 0.1 * jax.random.normal(key_list[17], (D,), jnp.float32), 0.5, 1.5).astype(jnp.bfloat16)
    gate_weight = gaussian(key_list[18], (D, FF), D ** -0.5, 0.1875, ((0, 8),))
    up_weight = gaussian(key_list[19], (D, FF), D ** -0.5, 0.1875, ((0, 8),))
    down_weight = gaussian(key_list[20], (FF, D), FF ** -0.5, 0.125, ((0, 8),))
    return {"tokens": tokens, "cotangent": cotangent, "lengths": lengths, "input_gain": input_gain, "query_weight": query_weight, "key_weight": key_weight, "value_weight": value_weight, "attention_out": attention_out, "mixer_in": mixer_in, "state_in": state_in, "step_in": step_in, "conv_weight": conv_weight, "conv_bias": conv_bias, "step_bias": step_bias, "decay_log": decay_log, "skip_gain": skip_gain, "mixer_out": mixer_out, "feed_gain": feed_gain, "gate_weight": gate_weight, "up_weight": up_weight, "down_weight": down_weight}


EPSILON = 1e-05
ROPE_BASE = 100000000000.0
HIGHEST = lax.Precision.HIGHEST

@jax.custom_vjp
def low(v):
    return lax.optimization_barrier(v.astype(jnp.bfloat16)).astype(jnp.float32)

@jax.custom_vjp
def low_back(v):
    return v

def low_keep(v):
    return (low(v), None)

def low_pass(kept, grad):
    return (grad,)

def back_keep(v):
    return (v, None)

def back_low(kept, grad):
    return (low(grad),)
low.defvjp(low_keep, low_pass)
low_back.defvjp(back_keep, back_low)

def product(left, right):
    return jnp.dot(left, right, precision=HIGHEST)

def rms_scale(values, gain_vector):
    return values * lax.rsqrt(lax.optimization_barrier(jnp.mean(values * values, axis=-1, keepdims=True)) + EPSILON) * gain_vector

def rope_tables(places):
    half_dim = HEAD_DIM // 2
    inverse = ROPE_BASE ** (-jnp.arange(half_dim, dtype=jnp.float32) / half_dim)
    angles = places.astype(jnp.float32)[:, None] * inverse[None, :]
    return (jnp.cos(angles), jnp.sin(angles))

def rotate(values, cosine, sine_part, head_count):
    token_count = values.shape[0]
    half_dim = HEAD_DIM // 2
    shaped = values.reshape(token_count, head_count, HEAD_DIM)
    lower_half = shaped[:, :, :half_dim]
    upper_half = shaped[:, :, half_dim:]
    cos_rows = cosine[:, None, :]
    sin_rows = sine_part[:, None, :]
    turned = jnp.concatenate([lower_half * cos_rows - upper_half * sin_rows, upper_half * cos_rows + lower_half * sin_rows], axis=-1)
    return turned.reshape(token_count, head_count * HEAD_DIM)

def document_ids(bounds, places):
    found_ids = lax.optimization_barrier(jnp.sum((places[:, None] >= bounds[None, :-1]).astype(jnp.int32), axis=1))
    return jnp.where(places >= 0, found_ids, -1).astype(jnp.int32)

def conv_silu(extended, extended_doc, own_doc, taps, shift_bias):
    token_count = own_doc.shape[0]
    total_sum = jnp.zeros((token_count, extended.shape[1]), jnp.float32) + shift_bias[None, :]
    for offset in range(CONV):
        window = extended[offset:offset + token_count]
        same_doc = (extended_doc[offset:offset + token_count] == own_doc)[:, None]
        total_sum = total_sum + taps[offset][None, :] * jnp.where(same_doc, window, 0.0)
    return jax.nn.silu(total_sum)

def step_terms(step_raw, step_shift, decay_rate):
    step_size = jax.nn.softplus(step_raw + step_shift[None, :])
    cumulative = jnp.cumsum(-step_size * jnp.exp(decay_rate)[None, :], axis=0)
    return (step_size, cumulative)

def block_map(mix_values, write_keys, step_raw, step_shift, decay_rate, doc_ids, doc_before):
    step_size, cumulative = step_terms(step_raw, step_shift, decay_rate)
    final_sum = cumulative[-1]
    weight_in = jnp.where((doc_ids == doc_ids[-1])[:, None], jnp.exp(final_sum[None, :] - cumulative), 0.0) * step_size
    block_state = jnp.einsum('sh,shp,sn->hpn', weight_in, mix_values, write_keys, precision=HIGHEST)
    block_decay = jnp.where(doc_ids[-1] == doc_before, jnp.exp(final_sum), 0.0)
    return (block_decay, block_state)

def block_out(mix_values, write_keys, read_keys, step_raw, step_shift, decay_rate, skip_scale, doc_ids, doc_before, entry_state):
    step_size, cumulative = step_terms(step_raw, step_shift, decay_rate)
    token_count = doc_ids.shape[0]
    places = jnp.arange(token_count)
    allowed = (places[None, :] <= places[:, None]) & (doc_ids[None, :] == doc_ids[:, None])
    cum_heads = cumulative.T
    spread = cum_heads[:, :, None] - cum_heads[:, None, :]
    decays = jnp.where(allowed[None], jnp.exp(jnp.where(allowed[None], spread, 0.0)), 0.0)
    inner_sum = jnp.dot(read_keys, write_keys.T, precision=HIGHEST)
    mixing = decays * inner_sum[None]
    driven = step_size[:, :, None] * mix_values
    result = jnp.einsum('hts,shp->thp', mixing, driven, precision=HIGHEST)
    carried = jnp.where((doc_ids == doc_before)[:, None], jnp.exp(cumulative), 0.0)
    result = result + carried[:, :, None] * jnp.einsum('hpn,tn->thp', entry_state, read_keys, precision=HIGHEST)
    return result + skip_scale[None, :, None] * mix_values

def attention(queries, keys_rot, values_low, places, doc_ids):
    token_count = places.shape[0]
    rows_block = math.gcd(512, token_count)
    block_count = token_count // rows_block
    group_size = HEADS // KV_HEADS
    score_scale = HEAD_DIM ** (-0.5)
    key_heads = keys_rot.reshape(token_count, KV_HEADS, HEAD_DIM)
    value_heads = values_low.reshape(token_count, KV_HEADS, HEAD_DIM)

    def attend(pieces):
        query_block, place_block, doc_block = pieces
        shaped = query_block.reshape(rows_block, KV_HEADS, group_size, HEAD_DIM)
        scores = low_back(jnp.einsum('qgrd,kgd->grqk', shaped, key_heads, precision=HIGHEST) * score_scale)
        allowed = (places[None, :] <= place_block[:, None]) & (doc_ids[None, :] == doc_block[:, None])
        scores = jnp.where(allowed[None, None], scores, -1e+30)
        row_peak = lax.optimization_barrier(jnp.max(scores, axis=-1, keepdims=True))
        shifted_exp = jnp.exp(scores - row_peak)
        weights = low(shifted_exp / lax.optimization_barrier(jnp.sum(shifted_exp, axis=-1, keepdims=True)))
        mixed = jnp.einsum('grqk,kgd->qgrd', weights, value_heads, precision=HIGHEST)
        return mixed.reshape(rows_block, QW)
    results = lax.map(jax.checkpoint(attend), (queries.reshape(block_count, rows_block, QW), places.reshape(block_count, rows_block), doc_ids.reshape(block_count, rows_block)))
    return results.reshape(token_count, QW)

def mamba(conv_out, step_raw, doc_ids, step_shift, decay_rate, skip_scale):
    token_count = doc_ids.shape[0]
    block_count = token_count // LB
    mix_values = conv_out[:, :MIX].reshape(block_count, LB, MIX_HEADS, MIX_DIM)
    write_keys = conv_out[:, MIX:MIX + STATE].reshape(block_count, LB, STATE)
    read_keys = conv_out[:, MIX + STATE:].reshape(block_count, LB, STATE)
    step_blocks = step_raw.reshape(block_count, LB, MIX_HEADS)
    doc_blocks = doc_ids.reshape(block_count, LB)
    doc_before = jnp.concatenate([jnp.full((1,), -1, jnp.int32), doc_blocks[:-1, -1]])

    def advance(entry_state, pieces):
        values_b, write_b, read_b, step_b, doc_b, before_b = pieces
        result = block_out(values_b, write_b, read_b, step_b, step_shift, decay_rate, skip_scale, doc_b, before_b, entry_state)
        block_decay, block_state = block_map(values_b, write_b, step_b, step_shift, decay_rate, doc_b, before_b)
        return (block_decay[:, None, None] * entry_state + block_state, result)
    start_state = jnp.zeros((MIX_HEADS, MIX_DIM, STATE), jnp.float32)
    _, results = lax.scan(jax.checkpoint(advance), start_state, (mix_values, write_keys, read_keys, step_blocks, doc_blocks, doc_before))
    return results.reshape(token_count, MIX)

def layer(x_rows, params, places, doc_ids):
    input_gain, query_weight, key_weight, value_weight, attention_out, mixer_in, state_in, step_in, conv_weight, conv_bias, step_bias, decay_log, skip_gain, mixer_out, feed_gain, gate_weight, up_weight, down_weight = params
    normed = low(rms_scale(x_rows, input_gain))
    cosine, sine_part = rope_tables(places)
    queries = low(rotate(low_back(product(normed, query_weight)), cosine, sine_part, HEADS))
    keys_rot = low(rotate(low_back(product(normed, key_weight)), cosine, sine_part, KV_HEADS))
    values_low = low(low_back(product(normed, value_weight)))
    attended = low(low_back(attention(queries, keys_rot, values_low, places, doc_ids)))
    attn_branch = low_back(product(attended, attention_out))
    mixed_in = low(low_back(product(normed, mixer_in)))
    state_part = low(low_back(product(normed, state_in)))
    step_raw = low_back(product(normed, step_in))
    conv_in = jnp.concatenate([mixed_in[:, MIX:], state_part], axis=1)
    extended = jnp.concatenate([jnp.zeros((CONV - 1, CH), jnp.float32), conv_in], axis=0)
    extended_doc = jnp.concatenate([jnp.full((CONV - 1,), -1, jnp.int32), doc_ids])
    conv_out = low(conv_silu(extended, extended_doc, doc_ids, conv_weight, conv_bias))
    scanned = mamba(conv_out, step_raw, doc_ids, step_bias, decay_log, skip_gain)
    gate_z = mixed_in[:, :MIX]
    gated = low(low_back(scanned * jax.nn.silu(gate_z)))
    mix_branch = low_back(product(gated, mixer_out))
    middle = x_rows + attn_branch + mix_branch
    normed_ff = low(rms_scale(middle, feed_gain))
    gate_vals = low_back(product(normed_ff, gate_weight))
    up_vals = low_back(product(normed_ff, up_weight))
    activ = low(jax.nn.silu(gate_vals) * up_vals)
    return middle + product(activ, down_weight)

def reference(tokens, cotangent, lengths, input_gain, query_weight, key_weight, value_weight, attention_out, mixer_in, state_in, step_in, conv_weight, conv_bias, step_bias, decay_log, skip_gain, mixer_out, feed_gain, gate_weight, up_weight, down_weight):
    params = tuple((weight.astype(jnp.float32) for weight in (input_gain, query_weight, key_weight, value_weight, attention_out, mixer_in, state_in, step_in, conv_weight, conv_bias, step_bias, decay_log, skip_gain, mixer_out, feed_gain, gate_weight, up_weight, down_weight)))
    places = jnp.arange(SEQ_LEN, dtype=jnp.int32)
    block_index = places // LB
    holder = jnp.where(block_index < N_CTX, block_index, 2 * N_CTX - 1 - block_index)
    upper_slot = (block_index >= N_CTX).astype(jnp.int32)
    row_of = (holder * 2 * LB + upper_slot * LB + places % LB).astype(jnp.int32)
    row_holder = places // (2 * LB)
    row_slot = places // LB % 2
    place_of = (jnp.where(row_slot == 0, row_holder, 2 * N_CTX - 1 - row_holder) * LB + places % LB).astype(jnp.int32)
    natural_x = tokens[:, row_of].astype(jnp.float32)
    natural_cot = cotangent[:, row_of].astype(jnp.float32)

    def one_sequence(totals, pieces):
        x_seq, cot_seq, length_row = pieces
        bounds = jnp.cumsum(length_row)
        doc_ids = document_ids(bounds, places)

        def forward(x_rows, *weights):
            return layer(x_rows, weights, places, doc_ids)
        result, pullback = jax.vjp(forward, x_seq, *params)
        grads_all = pullback(cot_seq)
        totals = tuple((running + extra for running, extra in zip(totals, grads_all[1:])))
        return (totals, (result.astype(jnp.bfloat16), grads_all[0]))
    start_totals = tuple((jnp.zeros_like(weight) for weight in params))
    totals, (results, input_rows) = lax.scan(one_sequence, start_totals, (natural_x, natural_cot, lengths))
    output = results[:, place_of]
    input_grad = input_rows[:, place_of]
    return (output, input_grad, totals[0], totals[1], totals[2], totals[3], totals[4], totals[5], totals[6], totals[7], totals[8], totals[9], totals[10], totals[11], totals[12], totals[13], totals[14], totals[15], totals[16], totals[17])
```

```python
import jax
import jax.numpy as jnp
from jax import lax
from jax.experimental import pallas as pl
from jax.experimental.pallas import tpu as pltpu
from jax.sharding import PartitionSpec as P

HEADS = 8
KV_HEADS = 2
HEAD_DIM = 64
MIX_HEADS = 24
MIX_DIM = 64
STATE = 128
CONV = 4
QW = 512
KW = 128
MIX = 1536
CH = 1792
LB = 128
SMALL = 11


EPSILON = 1e-05
ROPE_BASE = 100000000000.0
HIGHEST = lax.Precision.HIGHEST
NEG_LARGE = -1e30


def product(left, right):
    return jnp.dot(left, right, preferred_element_type=jnp.float32)


def left_product(left, right):
    return lax.dot_general(
        left, right, (((0,), (0,)), ((), ())), preferred_element_type=jnp.float32
    )


def right_product(left, right):
    return lax.dot_general(
        left, right, (((1,), (1,)), ((), ())), preferred_element_type=jnp.float32
    )


def rms_scale(values, gain_vector):
    return (
        values
        * lax.rsqrt(jnp.mean(values * values, axis=-1, keepdims=True) + EPSILON)
        * gain_vector
    )


def rope_tables(places):
    half_dim = HEAD_DIM // 2
    inverse = ROPE_BASE ** (-jnp.arange(half_dim, dtype=jnp.float32) / half_dim)
    angles = places.astype(jnp.float32)[:, None] * inverse[None, :]
    return (jnp.tile(jnp.cos(angles), (1, 4)), jnp.tile(jnp.sin(angles), (1, 4)))


def swap_matrix(width):
    row = lax.broadcasted_iota(jnp.int32, (width, width), 0)
    col = lax.broadcasted_iota(jnp.int32, (width, width), 1)
    half_dim = HEAD_DIM // 2
    lower = col % HEAD_DIM < half_dim
    return jnp.where(
        lower & (row == col + half_dim),
        -1.0,
        jnp.where(~lower & (row == col - half_dim), 1.0, 0.0),
    ).astype(jnp.float32)


def rotate(values, cosine, sine_part, sign):
    width = values.shape[1]
    swapped = jnp.dot(values, swap_matrix(width), precision=HIGHEST)
    repeats = width // cosine.shape[1]
    return values * jnp.tile(cosine, (1, repeats)) + sign * swapped * jnp.tile(
        sine_part, (1, repeats)
    )


WIDE = HEADS * LB


def split_heads(rows, target, half):
    turned = jnp.transpose(rows.astype(jnp.float32))
    zeros = jnp.zeros((HEAD_DIM, LB), target.dtype)
    for head in range(HEADS):
        group = head // (HEADS // KV_HEADS)
        cols = slice(head * LB, (head + 1) * LB)
        own = slice(group * HEAD_DIM, (group + 1) * HEAD_DIM)
        other = slice((1 - group) * HEAD_DIM, (2 - group) * HEAD_DIM)
        target[half, own, cols] = turned[head * HEAD_DIM : (head + 1) * HEAD_DIM].astype(
            target.dtype
        )
        target[half, other, cols] = zeros


def join_heads(wide):
    pieces = []
    for head in range(HEADS):
        group = head // (HEADS // KV_HEADS)
        pieces.append(
            wide[group * HEAD_DIM : (group + 1) * HEAD_DIM, head * LB : (head + 1) * LB]
        )
    return jnp.transpose(jnp.concatenate(pieces, axis=0))


def block_mask(rows_ref, block, half):
    base = jnp.where(half == 0, block, 31 - block) * LB
    key_at = lax.broadcasted_iota(jnp.int32, (LB, WIDE), 0) + base
    return (key_at <= rows_ref[half, 0:1, :]) & (key_at >= rows_ref[half, 1:2, :])


def pair_at(step, own):
    half = (step >= own).astype(jnp.int32)
    return step + half, half


def transposed_dot(left, right):
    return lax.dot_general(
        left, right, (((0,), (0,)), ((), ())), preferred_element_type=jnp.float32
    )


def attend_kernel(own_ref, rows_ref, query_ref, kv_ref, out_ref, log_ref, turned, total, peak, mass):
    own = own_ref[0]
    for half in range(2):
        scaled = query_ref[half * LB : (half + 1) * LB, :] * 0.125
        split_heads(scaled, turned, half)

    def scores(block, half):
        at = pl.multiple_of(half * LB, LB)
        keys = kv_ref[block, pl.ds(at, LB), 0:KW]
        values = kv_ref[block, pl.ds(at, LB), KW : 2 * KW]
        found = product(keys, turned[half])
        return jnp.where(block_mask(rows_ref, block, half), found, NEG_LARGE), values

    for half in range(2):
        found, values = scores(own, half)
        top = jnp.max(found, axis=0, keepdims=True)
        weights = jnp.exp(found - top)
        peak[half] = top
        mass[half] = jnp.sum(weights, axis=0, keepdims=True)
        total[half] = transposed_dot(values, weights.astype(jnp.bfloat16))

    def one(step, carry):
        block, half = pair_at(step, own)
        found, values = scores(block, half)
        old = peak[half]
        top = jnp.maximum(old, jnp.max(found, axis=0, keepdims=True))
        fade = jnp.exp(old - top)
        weights = jnp.exp(found - top)
        peak[half] = top
        mass[half] = mass[half] * fade + jnp.sum(weights, axis=0, keepdims=True)
        total[half] = total[half] * fade + transposed_dot(values, weights.astype(jnp.bfloat16))
        return carry

    lax.fori_loop(0, kv_ref.shape[0] - 1, one, 0)
    for half in range(2):
        out_ref[half * LB : (half + 1) * LB, :] = join_heads(total[half] / mass[half]).astype(
            out_ref.dtype
        )
        log_ref[half] = peak[half] + jnp.log(mass[half])


def attend_back_kernel(
    own_ref,
    rows_ref,
    query_ref,
    kv_ref,
    out_ref,
    log_ref,
    up_ref,
    d_query_ref,
    d_kv_ref,
    turned,
    turned_up,
    inner,
    total,
):
    own = own_ref[0]
    d_kv_ref[...] = jnp.zeros(d_kv_ref.shape, d_kv_ref.dtype)
    for half in range(2):
        rows = slice(half * LB, (half + 1) * LB)
        split_heads(query_ref[rows, :] * 0.125, turned, half)
        split_heads(up_ref[rows, :], turned_up, half)
        both = jnp.transpose(out_ref[rows, :].astype(jnp.float32) * up_ref[rows, :].astype(jnp.float32))
        for head in range(HEADS):
            inner[half, :, head * LB : (head + 1) * LB] = jnp.sum(
                both[head * HEAD_DIM : (head + 1) * HEAD_DIM], axis=0, keepdims=True
            )
        total[half] = jnp.zeros((KW, WIDE), jnp.float32)

    def visit(block, half):
        at = pl.multiple_of(half * LB, LB)
        keys = kv_ref[block, pl.ds(at, LB), 0:KW]
        values = kv_ref[block, pl.ds(at, LB), KW : 2 * KW]
        found = product(keys, turned[half])
        weights = jnp.where(
            block_mask(rows_ref, block, half), jnp.exp(found - log_ref[half]), 0.0
        )
        d_weights = product(values, turned_up[half])
        d_scores = (weights * (d_weights - inner[half])).astype(jnp.bfloat16)
        total[half] += transposed_dot(keys, d_scores)
        d_kv_ref[block, pl.ds(at, LB), 0:KW] = right_product(d_scores, turned[half]).astype(
            d_kv_ref.dtype
        )
        d_kv_ref[block, pl.ds(at, LB), KW : 2 * KW] = right_product(
            weights.astype(jnp.bfloat16), turned_up[half]
        ).astype(d_kv_ref.dtype)

    visit(own, 0)
    visit(own, 1)

    def one(step, carry):
        block, half = pair_at(step, own)
        visit(block, half)
        return carry

    lax.fori_loop(0, kv_ref.shape[0] - 1, one, 0)
    for half in range(2):
        d_query_ref[half * LB : (half + 1) * LB, :] = join_heads(total[half]) * 0.125


VMEM_SPEC = pl.BlockSpec(memory_space=pltpu.VMEM)
SMEM_SPEC = pl.BlockSpec(memory_space=pltpu.SMEM)


def attend(own, rows, queries, kv_all):
    return pl.pallas_call(
        attend_kernel,
        out_shape=(
            jax.ShapeDtypeStruct((2 * LB, QW), jnp.bfloat16),
            jax.ShapeDtypeStruct((2, 1, WIDE), jnp.float32),
        ),
        in_specs=[SMEM_SPEC, VMEM_SPEC, VMEM_SPEC, VMEM_SPEC],
        out_specs=(VMEM_SPEC, VMEM_SPEC),
        scratch_shapes=[
            pltpu.VMEM((2, KW, WIDE), jnp.bfloat16),
            pltpu.VMEM((2, KW, WIDE), jnp.float32),
            pltpu.VMEM((2, 1, WIDE), jnp.float32),
            pltpu.VMEM((2, 1, WIDE), jnp.float32),
        ],
        compiler_params=pltpu.CompilerParams(vmem_limit_bytes=32 * 1024 * 1024),
        cost_estimate=pl.CostEstimate(
            flops=17 * 4 * LB * KW * WIDE, bytes_accessed=3 * 2**20, transcendentals=17 * LB * WIDE
        ),
        name="attend",
    )(own, rows, queries, kv_all)


def attend_back(own, rows, queries, kv_all, attended, logs, upstream):
    return pl.pallas_call(
        attend_back_kernel,
        out_shape=(
            jax.ShapeDtypeStruct((2 * LB, QW), jnp.float32),
            jax.ShapeDtypeStruct(kv_all.shape, jnp.bfloat16),
        ),
        in_specs=[SMEM_SPEC] + [VMEM_SPEC] * 6,
        out_specs=(VMEM_SPEC, VMEM_SPEC),
        scratch_shapes=[
            pltpu.VMEM((2, KW, WIDE), jnp.bfloat16),
            pltpu.VMEM((2, KW, WIDE), jnp.bfloat16),
            pltpu.VMEM((2, 1, WIDE), jnp.float32),
            pltpu.VMEM((2, KW, WIDE), jnp.float32),
        ],
        compiler_params=pltpu.CompilerParams(vmem_limit_bytes=32 * 1024 * 1024),
        cost_estimate=pl.CostEstimate(
            flops=17 * 10 * LB * KW * WIDE, bytes_accessed=6 * 2**20, transcendentals=17 * LB * WIDE
        ),
        name="attend_back",
    )(own, rows, queries, kv_all, attended, logs, upstream)


PAIRS = MIX_HEADS // 2
PAIR = 2 * MIX_DIM


def lane_is_low():
    return lax.broadcasted_iota(jnp.int32, (LB, PAIR), 1) < MIX_DIM


def spread_pair(columns, pair, low_lanes):
    return jnp.where(
        low_lanes, columns[:, 2 * pair : 2 * pair + 1], columns[:, 2 * pair + 1 : 2 * pair + 2]
    )


def low_dot(left, right, left_dim, right_dim):
    return lax.dot_general(
        left.astype(jnp.bfloat16),
        right.astype(jnp.bfloat16),
        (((left_dim,), (right_dim,)), ((), ())),
        preferred_element_type=jnp.float32,
    )


def exact_dot(left, right):
    return jnp.dot(left, right, precision=HIGHEST, preferred_element_type=jnp.float32)


def triangle(lower):
    row = lax.broadcasted_iota(jnp.int32, (LB, LB), 0)
    col = lax.broadcasted_iota(jnp.int32, (LB, LB), 1)
    return jnp.where(col <= row if lower else col >= row, 1.0, 0.0).astype(jnp.float32)


def softplus(values):
    return jnp.maximum(values, 0.0) + jnp.log1p(jnp.exp(-jnp.abs(values)))


def sigmoid(values):
    return 1.0 / (1.0 + jnp.exp(-values))


def block_base(own, half):
    return (own if half == 0 else 31 - own) * LB


def stage_rows(pre_ref, stage, half):
    edge = 2 * LB + 8 * half
    cols = slice(2 * KW, 2 * KW + CH)
    stage[0:8, :] = pre_ref[edge : edge + 8, cols].astype(jnp.bfloat16).astype(jnp.float32)
    stage[8 : 8 + LB, :] = (
        pre_ref[half * LB : (half + 1) * LB, cols].astype(jnp.bfloat16).astype(jnp.float32)
    )


def window(stage, starts, base, offset):
    back = CONV - 1 - offset
    at = lax.broadcasted_iota(jnp.int32, (LB, 1), 0) + base - back
    keep = jnp.where(at >= starts, 1.0, 0.0)
    return stage[8 - back : 8 - back + LB, :] * keep


def mix_in_kernel(
    own_ref, pre_ref, starts_ref, taps_ref, shift_ref, heads_ref, conv_ref, step_ref, sum_ref,
    state_ref, decay_ref, stage
):
    own = own_ref[0]
    low_lanes = lane_is_low()
    lower = triangle(True)
    for half in range(2):
        rows = slice(half * LB, (half + 1) * LB)
        base = block_base(own, half)
        starts = starts_ref[rows, 0:1]
        stage_rows(pre_ref, stage, half)
        total = jnp.zeros((LB, CH), jnp.float32) + shift_ref[0:1, :]
        for offset in range(CONV):
            total = total + taps_ref[offset : offset + 1, :] * window(stage, starts, base, offset)
        conv_ref[rows, :] = (total * sigmoid(total)).astype(jnp.bfloat16)
        step = softplus(pre_ref[rows, 2 * KW + CH :] + heads_ref[0:1, :])
        summed = exact_dot(lower, -step * jnp.exp(heads_ref[1:2, :]))
        step_ref[rows, :] = step
        sum_ref[rows, :] = summed
        last = summed[LB - 1 : LB, :]
        same = starts == starts[LB - 1 : LB, :]
        weight = jnp.where(same, jnp.exp(last - summed), 0.0) * step
        decay_ref[half : half + 1, :] = jnp.where(
            starts[LB - 1 : LB, :] < base, jnp.exp(last), 0.0
        )
        write = conv_ref[rows, MIX : MIX + STATE]
        for pair in range(PAIRS):
            cols = slice(pair * PAIR, (pair + 1) * PAIR)
            driven = conv_ref[rows, cols].astype(jnp.float32) * spread_pair(weight, pair, low_lanes)
            state_ref[half, cols, :] = low_dot(driven, write, 0, 0).astype(jnp.bfloat16)


def block_terms(conv_ref, step_ref, sum_ref, starts_ref, rows, base):
    starts = starts_ref[rows, 0:1]
    summed = sum_ref[rows, :]
    step = step_ref[rows, :]
    summed_t = jnp.transpose(summed)
    step_t = jnp.transpose(step)
    row = lax.broadcasted_iota(jnp.int32, (LB, LB), 0)
    col = lax.broadcasted_iota(jnp.int32, (LB, LB), 1)
    allowed = (col <= row) & (col + base >= starts)
    write = conv_ref[rows, MIX : MIX + STATE]
    read = conv_ref[rows, MIX + STATE :]
    inner = low_dot(read, write, 1, 1)
    carried = jnp.where(starts < base, jnp.exp(summed), 0.0)
    return summed, step, summed_t, step_t, allowed, write, read, inner, carried


def head_decay(summed, summed_t, allowed, head):
    spread = summed[:, head : head + 1] - summed_t[head : head + 1, :]
    return jnp.exp(jnp.where(allowed, spread, NEG_LARGE))


def mix_out_kernel(
    own_ref, conv_ref, step_ref, sum_ref, starts_ref, skip_ref, entry_ref, gate_ref,
    scan_ref, gated_ref
):
    own = own_ref[0]
    low_lanes = lane_is_low()
    for half in range(2):
        rows = slice(half * LB, (half + 1) * LB)
        summed, step, summed_t, step_t, allowed, write, read, inner, carried = block_terms(
            conv_ref, step_ref, sum_ref, starts_ref, rows, block_base(own, half)
        )
        for pair in range(PAIRS):
            cols = slice(pair * PAIR, (pair + 1) * PAIR)
            values = conv_ref[rows, cols]
            found = []
            for head in (2 * pair, 2 * pair + 1):
                mixing = (
                    head_decay(summed, summed_t, allowed, head) * inner * step_t[head : head + 1, :]
                )
                found.append(low_dot(mixing, values, 1, 0))
            total = jnp.where(low_lanes, found[0], found[1])
            total = total + spread_pair(carried, pair, low_lanes) * low_dot(
                read, entry_ref[half, cols, :], 1, 1
            )
            total = total + skip_ref[0:1, cols] * values.astype(jnp.float32)
            gate = gate_ref[rows, cols].astype(jnp.float32)
            scan_ref[rows, cols] = total
            gated_ref[rows, cols] = (total * gate * sigmoid(gate)).astype(jnp.bfloat16)


def mix_back_kernel(
    own_ref, conv_ref, step_ref, sum_ref, starts_ref, skip_ref, entry_ref, gate_ref, scan_ref,
    up_ref, d_gate_ref, d_values_ref, d_entry_ref, d_keys_ref, d_sum_ref, d_step_ref, d_skip_ref,
    row_a, row_b
):
    own = own_ref[0]
    low_lanes = lane_is_low()
    lane = lax.broadcasted_iota(jnp.int32, (LB, LB), 1)
    row_a[...] = jnp.zeros(row_a.shape, jnp.float32)
    row_b[...] = jnp.zeros(row_b.shape, jnp.float32)
    for half in range(2):
        rows = slice(half * LB, (half + 1) * LB)
        summed, step, summed_t, step_t, allowed, write, read, inner, carried = block_terms(
            conv_ref, step_ref, sum_ref, starts_ref, rows, block_base(own, half)
        )
        d_inner = jnp.zeros((LB, LB), jnp.float32)
        d_read = jnp.zeros((LB, STATE), jnp.float32)
        d_sum = jnp.zeros((LB, LB), jnp.float32)
        for pair in range(PAIRS):
            cols = slice(pair * PAIR, (pair + 1) * PAIR)
            values = conv_ref[rows, cols]
            values32 = values.astype(jnp.float32)
            gate = gate_ref[rows, cols].astype(jnp.float32)
            sig = sigmoid(gate)
            up = up_ref[rows, cols].astype(jnp.float32)
            d_scan = up * gate * sig
            d_gate_ref[rows, cols] = (
                up * scan_ref[rows, cols] * sig * (1.0 + gate * (1.0 - sig))
            ).astype(jnp.bfloat16)
            d_skip_ref[half : half + 1, cols] = jnp.sum(d_scan * values32, axis=0, keepdims=True)
            d_values = skip_ref[0:1, cols] * d_scan
            entry = entry_ref[half, cols, :]
            through = low_dot(read, entry, 1, 1) * d_scan
            for place in range(2):
                head = 2 * pair + place
                own_lanes = low_lanes if place == 0 else jnp.logical_not(low_lanes)
                d_own = jnp.where(own_lanes, d_scan, 0.0).astype(jnp.bfloat16)
                decay = head_decay(summed, summed_t, allowed, head)
                step_row = step_t[head : head + 1, :]
                raw = low_dot(d_own, values, 1, 1) * decay
                scaled = raw * step_row
                d_inner = d_inner + scaled
                mixed = decay * inner * step_row
                d_values = d_values + low_dot(mixed, d_own, 0, 0)
                kept = raw * inner
                by_key = jnp.sum(kept, axis=0, keepdims=True)
                row_a[head : head + 1, :] = by_key
                row_b[head : head + 1, :] = by_key * step_row
                by_row = jnp.sum(scaled * inner, axis=1, keepdims=True) + carried[
                    :, head : head + 1
                ] * jnp.sum(jnp.where(own_lanes, through, 0.0), axis=1, keepdims=True)
                d_sum = d_sum + jnp.where(lane == head, by_row, 0.0)
            d_values_ref[rows, cols] = d_values
            d_carry = (d_scan * spread_pair(carried, pair, low_lanes)).astype(jnp.bfloat16)
            d_read = d_read + low_dot(d_carry, entry, 1, 0)
            d_entry_ref[half, cols, :] = low_dot(d_carry, read, 0, 0).astype(jnp.bfloat16)
        d_keys_ref[rows, 0:STATE] = low_dot(d_inner, read, 0, 0)
        d_keys_ref[rows, STATE:] = d_read + low_dot(d_inner, write, 1, 0)
        d_sum_ref[rows, :] = d_sum - jnp.transpose(row_b[...])
        d_step_ref[rows, :] = jnp.transpose(row_a[...])


def mix_end_kernel(
    own_ref, conv_ref, step_ref, sum_ref, starts_ref, pre_ref, taps_ref, shift_ref, heads_ref,
    decay_ref, entry_ref, after_ref, d_values_ref, d_keys_ref, d_sum_ref, d_step_ref,
    d_own_ref, d_pre_ref, d_taps_ref, d_heads_ref, stage, d_stage, d_conv, meet, edges
):
    own = own_ref[0]
    low_lanes = lane_is_low()
    lane = lax.broadcasted_iota(jnp.int32, (LB, LB), 1)
    upper = triangle(False)
    rate = jnp.exp(heads_ref[1:2, :])
    d_pre_ref[0 : 2 * LB, 0 : 2 * KW] = d_own_ref[...]
    quiet = jnp.zeros((16, 2 * KW), d_pre_ref.dtype)
    d_pre_ref[2 * LB :, 0 : 2 * KW] = quiet
    d_pre_ref[2 * LB :, 2 * KW + CH :] = quiet[:, 0:128]
    meet[...] = jnp.zeros(meet.shape, jnp.float32)
    d_taps_ref[...] = jnp.zeros(d_taps_ref.shape, jnp.float32)
    d_heads_ref[...] = jnp.zeros(d_heads_ref.shape, jnp.float32)
    for half in range(2):
        rows = slice(half * LB, (half + 1) * LB)
        base = block_base(own, half)
        starts = starts_ref[rows, 0:1]
        summed = sum_ref[rows, :]
        step = step_ref[rows, :]
        last = summed[LB - 1 : LB, :]
        same = starts == starts[LB - 1 : LB, :]
        fade = jnp.where(same, jnp.exp(last - summed), 0.0)
        weight = fade * step
        write = conv_ref[rows, MIX : MIX + STATE]
        d_write = jnp.zeros((LB, STATE), jnp.float32)
        d_weight = jnp.zeros((LB, LB), jnp.float32)
        for pair in range(PAIRS):
            cols = slice(pair * PAIR, (pair + 1) * PAIR)
            values = conv_ref[rows, cols].astype(jnp.float32)
            after = after_ref[half, cols, :]
            reach = low_dot(write, after, 1, 1)
            wide = spread_pair(weight, pair, low_lanes)
            d_conv[:, cols] = d_values_ref[rows, cols] + wide * reach
            d_write = d_write + low_dot(values * wide, after, 1, 0)
            both = values * reach
            overlap = after.astype(jnp.float32) * entry_ref[half, cols, :].astype(jnp.float32)
            for place in range(2):
                head = 2 * pair + place
                own_lanes = low_lanes if place == 0 else jnp.logical_not(low_lanes)
                column = jnp.sum(jnp.where(own_lanes, both, 0.0), axis=1, keepdims=True)
                d_weight = d_weight + jnp.where(lane == head, column, 0.0)
                meet[head : head + 1, :] = jnp.sum(
                    overlap[place * MIX_DIM : (place + 1) * MIX_DIM], axis=0, keepdims=True
                )
        d_conv[:, MIX : MIX + STATE] = d_keys_ref[rows, 0:STATE] + d_write
        d_conv[:, MIX + STATE :] = d_keys_ref[rows, STATE:]
        met = jnp.sum(jnp.transpose(meet[...]), axis=0, keepdims=True)
        moved = d_weight * weight
        d_last = (
            jnp.sum(moved, axis=0, keepdims=True) + decay_ref[half : half + 1, :] * met
        )
        at_last = lax.broadcasted_iota(jnp.int32, (LB, LB), 0) == LB - 1
        d_sum = d_sum_ref[rows, :] - moved + jnp.where(at_last, d_last, 0.0)
        d_rate = exact_dot(upper, d_sum)
        d_step = d_step_ref[rows, :] + d_weight * fade - d_rate * rate
        raw = pre_ref[rows, 2 * KW + CH :] + heads_ref[0:1, :]
        d_raw = jnp.where(lane < MIX_HEADS, d_step * sigmoid(raw), 0.0)
        d_heads_ref[0:1, :] += jnp.sum(d_raw, axis=0, keepdims=True)
        d_heads_ref[1:2, :] += jnp.sum(-d_rate * step * rate, axis=0, keepdims=True)
        d_pre_ref[rows, 2 * KW + CH :] = d_raw.astype(d_pre_ref.dtype)
        stage_rows(pre_ref, stage, half)
        total = jnp.zeros((LB, CH), jnp.float32) + shift_ref[0:1, :]
        for offset in range(CONV):
            total = total + taps_ref[offset : offset + 1, :] * window(stage, starts, base, offset)
        sig = sigmoid(total)
        d_total = d_conv[...] * sig * (1.0 + total * (1.0 - sig))
        d_taps_ref[CONV : CONV + 1, :] += jnp.sum(d_total, axis=0, keepdims=True)
        d_stage[...] = jnp.zeros(d_stage.shape, jnp.float32)
        for offset in range(CONV):
            back = CONV - 1 - offset
            at = lax.broadcasted_iota(jnp.int32, (LB, 1), 0) + base - back
            keep = jnp.where(at >= starts, 1.0, 0.0)
            kept = d_total * keep
            seen = stage[8 - back : 8 - back + LB, :]
            d_taps_ref[offset : offset + 1, :] += jnp.sum(kept * seen, axis=0, keepdims=True)
            d_stage[8 - back : 8 - back + LB, :] += taps_ref[offset : offset + 1, :] * kept
        edges[8 * half : 8 * half + 8, :] = d_stage[0:8, :]
        d_pre_ref[rows, 2 * KW : 2 * KW + CH] = d_stage[8 : 8 + LB, :].astype(d_pre_ref.dtype)
    d_pre_ref[2 * LB :, 2 * KW : 2 * KW + CH] = edges[...].astype(d_pre_ref.dtype)


def kernel_call(kernel, name, shapes, scratch, inputs):
    outs = tuple(jax.ShapeDtypeStruct(shape, dtype) for shape, dtype in shapes)
    moved = sum(value.size * value.dtype.itemsize for value in inputs) + sum(
        out.size * out.dtype.itemsize for out in outs
    )
    return pl.pallas_call(
        kernel,
        out_shape=outs,
        in_specs=[SMEM_SPEC] + [VMEM_SPEC] * (len(inputs) - 1),
        out_specs=tuple(VMEM_SPEC for _ in outs),
        scratch_shapes=[pltpu.VMEM(shape, dtype) for shape, dtype in scratch],
        compiler_params=pltpu.CompilerParams(vmem_limit_bytes=40 * 1024 * 1024),
        cost_estimate=pl.CostEstimate(
            flops=2 * 10**9, bytes_accessed=moved, transcendentals=10**6
        ),
        name=name,
    )(*inputs)


def ring_up(values):
    count = lax.axis_size("ctx")
    return lax.ppermute(values, "ctx", [(i, i + 1) for i in range(count - 1)])


def ring_down(values):
    count = lax.axis_size("ctx")
    return lax.ppermute(values, "ctx", [(i + 1, i) for i in range(count - 1)])


def gather(shard):
    return lax.all_gather(shard, "fsdp", axis=0, tiled=True)


def scatter(total):
    return lax.psum_scatter(total.astype(jnp.bfloat16), "fsdp", scatter_dimension=0, tiled=True)


def exchange(values):
    return lax.all_to_all(values, "ctx", 0, 0, tiled=True)


def spread(values, axis):
    count = lax.axis_size(axis)
    copies = jnp.broadcast_to(values[None], (count,) + values.shape)
    return lax.all_to_all(copies, axis, 0, 0, tiled=True)


def added(pieces):
    return jnp.sum(pieces.astype(jnp.float32), axis=0).astype(jnp.bfloat16)


def sum_ctx(shard):
    parts = lax.axis_size("ctx")
    pieces = exchange(shard.reshape((parts, -1) + shard.shape[1:]))
    return spread(added(pieces), "ctx").reshape(shard.shape)


def gather_across(shard):
    parts = lax.axis_size("ctx")
    count = shard.shape[0] // parts
    own = lax.dynamic_slice_in_dim(shard, lax.axis_index("ctx") * count, count, 0)
    whole = spread(spread(own, "fsdp"), "ctx")
    return whole.transpose(1, 0, 2, 3).reshape(-1, shard.shape[1])


def sum_across(total):
    parts = lax.axis_size("ctx")
    shards = lax.axis_size("fsdp")
    width = total.shape[1]
    pieces = total.reshape(shards, parts, -1, width).transpose(1, 0, 2, 3)
    held = added(exchange(pieces))
    held = added(lax.all_to_all(held, "fsdp", 0, 0, tiled=True))
    return spread(held, "ctx").reshape(-1, width)


def pack_small(parts, rows):
    flat = jnp.concatenate([part.reshape(-1) for part in parts])
    flat = jnp.pad(flat, (0, rows * SMALL - flat.shape[0]))
    return flat.reshape(rows, SMALL)


def small_sizes(shards):
    return (1024 // shards, CONV * CH // shards, CH // shards) + (MIX_HEADS // shards,) * 3 + (
        1024 // shards,
    )


def split_small(flat, shards):
    pieces = []
    start = 0
    for size in small_sizes(shards):
        pieces.append(flat[..., start : start + size])
        start += size
    return pieces


def head_rows(values, parts):
    return jnp.repeat(values, MIX_DIM, axis=-1).reshape(values.shape[0], parts, -1)


def send_states(states, parts):
    halves = states.shape[0]
    shaped = states.astype(jnp.bfloat16).reshape(halves, parts, MIX // parts, STATE)
    return shaped.transpose(1, 0, 2, 3)


def running(factors, states, ahead):
    count = states.shape[0]
    order = list(range(count)) if ahead else list(range(count - 1, -1, -1))
    found = [None] * count
    state = jnp.zeros_like(states[0])
    for place in order:
        found[place] = state
        state = factors[place][:, None] * state + states[place]
    return jnp.stack(found)


def local(
    tokens,
    cotangent,
    lengths,
    input_gain,
    query_weight,
    key_weight,
    value_weight,
    attention_out,
    mixer_in,
    state_in,
    step_in,
    conv_weight,
    conv_bias,
    step_bias,
    decay_log,
    skip_gain,
    mixer_out,
    feed_gain,
    gate_weight,
    up_weight,
    down_weight,
):
    shards = lax.axis_size("fsdp")
    parts = lax.axis_size("ctx")
    ctx_index = lax.axis_index("ctx")
    rows = input_gain.shape[0]
    small = pack_small(
        (input_gain, conv_weight, conv_bias, step_bias, decay_log, skip_gain, feed_gain), rows
    )
    pad_cols = 128 - MIX_HEADS - SMALL
    first_proj = gather(
        jnp.concatenate(
            [
                key_weight,
                value_weight,
                mixer_in[:, MIX:],
                state_in,
                step_in,
                small,
                jnp.zeros((rows, pad_cols), jnp.bfloat16),
            ],
            axis=1,
        )
    )
    second_proj = gather(jnp.concatenate([query_weight, mixer_in[:, :MIX]], axis=1))
    out_proj = gather(jnp.concatenate([attention_out, mixer_out], axis=0))
    gate_up_proj = gather(jnp.concatenate([gate_weight, up_weight], axis=1))
    down_proj = gather_across(down_weight)
    step_at = 2 * KW + CH
    small_at = step_at + MIX_HEADS
    small_all = first_proj[:, small_at : small_at + SMALL].astype(jnp.float32).reshape(shards, -1)
    gain_in32, taps32, shift32, step_shift32, decay32, skip32, feed32 = split_small(
        small_all, shards
    )
    gain_in32 = gain_in32.reshape(-1)
    taps32 = taps32.reshape(shards, CONV, -1).transpose(1, 0, 2).reshape(CONV, CH)
    shift32 = shift32.reshape(-1)
    step_shift32 = step_shift32.reshape(-1)
    decay32 = decay32.reshape(-1)
    skip32 = skip32.reshape(-1)
    feed32 = feed32.reshape(-1)

    row_count = tokens.shape[1]
    half_rows = row_count // 2
    first_start = ctx_index * half_rows
    second_start = (2 * parts - 1 - ctx_index) * half_rows
    offsets = jnp.arange(half_rows, dtype=jnp.int32)
    places = jnp.concatenate([first_start + offsets, second_start + offsets])
    bounds = jnp.cumsum(lengths[0])
    doc_starts = jnp.max(
        jnp.where(bounds[None, :-1] <= places[:, None], bounds[None, :-1], 0), axis=1
    )
    row_limits = jnp.tile(
        jnp.stack([places, doc_starts]).reshape(2, 2, half_rows).transpose(1, 0, 2), (1, 1, HEADS)
    )
    own = ctx_index.reshape(1).astype(jnp.int32)
    cosine, sine_part = rope_tables(places)

    x_own = tokens[0]
    x_ext = jnp.concatenate(
        [x_own, ring_up(x_own[half_rows - 8 : half_rows]), ring_down(x_own[row_count - 8 :])]
    ).astype(jnp.float32)
    normed_ext = rms_scale(x_ext, gain_in32).astype(jnp.bfloat16)
    normed = normed_ext[:row_count]
    first_pre = product(normed_ext, first_proj)
    keys_rot = rotate(first_pre[:row_count, :KW], cosine, sine_part, 1.0).astype(jnp.bfloat16)
    values_low = first_pre[:row_count, KW : 2 * KW].astype(jnp.bfloat16)
    kv_all = spread(jnp.concatenate([keys_rot, values_low], axis=1), "ctx")
    starts_col = jnp.broadcast_to(doc_starts[:, None], (row_count, 128)).astype(jnp.int32)
    pad_heads = 128 - MIX_HEADS
    head_terms = jnp.pad(jnp.stack([step_shift32, decay32]), ((0, 6), (0, pad_heads)))
    taps_pad = jnp.pad(taps32, ((0, 4), (0, 0)))
    shift_row = shift32[None]
    skip_row = jnp.repeat(skip32, MIX_DIM)[None]
    conv_out, steps, sums, states, block_decay = kernel_call(
        mix_in_kernel,
        "mix_in",
        (
            ((row_count, CH), jnp.bfloat16),
            ((row_count, 128), jnp.float32),
            ((row_count, 128), jnp.float32),
            ((2, MIX, STATE), jnp.bfloat16),
            ((2, 128), jnp.float32),
        ),
        (((LB + 8, CH), jnp.float32),),
        (own, first_pre, starts_col, taps_pad, shift_row, head_terms),
    )

    decay_rows = head_rows(block_decay[:, :MIX_HEADS], parts).transpose(1, 0, 2)
    decay_high = decay_rows.astype(jnp.bfloat16)
    decay_low = (decay_rows - decay_high.astype(jnp.float32)).astype(jnp.bfloat16)
    decay_both = jnp.stack([decay_high, decay_low], axis=2)
    decay_both = jnp.pad(decay_both, ((0, 0), (0, 0), (0, 14), (0, STATE - MIX // parts)))
    states_out = send_states(states, parts)
    seen = exchange(jnp.concatenate([states_out, decay_both], axis=2)).astype(jnp.float32)
    slice_rows = MIX // parts
    seen_states = seen[:, :, :slice_rows]
    seen_decay = (seen[:, :, slice_rows] + seen[:, :, slice_rows + 1])[:, :, :slice_rows]
    entries = jnp.stack(
        [
            running(seen_decay[:, 0], seen_states[:, 0], True),
            running(seen_decay[:, 1], seen_states[:, 1], False),
        ],
        axis=1,
    ).astype(jnp.bfloat16)
    entries = exchange(entries).transpose(1, 0, 2, 3).reshape(2, MIX, STATE)

    second_pre = product(normed, second_proj)
    queries = rotate(second_pre[:, :QW], cosine, sine_part, 1.0).astype(jnp.bfloat16)
    gate_z = second_pre[:, QW:].astype(jnp.bfloat16)
    attended_low, log_totals = attend(own, row_limits, queries, kv_all)

    scanned, gated_low = kernel_call(
        mix_out_kernel,
        "mix_out",
        (((row_count, MIX), jnp.float32), ((row_count, MIX), jnp.bfloat16)),
        (),
        (own, conv_out, steps, sums, starts_col, skip_row, entries, gate_z),
    )
    x_rows = x_ext[:row_count]
    out_split = out_proj.reshape(shards, -1, out_proj.shape[1])
    attn_proj = out_split[:, : QW // shards].reshape(QW, -1)
    mix_proj = out_split[:, QW // shards :].reshape(MIX, -1)
    middle = x_rows + product(attended_low, attn_proj) + product(gated_low, mix_proj)
    normed_ff = rms_scale(middle, feed32).astype(jnp.bfloat16)
    gate_up = product(normed_ff, gate_up_proj)
    width = gate_up.shape[1] // 2
    gate_vals = gate_up[:, :width]
    up_vals = gate_up[:, width:]
    activ = (jax.nn.silu(gate_vals) * up_vals).astype(jnp.bfloat16)
    output = (middle + product(activ, down_proj)).astype(jnp.bfloat16)

    grad_out = cotangent[0]
    d_activ = right_product(grad_out, down_proj)
    d_down_own = sum_across(left_product(activ, grad_out).astype(jnp.bfloat16))
    sig_gate = jax.nn.sigmoid(gate_vals)
    d_gate = d_activ * up_vals * sig_gate * (1.0 + gate_vals * (1.0 - sig_gate))
    d_up = d_activ * gate_vals * sig_gate
    d_gate_up = jnp.concatenate([d_gate, d_up], axis=1).astype(jnp.bfloat16)
    d_gate_up_shard = scatter(left_product(normed_ff, d_gate_up))
    d_normed_ff = right_product(d_gate_up, gate_up_proj)
    _, feed_pull = jax.vjp(rms_scale, middle, feed32)
    d_middle_norm, d_feed_gain = feed_pull(d_normed_ff)
    d_middle = grad_out.astype(jnp.float32) + d_middle_norm
    d_middle_low = d_middle.astype(jnp.bfloat16)
    d_out_total = jnp.concatenate(
        [
            left_product(attended_low, d_middle_low)
            .astype(jnp.bfloat16)
            .reshape(shards, QW // shards, -1),
            left_product(gated_low, d_middle_low)
            .astype(jnp.bfloat16)
            .reshape(shards, MIX // shards, -1),
        ],
        axis=1,
    )
    d_out_shard = scatter(d_out_total.reshape(QW + MIX, -1))
    d_attended = right_product(d_middle_low, attn_proj).astype(jnp.bfloat16)
    d_gated = right_product(d_middle_low, mix_proj).astype(jnp.bfloat16)

    d_queries, d_kv = attend_back(
        own, row_limits, queries, kv_all, attended_low, log_totals, d_attended
    )
    d_kv_own = jnp.sum(exchange(d_kv).astype(jnp.float32), axis=0)
    d_query_pre = rotate(d_queries, cosine, sine_part, -1.0).astype(jnp.bfloat16)

    d_gate_z, d_values_part, d_entries, d_keys_part, d_sums, d_steps, d_skip_cols = kernel_call(
        mix_back_kernel,
        "mix_back",
        (
            ((row_count, MIX), jnp.bfloat16),
            ((row_count, MIX), jnp.float32),
            ((2, MIX, STATE), jnp.bfloat16),
            ((row_count, 2 * STATE), jnp.float32),
            ((row_count, 128), jnp.float32),
            ((row_count, 128), jnp.float32),
            ((2, MIX), jnp.float32),
        ),
        (((128, 128), jnp.float32), ((128, 128), jnp.float32)),
        (own, conv_out, steps, sums, starts_col, skip_row, entries, gate_z, scanned, d_gated),
    )
    d_second = jnp.concatenate([d_query_pre, d_gate_z], axis=1)
    d_second_shard = scatter(left_product(normed, d_second))
    seen_back = exchange(send_states(d_entries, parts)).astype(jnp.float32)
    afters = jnp.stack(
        [
            running(seen_decay[:, 0], seen_back[:, 0], False),
            running(seen_decay[:, 1], seen_back[:, 1], True),
        ],
        axis=1,
    ).astype(jnp.bfloat16)
    afters = exchange(afters).transpose(1, 0, 2, 3).reshape(2, MIX, STATE)
    d_key_pre = rotate(d_kv_own[:, :KW], cosine, sine_part, -1.0)
    d_first_own = jnp.concatenate([d_key_pre, d_kv_own[:, KW:]], axis=1).astype(jnp.bfloat16)
    d_first, d_taps_all, d_heads = kernel_call(
        mix_end_kernel,
        "mix_end",
        (
            ((row_count + 16, step_at + 128), jnp.bfloat16),
            ((8, CH), jnp.float32),
            ((8, 128), jnp.float32),
        ),
        (
            ((LB + 8, CH), jnp.float32),
            ((LB + 8, CH), jnp.float32),
            ((LB, CH), jnp.float32),
            ((128, 128), jnp.float32),
            ((16, CH), jnp.float32),
        ),
        (
            own,
            conv_out,
            steps,
            sums,
            starts_col,
            first_pre,
            taps_pad,
            shift_row,
            head_terms,
            block_decay,
            entries,
            afters,
            d_values_part,
            d_keys_part,
            d_sums,
            d_steps,
            d_first_own,
        ),
    )
    d_step_shift = d_heads[0, :MIX_HEADS]
    d_decay = d_heads[1, :MIX_HEADS]
    d_skip = d_skip_cols.sum(axis=0).reshape(MIX_HEADS, MIX_DIM).sum(axis=1)
    d_normed = right_product(d_first, first_proj) + jnp.pad(
        right_product(d_second, second_proj), ((0, 16), (0, 0))
    )
    _, input_pull = jax.vjp(rms_scale, x_ext, gain_in32)
    d_rows_norm, d_input_gain = input_pull(d_normed)
    edge_low = ring_down(d_rows_norm[row_count : row_count + 8])
    edge_high = ring_up(d_rows_norm[row_count + 8 :])
    input_grad = d_middle + d_rows_norm[:row_count]
    input_grad = input_grad.at[half_rows - 8 : half_rows].add(edge_low)
    input_grad = input_grad.at[row_count - 8 :].add(edge_high)[None]

    d_taps = (
        d_taps_all[:CONV].reshape(CONV, shards, -1).transpose(1, 0, 2)
    )
    d_small = jnp.concatenate(
        [
            piece.reshape(shards, -1)
            for piece in (
                d_input_gain,
                d_taps,
                d_taps_all[CONV],
                d_step_shift,
                d_decay,
                d_skip,
                d_feed_gain,
            )
        ],
        axis=1,
    )
    d_small = jnp.pad(d_small, ((0, 0), (0, rows * SMALL - d_small.shape[1])))
    d_first_total = left_product(normed_ext, d_first).astype(jnp.bfloat16)
    d_first_total = lax.dynamic_update_slice(
        d_first_total, d_small.reshape(shards * rows, SMALL).astype(jnp.bfloat16), (0, small_at)
    )
    d_first_own, d_second_own, d_out_own, d_gate_up_own, d_down_own = (
        total.astype(jnp.float32)
        for total in (
            sum_ctx(scatter(d_first_total)),
            sum_ctx(d_second_shard),
            sum_ctx(d_out_shard),
            sum_ctx(d_gate_up_shard),
            d_down_own,
        )
    )
    grad_gain, grad_taps, grad_shift, grad_step, grad_decay, grad_skip, grad_feed = split_small(
        d_first_own[:, small_at : small_at + SMALL].reshape(-1), shards
    )
    attn_rows = QW // shards
    return (
        output[None],
        input_grad,
        grad_gain,
        d_second_own[:, :QW],
        d_first_own[:, :KW],
        d_first_own[:, KW : 2 * KW],
        d_out_own[:attn_rows],
        jnp.concatenate([d_second_own[:, QW:], d_first_own[:, 2 * KW : 2 * KW + MIX]], axis=1),
        d_first_own[:, 2 * KW + MIX : step_at],
        d_first_own[:, step_at:small_at],
        grad_taps.reshape(CONV, -1),
        grad_shift,
        grad_step,
        grad_decay,
        grad_skip,
        d_out_own[attn_rows:],
        grad_feed,
        d_gate_up_own[:, :width],
        d_gate_up_own[:, width:],
        d_down_own,
    )


def solution(mesh):
    return jax.shard_map(
        local,
        mesh=mesh,
        in_specs=(
            P("fsdp", "ctx", None),
            P("fsdp", "ctx", None),
            P("fsdp", None),
            P("fsdp"),
            P("fsdp", None),
            P("fsdp", None),
            P("fsdp", None),
            P("fsdp", None),
            P("fsdp", None),
            P("fsdp", None),
            P("fsdp", None),
            P(None, "fsdp"),
            P("fsdp"),
            P("fsdp"),
            P("fsdp"),
            P("fsdp"),
            P("fsdp", None),
            P("fsdp"),
            P("fsdp", None),
            P("fsdp", None),
            P("fsdp", None),
        ),
        out_specs=(
            P("fsdp", "ctx", None),
            P("fsdp", "ctx", None),
            P("fsdp"),
            P("fsdp", None),
            P("fsdp", None),
            P("fsdp", None),
            P("fsdp", None),
            P("fsdp", None),
            P("fsdp", None),
            P("fsdp", None),
            P(None, "fsdp"),
            P("fsdp"),
            P("fsdp"),
            P("fsdp"),
            P("fsdp"),
            P("fsdp", None),
            P("fsdp"),
            P("fsdp", None),
            P("fsdp", None),
            P("fsdp", None),
        ),
        check_vma=False,
    )
```

```python
import jax
import jax.numpy as jnp
from jax import lax
from jax.experimental import pallas as pl
from jax.experimental.pallas import tpu as pltpu
from jax.sharding import PartitionSpec as P

HEADS = 8
KV_HEADS = 2
HEAD_DIM = 64
MIX_HEADS = 24
MIX_DIM = 64
STATE = 128
CONV = 4
QW = 512
KW = 128
MIX = 1536
CH = 1792
LB = 128
SMALL = 11
GROUPS = 8


EPSILON = 1e-05
ROPE_BASE = 100000000000.0
HIGHEST = lax.Precision.HIGHEST
NEG_LARGE = -1e30


def product(left, right):
    return jnp.dot(left, right, preferred_element_type=jnp.float32)


def left_product(left, right):
    return lax.dot_general(
        left, right, (((0,), (0,)), ((), ())), preferred_element_type=jnp.float32
    )


def right_product(left, right):
    return lax.dot_general(
        left, right, (((1,), (1,)), ((), ())), preferred_element_type=jnp.float32
    )


def rms_scale(values, gain_vector):
    return (
        values
        * lax.rsqrt(jnp.mean(values * values, axis=-1, keepdims=True) + EPSILON)
        * gain_vector
    )


def rope_tables(places):
    half_dim = HEAD_DIM // 2
    inverse = ROPE_BASE ** (-jnp.arange(half_dim, dtype=jnp.float32) / half_dim)
    angles = places.astype(jnp.float32)[:, None] * inverse[None, :]
    return (jnp.tile(jnp.cos(angles), (1, 4)), jnp.tile(jnp.sin(angles), (1, 4)))


def swap_matrix(width):
    row = lax.broadcasted_iota(jnp.int32, (width, width), 0)
    col = lax.broadcasted_iota(jnp.int32, (width, width), 1)
    half_dim = HEAD_DIM // 2
    lower = col % HEAD_DIM < half_dim
    return jnp.where(
        lower & (row == col + half_dim),
        -1.0,
        jnp.where(~lower & (row == col - half_dim), 1.0, 0.0),
    ).astype(jnp.float32)


def rotate(values, cosine, sine_part, sign):
    width = values.shape[1]
    swapped = jnp.dot(values, swap_matrix(width), precision=HIGHEST)
    repeats = width // cosine.shape[1]
    return values * jnp.tile(cosine, (1, repeats)) + sign * swapped * jnp.tile(
        sine_part, (1, repeats)
    )


WIDE = HEADS * LB


def split_heads(rows, target, half, stride=HEAD_DIM):
    turned = jnp.transpose(rows.astype(jnp.float32))
    zeros = jnp.zeros((HEAD_DIM, LB), target.dtype)
    for head in range(HEADS):
        group = head // (HEADS // KV_HEADS)
        cols = slice(head * LB, (head + 1) * LB)
        own = slice(group * HEAD_DIM, (group + 1) * HEAD_DIM)
        other = slice((1 - group) * HEAD_DIM, (2 - group) * HEAD_DIM)
        target[half, own, cols] = turned[head * stride : head * stride + HEAD_DIM].astype(
            target.dtype
        )
        target[half, other, cols] = zeros


def join_heads(wide):
    pieces = []
    for head in range(HEADS):
        group = head // (HEADS // KV_HEADS)
        pieces.append(
            wide[group * HEAD_DIM : (group + 1) * HEAD_DIM, head * LB : (head + 1) * LB]
        )
    return jnp.transpose(jnp.concatenate(pieces, axis=0))


def block_mask(rows_ref, block, half):
    base = jnp.where(half == 0, block, 31 - block) * LB
    key_at = lax.broadcasted_iota(jnp.int32, (LB, WIDE), 0) + base
    return (key_at <= rows_ref[half, 0:1, :]) & (key_at >= rows_ref[half, 1:2, :])


def pair_at(step, own):
    half = (step >= own).astype(jnp.int32)
    return step + half, half


def transposed_dot(left, right):
    return lax.dot_general(
        left, right, (((0,), (0,)), ((), ())), preferred_element_type=jnp.float32
    )


def attend_kernel(
    own_ref, rows_ref, query_ref, kv_ref, near_ref, out_ref, log_ref, turned, total, peak, mass
):
    own = own_ref[0]
    for half in range(2):
        scaled = query_ref[half * LB : (half + 1) * LB, :] * 0.125
        split_heads(scaled, turned, half)

    def scores(keys, values, block, half):
        found = product(keys, turned[half])
        return jnp.where(block_mask(rows_ref, block, half), found, NEG_LARGE), values

    for half in range(2):
        near = near_ref[half * LB : (half + 1) * LB, :]
        found, values = scores(near[:, 0:KW], near[:, KW:], own, half)
        top = jnp.max(found, axis=0, keepdims=True)
        weights = jnp.exp(found - top)
        peak[half] = top
        mass[half] = jnp.sum(weights, axis=0, keepdims=True)
        total[half] = transposed_dot(values, weights.astype(jnp.bfloat16))

    def one(step, carry):
        block, half = pair_at(step, own)
        found, values = scores(
            kv_ref[block, :, 0:KW], kv_ref[block, :, KW : 2 * KW], block, half
        )
        old = peak[half]
        top = jnp.maximum(old, jnp.max(found, axis=0, keepdims=True))
        fade = jnp.exp(old - top)
        weights = jnp.exp(found - top)
        peak[half] = top
        mass[half] = mass[half] * fade + jnp.sum(weights, axis=0, keepdims=True)
        total[half] = total[half] * fade + transposed_dot(values, weights.astype(jnp.bfloat16))
        return carry

    lax.fori_loop(0, kv_ref.shape[0] - 1, one, 0)
    for half in range(2):
        out_ref[half * LB : (half + 1) * LB, :] = join_heads(total[half] / mass[half]).astype(
            out_ref.dtype
        )
        log_ref[half] = peak[half] + jnp.log(mass[half])


def attend_back_kernel(
    own_ref,
    rows_ref,
    query_ref,
    kv_ref,
    near_ref,
    out_ref,
    log_ref,
    up_ref,
    d_query_ref,
    d_kv_ref,
    d_near_ref,
    turned,
    turned_up,
    inner,
    total,
):
    own = own_ref[0]
    d_kv_ref[own] = jnp.zeros((LB, 2 * KW), d_kv_ref.dtype)
    for half in range(2):
        rows = slice(half * LB, (half + 1) * LB)
        split_heads(query_ref[rows, :] * 0.125, turned, half)
        split_heads(up_ref[rows, :], turned_up, half, LB)
        seen = jnp.transpose(out_ref[rows, :].astype(jnp.float32))
        for head in range(HEADS):
            group = head // (HEADS // KV_HEADS)
            cols = slice(head * LB, (head + 1) * LB)
            up = turned_up[half, group * HEAD_DIM : (group + 1) * HEAD_DIM, cols]
            inner[half, :, cols] = jnp.sum(
                seen[head * HEAD_DIM : (head + 1) * HEAD_DIM] * up.astype(jnp.float32),
                axis=0,
                keepdims=True,
            )
        total[half] = jnp.zeros((KW, WIDE), jnp.float32)

    def visit(keys, values, block, half):
        found = product(keys, turned[half])
        weights = jnp.where(
            block_mask(rows_ref, block, half), jnp.exp(found - log_ref[half]), 0.0
        )
        d_weights = product(values, turned_up[half])
        d_scores = (weights * (d_weights - inner[half])).astype(jnp.bfloat16)
        total[half] += transposed_dot(keys, d_scores)
        d_keys = right_product(d_scores, turned[half])
        d_values = right_product(weights.astype(jnp.bfloat16), turned_up[half])
        return d_keys, d_values

    for half in range(2):
        rows = slice(half * LB, (half + 1) * LB)
        near = near_ref[rows, :]
        d_keys, d_values = visit(near[:, 0:KW], near[:, KW:], own, half)
        d_near_ref[rows, 0:KW] = d_keys
        d_near_ref[rows, KW:] = d_values

    def one(step, carry):
        block, half = pair_at(step, own)
        d_keys, d_values = visit(
            kv_ref[block, :, 0:KW], kv_ref[block, :, KW : 2 * KW], block, half
        )
        d_kv_ref[block, :, 0:KW] = d_keys.astype(d_kv_ref.dtype)
        d_kv_ref[block, :, KW : 2 * KW] = d_values.astype(d_kv_ref.dtype)
        return carry

    lax.fori_loop(0, kv_ref.shape[0] - 1, one, 0)
    for half in range(2):
        d_query_ref[half * LB : (half + 1) * LB, :] = join_heads(total[half]) * 0.125


VMEM_SPEC = pl.BlockSpec(memory_space=pltpu.VMEM)
SMEM_SPEC = pl.BlockSpec(memory_space=pltpu.SMEM)


def attend(own, rows, queries, kv_all, near):
    return pl.pallas_call(
        attend_kernel,
        out_shape=(
            jax.ShapeDtypeStruct((2 * LB, QW), jnp.bfloat16),
            jax.ShapeDtypeStruct((2, 1, WIDE), jnp.float32),
        ),
        in_specs=[SMEM_SPEC] + [VMEM_SPEC] * 4,
        out_specs=(VMEM_SPEC, VMEM_SPEC),
        scratch_shapes=[
            pltpu.VMEM((2, KW, WIDE), jnp.bfloat16),
            pltpu.VMEM((2, KW, WIDE), jnp.float32),
            pltpu.VMEM((2, 1, WIDE), jnp.float32),
            pltpu.VMEM((2, 1, WIDE), jnp.float32),
        ],
        compiler_params=pltpu.CompilerParams(vmem_limit_bytes=32 * 1024 * 1024),
        cost_estimate=pl.CostEstimate(
            flops=17 * 4 * LB * KW * WIDE, bytes_accessed=3 * 2**20, transcendentals=17 * LB * WIDE
        ),
        name="attend",
    )(own, rows, queries, kv_all, near)


def attend_back(own, rows, queries, kv_all, near, attended, logs, upstream):
    return pl.pallas_call(
        attend_back_kernel,
        out_shape=(
            jax.ShapeDtypeStruct((2 * LB, QW), jnp.float32),
            jax.ShapeDtypeStruct(kv_all.shape, jnp.bfloat16),
            jax.ShapeDtypeStruct(near.shape, jnp.float32),
        ),
        in_specs=[SMEM_SPEC] + [VMEM_SPEC] * 7,
        out_specs=(VMEM_SPEC, VMEM_SPEC, VMEM_SPEC),
        scratch_shapes=[
            pltpu.VMEM((2, KW, WIDE), jnp.bfloat16),
            pltpu.VMEM((2, KW, WIDE), jnp.bfloat16),
            pltpu.VMEM((2, 1, WIDE), jnp.float32),
            pltpu.VMEM((2, KW, WIDE), jnp.float32),
        ],
        compiler_params=pltpu.CompilerParams(vmem_limit_bytes=32 * 1024 * 1024),
        cost_estimate=pl.CostEstimate(
            flops=17 * 10 * LB * KW * WIDE, bytes_accessed=6 * 2**20, transcendentals=17 * LB * WIDE
        ),
        name="attend_back",
    )(own, rows, queries, kv_all, near, attended, logs, upstream)


SLICE = MIX // 16
EXTRA = 16


def row_pieces(pair):
    start = pair * PAIR
    pieces = []
    done = 0
    while done < PAIR:
        chunk, offset = divmod(start + done, SLICE)
        count = min(SLICE - offset, PAIR - done)
        pieces.append((chunk, offset, done, count))
        done += count
    return pieces


def put_rows(ref, half, pair, value):
    for chunk, offset, done, count in row_pieces(pair):
        ref[chunk, half, offset : offset + count, :] = value[done : done + count]


def take_rows(ref, half, pair):
    return jnp.concatenate(
        [
            ref[chunk, half, offset : offset + count, :]
            for chunk, offset, _, count in row_pieces(pair)
        ],
        axis=0,
    )


def put_decays(ref, half, decay):
    lane = lax.broadcasted_iota(jnp.int32, (1, 128), 1)
    level = lax.broadcasted_iota(jnp.int32, (EXTRA, 128), 0)
    for chunk in range(ref.shape[0]):
        first = chunk * SLICE // MIX_DIM
        last = ((chunk + 1) * SLICE - 1) // MIX_DIM
        row = jnp.zeros((1, 128), jnp.float32)
        for head in range(first, last + 1):
            row = jnp.where(lane >= head * MIX_DIM - chunk * SLICE, decay[:, head : head + 1], row)
        high = row.astype(jnp.bfloat16).astype(jnp.float32)
        ref[chunk, half, SLICE:, :] = jnp.where(
            level == 0, high, jnp.where(level == 1, row - high, 0.0)
        ).astype(jnp.bfloat16)


def scan_kernel(seen_ref, entry_ref, factor_ref, rows):
    count = seen_ref.shape[0]
    rows[...] = jnp.zeros(rows.shape, jnp.float32)
    for half in range(2):
        for place in range(count):
            extra = seen_ref[place, half, SLICE:, :].astype(jnp.float32)
            rows[place : place + 1, :] = extra[0:1, :] + extra[1:2, :]
        factors = jnp.transpose(rows[...])
        factor_ref[half] = factors
        state = jnp.zeros((SLICE, STATE), jnp.float32)
        for step in range(count):
            place = step if half == 0 else count - 1 - step
            entry_ref[place, half] = state.astype(jnp.bfloat16)
            state = factors[:SLICE, place : place + 1] * state + seen_ref[
                place, half, 0:SLICE, :
            ].astype(jnp.float32)


def scan_back_kernel(seen_ref, factor_ref, after_ref):
    count = seen_ref.shape[0]
    for half in range(2):
        factors = factor_ref[half]
        state = jnp.zeros((SLICE, STATE), jnp.float32)
        for step in range(count):
            place = count - 1 - step if half == 0 else step
            after_ref[place, half] = state.astype(jnp.bfloat16)
            state = factors[:SLICE, place : place + 1] * state + seen_ref[place, half].astype(
                jnp.float32
            )


PAIRS = MIX_HEADS // 2
PAIR = 2 * MIX_DIM


def lane_is_low():
    return lax.broadcasted_iota(jnp.int32, (LB, PAIR), 1) < MIX_DIM


def spread_pair(columns, pair, low_lanes):
    return jnp.where(
        low_lanes, columns[:, 2 * pair : 2 * pair + 1], columns[:, 2 * pair + 1 : 2 * pair + 2]
    )


def low_dot(left, right, left_dim, right_dim):
    return lax.dot_general(
        left.astype(jnp.bfloat16),
        right.astype(jnp.bfloat16),
        (((left_dim,), (right_dim,)), ((), ())),
        preferred_element_type=jnp.float32,
    )


def exact_dot(left, right):
    return jnp.dot(left, right, precision=HIGHEST, preferred_element_type=jnp.float32)


def triangle(lower):
    row = lax.broadcasted_iota(jnp.int32, (LB, LB), 0)
    col = lax.broadcasted_iota(jnp.int32, (LB, LB), 1)
    return jnp.where(col <= row if lower else col >= row, 1.0, 0.0).astype(jnp.float32)


def softplus(values):
    return jnp.maximum(values, 0.0) + jnp.log1p(jnp.exp(-jnp.abs(values)))


def sigmoid(values):
    return 1.0 / (1.0 + jnp.exp(-values))


def block_base(own, half):
    return (own if half == 0 else 31 - own) * LB


def stage_rows(pre_ref, stage, half):
    edge = 2 * LB + 8 * half
    cols = slice(2 * KW, 2 * KW + CH)
    stage[0:8, :] = pre_ref[edge : edge + 8, cols].astype(jnp.bfloat16).astype(jnp.float32)
    stage[8 : 8 + LB, :] = (
        pre_ref[half * LB : (half + 1) * LB, cols].astype(jnp.bfloat16).astype(jnp.float32)
    )


def window(stage, starts, base, offset):
    back = CONV - 1 - offset
    at = lax.broadcasted_iota(jnp.int32, (LB, 1), 0) + base - back
    keep = jnp.where(at >= starts, 1.0, 0.0)
    return stage[8 - back : 8 - back + LB, :] * keep


def mix_in_kernel(
    own_ref, pre_ref, starts_ref, taps_ref, shift_ref, heads_ref, conv_ref, step_ref, sum_ref,
    state_ref, decay_ref, stage
):
    own = own_ref[0]
    low_lanes = lane_is_low()
    lower = triangle(True)
    for half in range(2):
        rows = slice(half * LB, (half + 1) * LB)
        base = block_base(own, half)
        starts = starts_ref[rows, 0:1]
        stage_rows(pre_ref, stage, half)
        total = jnp.zeros((LB, CH), jnp.float32) + shift_ref[0:1, :]
        for offset in range(CONV):
            total = total + taps_ref[offset : offset + 1, :] * window(stage, starts, base, offset)
        conv_ref[rows, :] = (total * sigmoid(total)).astype(jnp.bfloat16)
        step = softplus(pre_ref[rows, 2 * KW + CH :] + heads_ref[0:1, :])
        summed = exact_dot(lower, -step * jnp.exp(heads_ref[1:2, :]))
        step_ref[rows, :] = step
        sum_ref[rows, :] = summed
        last = summed[LB - 1 : LB, :]
        same = starts == starts[LB - 1 : LB, :]
        weight = jnp.where(same, jnp.exp(last - summed), 0.0) * step
        decay = jnp.where(starts[LB - 1 : LB, :] < base, jnp.exp(last), 0.0)
        decay_ref[half : half + 1, :] = decay
        put_decays(state_ref, half, decay)
        write = conv_ref[rows, MIX : MIX + STATE]
        for pair in range(PAIRS):
            cols = slice(pair * PAIR, (pair + 1) * PAIR)
            driven = conv_ref[rows, cols].astype(jnp.float32) * spread_pair(weight, pair, low_lanes)
            put_rows(state_ref, half, pair, low_dot(driven, write, 0, 0).astype(jnp.bfloat16))


def block_terms(conv_ref, step_ref, sum_ref, starts_ref, rows, base):
    starts = starts_ref[rows, 0:1]
    summed = sum_ref[rows, :]
    step = step_ref[rows, :]
    summed_t = jnp.transpose(summed)
    step_t = jnp.transpose(step)
    row = lax.broadcasted_iota(jnp.int32, (LB, LB), 0)
    col = lax.broadcasted_iota(jnp.int32, (LB, LB), 1)
    allowed = (col <= row) & (col + base >= starts)
    write = conv_ref[rows, MIX : MIX + STATE]
    read = conv_ref[rows, MIX + STATE :]
    inner = low_dot(read, write, 1, 1)
    carried = jnp.where(starts < base, jnp.exp(summed), 0.0)
    return summed, step, summed_t, step_t, allowed, write, read, inner, carried


def head_decay(summed, summed_t, allowed, head):
    spread = summed[:, head : head + 1] - summed_t[head : head + 1, :]
    return jnp.exp(jnp.where(allowed, spread, NEG_LARGE))


def mix_out_kernel(
    own_ref, conv_ref, step_ref, sum_ref, starts_ref, skip_ref, entry_ref, gate_ref,
    scan_ref, gated_ref
):
    own = own_ref[0]
    low_lanes = lane_is_low()
    for half in range(2):
        rows = slice(half * LB, (half + 1) * LB)
        summed, step, summed_t, step_t, allowed, write, read, inner, carried = block_terms(
            conv_ref, step_ref, sum_ref, starts_ref, rows, block_base(own, half)
        )
        for pair in range(PAIRS):
            cols = slice(pair * PAIR, (pair + 1) * PAIR)
            values = conv_ref[rows, cols]
            found = []
            for head in (2 * pair, 2 * pair + 1):
                mixing = (
                    head_decay(summed, summed_t, allowed, head) * inner * step_t[head : head + 1, :]
                )
                found.append(low_dot(mixing, values, 1, 0))
            total = jnp.where(low_lanes, found[0], found[1])
            total = total + spread_pair(carried, pair, low_lanes) * low_dot(
                read, take_rows(entry_ref, half, pair), 1, 1
            )
            total = total + skip_ref[0:1, cols] * values.astype(jnp.float32)
            gate = gate_ref[rows, cols].astype(jnp.float32)
            scan_ref[rows, cols] = total
            gated_ref[rows, cols] = (total * gate * sigmoid(gate)).astype(jnp.bfloat16)


def branch_pair(low_ref, high_ref, rows, pair, low_lanes):
    found = []
    for place in range(2):
        group, turn = divmod(2 * pair + place, MIX_HEADS // GROUPS)
        source = low_ref if turn == 0 else high_ref
        block = source[rows, group * LB : (group + 1) * LB].astype(jnp.float32)
        if (turn != 1) != (place == 1):
            block = pltpu.roll(block, MIX_DIM, 1)
        found.append(block)
    return jnp.where(low_lanes, found[0], found[1])


def mix_back_kernel(
    own_ref, conv_ref, step_ref, sum_ref, starts_ref, skip_ref, entry_ref, gate_ref, scan_ref,
    up_low_ref, up_high_ref, d_gate_ref, d_values_ref, d_entry_ref, d_keys_ref, d_sum_ref, d_step_ref, d_skip_ref,
    row_a, row_b
):
    own = own_ref[0]
    low_lanes = lane_is_low()
    lane = lax.broadcasted_iota(jnp.int32, (LB, LB), 1)
    row_a[...] = jnp.zeros(row_a.shape, jnp.float32)
    row_b[...] = jnp.zeros(row_b.shape, jnp.float32)
    for half in range(2):
        rows = slice(half * LB, (half + 1) * LB)
        summed, step, summed_t, step_t, allowed, write, read, inner, carried = block_terms(
            conv_ref, step_ref, sum_ref, starts_ref, rows, block_base(own, half)
        )
        d_inner = jnp.zeros((LB, LB), jnp.float32)
        d_read = jnp.zeros((LB, STATE), jnp.float32)
        d_sum = jnp.zeros((LB, LB), jnp.float32)
        for pair in range(PAIRS):
            cols = slice(pair * PAIR, (pair + 1) * PAIR)
            values = conv_ref[rows, cols]
            values32 = values.astype(jnp.float32)
            gate = gate_ref[rows, cols].astype(jnp.float32)
            sig = sigmoid(gate)
            up = branch_pair(up_low_ref, up_high_ref, rows, pair, low_lanes)
            d_scan = up * gate * sig
            d_gate_ref[rows, cols] = (
                up * scan_ref[rows, cols] * sig * (1.0 + gate * (1.0 - sig))
            ).astype(jnp.bfloat16)
            d_skip_ref[half : half + 1, cols] = jnp.sum(d_scan * values32, axis=0, keepdims=True)
            d_values = skip_ref[0:1, cols] * d_scan
            entry = take_rows(entry_ref, half, pair)
            through = low_dot(read, entry, 1, 1) * d_scan
            for place in range(2):
                head = 2 * pair + place
                own_lanes = low_lanes if place == 0 else jnp.logical_not(low_lanes)
                d_own = jnp.where(own_lanes, d_scan, 0.0).astype(jnp.bfloat16)
                decay = head_decay(summed, summed_t, allowed, head)
                step_row = step_t[head : head + 1, :]
                raw = low_dot(d_own, values, 1, 1) * decay
                scaled = raw * step_row
                d_inner = d_inner + scaled
                mixed = decay * inner * step_row
                d_values = d_values + low_dot(mixed, d_own, 0, 0)
                kept = raw * inner
                by_key = jnp.sum(kept, axis=0, keepdims=True)
                row_a[head : head + 1, :] = by_key
                row_b[head : head + 1, :] = by_key * step_row
                by_row = jnp.sum(scaled * inner, axis=1, keepdims=True) + carried[
                    :, head : head + 1
                ] * jnp.sum(jnp.where(own_lanes, through, 0.0), axis=1, keepdims=True)
                d_sum = d_sum + jnp.where(lane == head, by_row, 0.0)
            d_values_ref[rows, cols] = d_values
            d_carry = (d_scan * spread_pair(carried, pair, low_lanes)).astype(jnp.bfloat16)
            d_read = d_read + low_dot(d_carry, entry, 1, 0)
            put_rows(d_entry_ref, half, pair, low_dot(d_carry, read, 0, 0).astype(jnp.bfloat16))
        d_keys_ref[rows, 0:STATE] = low_dot(d_inner, read, 0, 0)
        d_keys_ref[rows, STATE:] = d_read + low_dot(d_inner, write, 1, 0)
        d_sum_ref[rows, :] = d_sum - jnp.transpose(row_b[...])
        d_step_ref[rows, :] = jnp.transpose(row_a[...])


def mix_end_kernel(
    own_ref, conv_ref, step_ref, sum_ref, starts_ref, pre_ref, taps_ref, shift_ref, heads_ref,
    decay_ref, entry_ref, after_ref, d_values_ref, d_keys_ref, d_sum_ref, d_step_ref,
    d_pre_ref, d_taps_ref, d_heads_ref, stage, d_stage, d_conv, meet, edges
):
    own = own_ref[0]
    low_lanes = lane_is_low()
    lane = lax.broadcasted_iota(jnp.int32, (LB, LB), 1)
    upper = triangle(False)
    rate = jnp.exp(heads_ref[1:2, :])
    d_pre_ref[2 * LB :, CH:] = jnp.zeros((16, 128), d_pre_ref.dtype)
    meet[...] = jnp.zeros(meet.shape, jnp.float32)
    d_taps_ref[...] = jnp.zeros(d_taps_ref.shape, jnp.float32)
    d_heads_ref[...] = jnp.zeros(d_heads_ref.shape, jnp.float32)
    for half in range(2):
        rows = slice(half * LB, (half + 1) * LB)
        base = block_base(own, half)
        starts = starts_ref[rows, 0:1]
        summed = sum_ref[rows, :]
        step = step_ref[rows, :]
        last = summed[LB - 1 : LB, :]
        same = starts == starts[LB - 1 : LB, :]
        fade = jnp.where(same, jnp.exp(last - summed), 0.0)
        weight = fade * step
        write = conv_ref[rows, MIX : MIX + STATE]
        d_write = jnp.zeros((LB, STATE), jnp.float32)
        d_weight = jnp.zeros((LB, LB), jnp.float32)
        for pair in range(PAIRS):
            cols = slice(pair * PAIR, (pair + 1) * PAIR)
            values = conv_ref[rows, cols].astype(jnp.float32)
            after = take_rows(after_ref, half, pair)
            reach = low_dot(write, after, 1, 1)
            wide = spread_pair(weight, pair, low_lanes)
            d_conv[:, cols] = d_values_ref[rows, cols] + wide * reach
            d_write = d_write + low_dot(values * wide, after, 1, 0)
            both = values * reach
            overlap = after.astype(jnp.float32) * take_rows(
                entry_ref, half, pair
            ).astype(jnp.float32)
            for place in range(2):
                head = 2 * pair + place
                own_lanes = low_lanes if place == 0 else jnp.logical_not(low_lanes)
                column = jnp.sum(jnp.where(own_lanes, both, 0.0), axis=1, keepdims=True)
                d_weight = d_weight + jnp.where(lane == head, column, 0.0)
                meet[head : head + 1, :] = jnp.sum(
                    overlap[place * MIX_DIM : (place + 1) * MIX_DIM], axis=0, keepdims=True
                )
        d_conv[:, MIX : MIX + STATE] = d_keys_ref[rows, 0:STATE] + d_write
        d_conv[:, MIX + STATE :] = d_keys_ref[rows, STATE:]
        met = jnp.sum(jnp.transpose(meet[...]), axis=0, keepdims=True)
        moved = d_weight * weight
        d_last = (
            jnp.sum(moved, axis=0, keepdims=True) + decay_ref[half : half + 1, :] * met
        )
        at_last = lax.broadcasted_iota(jnp.int32, (LB, LB), 0) == LB - 1
        d_sum = d_sum_ref[rows, :] - moved + jnp.where(at_last, d_last, 0.0)
        d_rate = exact_dot(upper, d_sum)
        d_step = d_step_ref[rows, :] + d_weight * fade - d_rate * rate
        raw = pre_ref[rows, 2 * KW + CH :] + heads_ref[0:1, :]
        d_raw = jnp.where(lane < MIX_HEADS, d_step * sigmoid(raw), 0.0)
        d_heads_ref[0:1, :] += jnp.sum(d_raw, axis=0, keepdims=True)
        d_heads_ref[1:2, :] += jnp.sum(-d_rate * step * rate, axis=0, keepdims=True)
        d_pre_ref[rows, CH:] = d_raw.astype(d_pre_ref.dtype)
        stage_rows(pre_ref, stage, half)
        total = jnp.zeros((LB, CH), jnp.float32) + shift_ref[0:1, :]
        for offset in range(CONV):
            total = total + taps_ref[offset : offset + 1, :] * window(stage, starts, base, offset)
        sig = sigmoid(total)
        d_total = d_conv[...] * sig * (1.0 + total * (1.0 - sig))
        d_taps_ref[CONV : CONV + 1, :] += jnp.sum(d_total, axis=0, keepdims=True)
        d_stage[...] = jnp.zeros(d_stage.shape, jnp.float32)
        for offset in range(CONV):
            back = CONV - 1 - offset
            at = lax.broadcasted_iota(jnp.int32, (LB, 1), 0) + base - back
            keep = jnp.where(at >= starts, 1.0, 0.0)
            kept = d_total * keep
            seen = stage[8 - back : 8 - back + LB, :]
            d_taps_ref[offset : offset + 1, :] += jnp.sum(kept * seen, axis=0, keepdims=True)
            d_stage[8 - back : 8 - back + LB, :] += taps_ref[offset : offset + 1, :] * kept
        edges[8 * half : 8 * half + 8, :] = d_stage[0:8, :]
        d_pre_ref[rows, 0:CH] = d_stage[8 : 8 + LB, :].astype(d_pre_ref.dtype)
    d_pre_ref[2 * LB :, 0:CH] = edges[...].astype(d_pre_ref.dtype)


def whole_spec(shape):
    return pl.BlockSpec(shape, lambda step: (0,) * len(shape))


def streamed_call(kernel, name, shapes, scratch, inputs):
    outs = tuple(jax.ShapeDtypeStruct(shape, dtype) for shape, dtype in shapes)
    return pl.pallas_call(
        kernel,
        grid=(1,),
        out_shape=outs,
        in_specs=[SMEM_SPEC] + [whole_spec(value.shape) for value in inputs[1:]],
        out_specs=tuple(whole_spec(out.shape) for out in outs),
        scratch_shapes=[pltpu.VMEM(shape, dtype) for shape, dtype in scratch],
        compiler_params=pltpu.CompilerParams(vmem_limit_bytes=48 * 1024 * 1024),
        cost_estimate=pl.CostEstimate(
            flops=2 * 10**9, bytes_accessed=10**7, transcendentals=10**6
        ),
        name=name,
    )(*inputs)


def kernel_call(kernel, name, shapes, scratch, inputs):
    outs = tuple(jax.ShapeDtypeStruct(shape, dtype) for shape, dtype in shapes)
    moved = sum(value.size * value.dtype.itemsize for value in inputs) + sum(
        out.size * out.dtype.itemsize for out in outs
    )
    return pl.pallas_call(
        kernel,
        out_shape=outs,
        in_specs=[SMEM_SPEC] + [VMEM_SPEC] * (len(inputs) - 1),
        out_specs=tuple(VMEM_SPEC for _ in outs),
        scratch_shapes=[pltpu.VMEM(shape, dtype) for shape, dtype in scratch],
        compiler_params=pltpu.CompilerParams(vmem_limit_bytes=40 * 1024 * 1024),
        cost_estimate=pl.CostEstimate(
            flops=2 * 10**9, bytes_accessed=moved, transcendentals=10**6
        ),
        name=name,
    )(*inputs)


def grad_kernel(counts, *refs):
    sides = len(counts)
    left_refs, right_refs = refs[:sides], refs[sides : 2 * sides]
    out_ref, turned = refs[2 * sides], refs[2 * sides + 1 :]
    step = pl.program_id(0)

    @pl.when(step == 0)
    def _():
        for left_ref, held in zip(left_refs, turned):
            held[...] = jnp.transpose(left_ref[...])

    start = 0
    for count, right_ref, held in zip(counts, right_refs, turned):

        @pl.when((step >= start) & (step < start + count))
        def _(right_ref=right_ref, held=held):
            out_ref[...] = product(held[...], right_ref[...]).astype(out_ref.dtype)

        start += count


def stacked_gradients(pairs, block, name):
    counts = tuple(right.shape[1] // block for _, right in pairs)
    starts = [sum(counts[:place]) for place in range(len(counts))]

    def right_spec(place):
        def at(step):
            return (0, jnp.clip(step - starts[place], 0, counts[place] - 1))

        return pl.BlockSpec((pairs[place][1].shape[0], block), at)

    lefts = [left for left, _ in pairs]
    rights = [right for _, right in pairs]
    height = lefts[0].shape[1]
    total = sum(counts) * block
    flops = sum(2 * left.shape[0] * height * right.shape[1] for left, right in pairs)
    return pl.pallas_call(
        lambda *refs: grad_kernel(counts, *refs),
        grid=(sum(counts),),
        out_shape=jax.ShapeDtypeStruct((height, total), jnp.bfloat16),
        in_specs=[pl.BlockSpec(left.shape, lambda step: (0, 0)) for left in lefts]
        + [right_spec(place) for place in range(len(pairs))],
        out_specs=pl.BlockSpec((height, block), lambda step: (0, step)),
        scratch_shapes=[pltpu.VMEM((height, left.shape[0]), jnp.bfloat16) for left in lefts],
        compiler_params=pltpu.CompilerParams(vmem_limit_bytes=40 * 1024 * 1024),
        cost_estimate=pl.CostEstimate(
            flops=flops, bytes_accessed=2 * height * total, transcendentals=0
        ),
        name=name,
    )(*lefts, *rights)


def plain_call(kernel, name, shapes, scratch, inputs):
    outs = tuple(jax.ShapeDtypeStruct(shape, dtype) for shape, dtype in shapes)
    return pl.pallas_call(
        kernel,
        out_shape=outs,
        in_specs=[VMEM_SPEC] * len(inputs),
        out_specs=tuple(VMEM_SPEC for _ in outs),
        scratch_shapes=[pltpu.VMEM(shape, dtype) for shape, dtype in scratch],
        compiler_params=pltpu.CompilerParams(vmem_limit_bytes=40 * 1024 * 1024),
        cost_estimate=pl.CostEstimate(flops=10**8, bytes_accessed=2**22, transcendentals=0),
        name=name,
    )(*inputs)


def ring_up(values):
    count = lax.axis_size("ctx")
    return lax.ppermute(values, "ctx", [(i, i + 1) for i in range(count - 1)])


def ring_down(values):
    count = lax.axis_size("ctx")
    return lax.ppermute(values, "ctx", [(i + 1, i) for i in range(count - 1)])


def gather(shard):
    return lax.all_gather(shard, "fsdp", axis=0, tiled=True)


def scatter(total):
    return lax.psum_scatter(total.astype(jnp.bfloat16), "fsdp", scatter_dimension=0, tiled=True)


def exchange(values):
    return lax.all_to_all(values, "ctx", 0, 0, tiled=True)


def spread(values, axis):
    count = lax.axis_size(axis)
    copies = jnp.broadcast_to(values[None], (count,) + values.shape)
    return lax.all_to_all(copies, axis, 0, 0, tiled=True)


def added(pieces):
    return jnp.sum(pieces.astype(jnp.float32), axis=0).astype(jnp.bfloat16)


def sum_pieces(shard):
    parts = lax.axis_size("ctx")
    return added(exchange(shard.reshape((parts, -1) + shard.shape[1:])))


def hidden_split(weight):
    shaped = weight.reshape(weight.shape[0], GROUPS, 2, LB)
    return shaped.transpose(0, 2, 1, 3).reshape(weight.shape)


def hidden_join(weight):
    shaped = weight.reshape(weight.shape[0], 2, GROUPS, LB)
    return shaped.transpose(0, 2, 1, 3).reshape(weight.shape)


def side_by_side(weight):
    return jnp.concatenate([weight[:, :LB], weight[:, LB:]], axis=2).reshape(
        weight.shape[0] * LB, -1
    )


def one_above(weight):
    shaped = weight.reshape(-1, LB, weight.shape[1])
    cols = weight.shape[1] // 2
    return jnp.concatenate([shaped[:, :, :cols], shaped[:, :, cols:]], axis=1)


def hidden_pieces(pieces, width):
    return jnp.concatenate(
        [
            hidden_join(pieces[:, :width]),
            hidden_join(pieces[:, width : 2 * width]),
            pieces[:, 2 * width :],
        ],
        axis=1,
    )


def pack_small(parts, rows):
    flat = jnp.concatenate([part.reshape(-1) for part in parts])
    flat = jnp.pad(flat, (0, rows * SMALL - flat.shape[0]))
    return flat.reshape(rows, SMALL)


def small_sizes(shards):
    return (1024 // shards, CONV * CH // shards, CH // shards) + (MIX_HEADS // shards,) * 3 + (
        1024 // shards,
    )


def split_small(flat, shards):
    pieces = []
    start = 0
    for size in small_sizes(shards):
        pieces.append(flat[..., start : start + size])
        start += size
    return pieces


def local(
    tokens,
    cotangent,
    lengths,
    input_gain,
    query_weight,
    key_weight,
    value_weight,
    attention_out,
    mixer_in,
    state_in,
    step_in,
    conv_weight,
    conv_bias,
    step_bias,
    decay_log,
    skip_gain,
    mixer_out,
    feed_gain,
    gate_weight,
    up_weight,
    down_weight,
):
    shards = lax.axis_size("fsdp")
    parts = lax.axis_size("ctx")
    ctx_index = lax.axis_index("ctx")
    rows = input_gain.shape[0]
    small = pack_small(
        (input_gain, conv_weight, conv_bias, step_bias, decay_log, skip_gain, feed_gain), rows
    )
    pad_cols = 128 - MIX_HEADS - SMALL
    held = rows // LB
    width = gate_weight.shape[1]
    attn_rows = QW // GROUPS
    mix_rows = MIX // GROUPS
    first_all = gather(
        jnp.concatenate(
            [
                key_weight,
                value_weight,
                mixer_in[:, MIX:],
                state_in,
                step_in,
                small,
                jnp.zeros((rows, pad_cols), jnp.bfloat16),
                query_weight,
                mixer_in[:, :MIX],
            ],
            axis=1,
        )
    )
    later = jnp.concatenate(
        [
            side_by_side(
                jnp.concatenate(
                    [
                        attention_out.reshape(held, attn_rows, -1),
                        mixer_out.reshape(held, mix_rows, -1),
                    ],
                    axis=1,
                )
            ),
            hidden_split(gate_weight),
            hidden_split(up_weight),
            side_by_side(down_weight.reshape(held, 2 * LB, -1)),
        ],
        axis=1,
    )
    later = lax.dynamic_slice_in_dim(later, ctx_index * (rows // parts), rows // parts, 0)
    later_all = lax.all_gather(later, ("fsdp", "ctx"), axis=0, tiled=True)
    first_width = 2 * KW + CH + 128
    first_proj = first_all[:, :first_width]
    second_proj = first_all[:, first_width:]
    out_low = later_all[:, :1024]
    out_high = later_all[:, 1024:2048]
    gate_up_proj = later_all[:, 2048 : 2048 + 2 * width]
    down_low = later_all[:, 2048 + 2 * width : 3072 + 2 * width]
    down_high = later_all[:, 3072 + 2 * width :]
    step_at = 2 * KW + CH
    small_at = step_at + MIX_HEADS
    small_all = first_all[:, small_at : small_at + SMALL].astype(jnp.float32).reshape(shards, -1)
    gain_in32, taps32, shift32, step_shift32, decay32, skip32, feed32 = split_small(
        small_all, shards
    )
    gain_in32 = gain_in32.reshape(-1)
    taps32 = taps32.reshape(shards, CONV, -1).transpose(1, 0, 2).reshape(CONV, CH)
    shift32 = shift32.reshape(-1)
    step_shift32 = step_shift32.reshape(-1)
    decay32 = decay32.reshape(-1)
    skip32 = skip32.reshape(-1)
    feed32 = feed32.reshape(-1)

    row_count = tokens.shape[1]
    half_rows = row_count // 2
    first_start = ctx_index * half_rows
    second_start = (2 * parts - 1 - ctx_index) * half_rows
    offsets = jnp.arange(half_rows, dtype=jnp.int32)
    places = jnp.concatenate([first_start + offsets, second_start + offsets])
    bounds = jnp.cumsum(lengths[0])
    doc_starts = jnp.max(
        jnp.where(bounds[None, :-1] <= places[:, None], bounds[None, :-1], 0), axis=1
    )
    row_limits = jnp.tile(
        jnp.stack([places, doc_starts]).reshape(2, 2, half_rows).transpose(1, 0, 2), (1, 1, HEADS)
    )
    own = ctx_index.reshape(1).astype(jnp.int32)
    cosine, sine_part = rope_tables(places)

    x_own = tokens[0]
    x_ext = jnp.concatenate(
        [x_own, ring_up(x_own[half_rows - 8 : half_rows]), ring_down(x_own[row_count - 8 :])]
    ).astype(jnp.float32)
    normed_ext = rms_scale(x_ext, gain_in32).astype(jnp.bfloat16)
    normed = normed_ext[:row_count]
    first_pre = product(normed_ext, first_proj)
    keys_rot = rotate(first_pre[:row_count, :KW], cosine, sine_part, 1.0).astype(jnp.bfloat16)
    values_low = first_pre[:row_count, KW : 2 * KW].astype(jnp.bfloat16)
    kv_own = jnp.concatenate([keys_rot, values_low], axis=1)
    holders = jnp.arange(parts, dtype=jnp.int32)[:, None, None]
    kv_all = exchange(jnp.where(holders > ctx_index, kv_own[:half_rows], kv_own[half_rows:]))
    starts_col = jnp.broadcast_to(doc_starts[:, None], (row_count, 128)).astype(jnp.int32)
    pad_heads = 128 - MIX_HEADS
    head_terms = jnp.pad(jnp.stack([step_shift32, decay32]), ((0, 6), (0, pad_heads)))
    taps_pad = jnp.pad(taps32, ((0, 4), (0, 0)))
    shift_row = shift32[None]
    skip_row = jnp.repeat(skip32, MIX_DIM)[None]
    conv_out, steps, sums, states, block_decay = kernel_call(
        mix_in_kernel,
        "mix_in",
        (
            ((row_count, CH), jnp.bfloat16),
            ((row_count, 128), jnp.float32),
            ((row_count, 128), jnp.float32),
            ((parts, 2, SLICE + EXTRA, STATE), jnp.bfloat16),
            ((2, 128), jnp.float32),
        ),
        (((LB + 8, CH), jnp.float32),),
        (own, first_pre, starts_col, taps_pad, shift_row, head_terms),
    )

    entries, factors = plain_call(
        scan_kernel,
        "state_scan",
        (
            ((parts, 2, SLICE, STATE), jnp.bfloat16),
            ((2, 128, 128), jnp.float32),
        ),
        (((128, 128), jnp.float32),),
        (exchange(states),),
    )
    entries = exchange(entries)

    second_pre = product(normed, second_proj)
    queries = rotate(second_pre[:, :QW], cosine, sine_part, 1.0).astype(jnp.bfloat16)
    gate_z = second_pre[:, QW:].astype(jnp.bfloat16)
    attended_low, log_totals = attend(own, row_limits, queries, kv_all, kv_own)

    scanned, gated_low = kernel_call(
        mix_out_kernel,
        "mix_out",
        (((row_count, MIX), jnp.float32), ((row_count, MIX), jnp.bfloat16)),
        (),
        (own, conv_out, steps, sums, starts_col, skip_row, entries, gate_z),
    )
    x_rows = x_ext[:row_count]
    gated_groups = gated_low.reshape(row_count, GROUPS, mix_rows)
    branch_low = jnp.concatenate(
        [
            attended_low.reshape(row_count, GROUPS, attn_rows),
            gated_groups[:, :, : LB - attn_rows],
        ],
        axis=2,
    ).reshape(row_count, -1)
    branch_high = gated_groups[:, :, LB - attn_rows :].reshape(row_count, -1)
    middle = x_rows + product(branch_low, out_low) + product(branch_high, out_high)
    normed_ff = rms_scale(middle, feed32).astype(jnp.bfloat16)
    gate_up = product(normed_ff, gate_up_proj)
    gate_vals = gate_up[:, :width]
    up_vals = gate_up[:, width:]
    activ = (jax.nn.silu(gate_vals) * up_vals).astype(jnp.bfloat16)
    activ_low = activ[:, :1024]
    activ_high = activ[:, 1024:]
    output = (
        middle + product(activ_low, down_low) + product(activ_high, down_high)
    ).astype(jnp.bfloat16)

    grad_out = cotangent[0]
    d_activ = jnp.concatenate(
        [right_product(grad_out, down_low), right_product(grad_out, down_high)], axis=1
    )
    sig_gate = jax.nn.sigmoid(gate_vals)
    d_gate = d_activ * up_vals * sig_gate * (1.0 + gate_vals * (1.0 - sig_gate))
    d_up = d_activ * gate_vals * sig_gate
    d_gate_up = jnp.concatenate([d_gate, d_up], axis=1).astype(jnp.bfloat16)
    third_shard = scatter(
        stacked_gradients(
            ((normed_ff, d_gate_up), (activ_low, grad_out), (activ_high, grad_out)),
            512,
            "third_gradients",
        )
    )
    d_normed_ff = right_product(d_gate_up, gate_up_proj)
    _, feed_pull = jax.vjp(rms_scale, middle, feed32)
    d_middle_norm, d_feed_gain = feed_pull(d_normed_ff)
    d_middle = grad_out.astype(jnp.float32) + d_middle_norm
    d_middle_low = d_middle.astype(jnp.bfloat16)
    d_branch_low = right_product(d_middle_low, out_low).astype(jnp.bfloat16)
    d_branch_high = right_product(d_middle_low, out_high).astype(jnp.bfloat16)

    d_queries, d_kv, d_kv_near = attend_back(
        own, row_limits, queries, kv_all, kv_own, attended_low, log_totals, d_branch_low
    )
    d_query_pre = rotate(d_queries, cosine, sine_part, -1.0).astype(jnp.bfloat16)

    d_gate_z, d_values_part, d_entries, d_keys_part, d_sums, d_steps, d_skip_cols = kernel_call(
        mix_back_kernel,
        "mix_back",
        (
            ((row_count, MIX), jnp.bfloat16),
            ((row_count, MIX), jnp.float32),
            ((parts, 2, SLICE, STATE), jnp.bfloat16),
            ((row_count, 2 * STATE), jnp.float32),
            ((row_count, 128), jnp.float32),
            ((row_count, 128), jnp.float32),
            ((2, MIX), jnp.float32),
        ),
        (((128, 128), jnp.float32), ((128, 128), jnp.float32)),
        (own, conv_out, steps, sums, starts_col, skip_row, entries, gate_z, scanned, d_branch_low, d_branch_high),
    )
    d_second = jnp.concatenate([d_query_pre, d_gate_z], axis=1)
    seen_back = exchange(d_entries)
    d_second, seen_back = lax.optimization_barrier((d_second, seen_back))
    second_shard = scatter(
        stacked_gradients(
            ((normed, d_second), (branch_low, d_middle_low), (branch_high, d_middle_low)),
            512,
            "second_gradients",
        )
    )
    (afters,) = plain_call(
        scan_back_kernel,
        "state_scan_back",
        (((parts, 2, SLICE, STATE), jnp.bfloat16),),
        (),
        (seen_back, factors),
    )
    afters = exchange(afters)
    d_kv, afters = lax.optimization_barrier((d_kv, afters))
    d_kv_seen = exchange(d_kv)
    third_shard, d_kv_seen = lax.optimization_barrier((third_shard, d_kv_seen))
    third_pieces = hidden_pieces(sum_pieces(third_shard), width)
    second_shard, third_pieces = lax.optimization_barrier((second_shard, third_pieces))
    second_pieces = sum_pieces(second_shard)
    d_kv_seen = d_kv_seen.astype(jnp.float32)
    d_kv_own = d_kv_near + jnp.concatenate(
        [
            jnp.sum(jnp.where(holders > ctx_index, d_kv_seen, 0.0), axis=0),
            jnp.sum(jnp.where(holders < ctx_index, d_kv_seen, 0.0), axis=0),
        ]
    )
    d_key_pre = rotate(d_kv_own[:, :KW], cosine, sine_part, -1.0)
    d_kv_pre = jnp.concatenate([d_key_pre, d_kv_own[:, KW:]], axis=1).astype(jnp.bfloat16)
    d_main, d_taps_all, d_heads = streamed_call(
        mix_end_kernel,
        "mix_end",
        (
            ((row_count + 16, CH + 128), jnp.bfloat16),
            ((8, CH), jnp.float32),
            ((8, 128), jnp.float32),
        ),
        (
            ((LB + 8, CH), jnp.float32),
            ((LB + 8, CH), jnp.float32),
            ((LB, CH), jnp.float32),
            ((128, 128), jnp.float32),
            ((16, CH), jnp.float32),
        ),
        (
            own,
            conv_out,
            steps,
            sums,
            starts_col,
            first_pre,
            taps_pad,
            shift_row,
            head_terms,
            block_decay,
            entries,
            afters,
            d_values_part,
            d_keys_part,
            d_sums,
            d_steps,
        ),
    )
    d_step_shift = d_heads[0, :MIX_HEADS]
    d_decay = d_heads[1, :MIX_HEADS]
    d_skip = d_skip_cols.sum(axis=0).reshape(MIX_HEADS, MIX_DIM).sum(axis=1)
    d_first = jnp.concatenate([jnp.pad(d_kv_pre, ((0, 16), (0, 0))), d_main], axis=1)
    d_normed = right_product(d_first, first_proj) + jnp.pad(
        right_product(d_second, second_proj), ((0, 16), (0, 0))
    )
    _, input_pull = jax.vjp(rms_scale, x_ext, gain_in32)
    d_rows_norm, d_input_gain = input_pull(d_normed)
    edge_low = ring_down(d_rows_norm[row_count : row_count + 8])
    edge_high = ring_up(d_rows_norm[row_count + 8 :])
    input_grad = d_middle + d_rows_norm[:row_count]
    input_grad = input_grad.at[half_rows - 8 : half_rows].add(edge_low)
    input_grad = input_grad.at[row_count - 8 :].add(edge_high)[None]

    d_taps = (
        d_taps_all[:CONV].reshape(CONV, shards, -1).transpose(1, 0, 2)
    )
    d_small = jnp.concatenate(
        [
            piece.reshape(shards, -1)
            for piece in (
                d_input_gain,
                d_taps,
                d_taps_all[CONV],
                d_step_shift,
                d_decay,
                d_skip,
                d_feed_gain,
            )
        ],
        axis=1,
    )
    d_small = jnp.pad(d_small, ((0, 0), (0, rows * SMALL - d_small.shape[1])))
    small_cols = jnp.pad(
        d_small.reshape(shards * rows, SMALL),
        ((0, 0), (small_at, first_width - small_at - SMALL)),
    )
    first_total = left_product(normed_ext, d_first) + small_cols
    first_shard = scatter(first_total)
    first_shard, third_pieces, second_pieces = lax.optimization_barrier(
        (first_shard, third_pieces, second_pieces)
    )
    third_own = lax.all_gather(third_pieces, "ctx", axis=0, tiled=True).astype(jnp.float32)
    first_pieces = sum_pieces(first_shard)
    both = spread(jnp.concatenate([first_pieces, second_pieces], axis=1), "ctx")
    both = both.reshape(rows, -1).astype(jnp.float32)
    d_first_own = both[:, : first_pieces.shape[1]]
    d_second_own = both[:, first_pieces.shape[1] :]
    d_out_own = one_above(d_second_own[:, QW + MIX :])
    grad_gain, grad_taps, grad_shift, grad_step, grad_decay, grad_skip, grad_feed = split_small(
        d_first_own[:, small_at : small_at + SMALL].reshape(-1), shards
    )
    return (
        output[None],
        input_grad,
        grad_gain,
        d_second_own[:, :QW],
        d_first_own[:, :KW],
        d_first_own[:, KW : 2 * KW],
        d_out_own[:, :attn_rows].reshape(-1, 1024),
        jnp.concatenate(
            [d_second_own[:, QW : QW + MIX], d_first_own[:, 2 * KW : 2 * KW + MIX]], axis=1
        ),
        d_first_own[:, 2 * KW + MIX : step_at],
        d_first_own[:, step_at:small_at],
        grad_taps.reshape(CONV, -1),
        grad_shift,
        grad_step,
        grad_decay,
        grad_skip,
        d_out_own[:, attn_rows:].reshape(-1, 1024),
        grad_feed,
        third_own[:, :width],
        third_own[:, width : 2 * width],
        one_above(third_own[:, 2 * width :]).reshape(-1, 1024),
    )


def solution(mesh):
    return jax.shard_map(
        local,
        mesh=mesh,
        in_specs=(
            P("fsdp", "ctx", None),
            P("fsdp", "ctx", None),
            P("fsdp", None),
            P("fsdp"),
            P("fsdp", None),
            P("fsdp", None),
            P("fsdp", None),
            P("fsdp", None),
            P("fsdp", None),
            P("fsdp", None),
            P("fsdp", None),
            P(None, "fsdp"),
            P("fsdp"),
            P("fsdp"),
            P("fsdp"),
            P("fsdp"),
            P("fsdp", None),
            P("fsdp"),
            P("fsdp", None),
            P("fsdp", None),
            P("fsdp", None),
        ),
        out_specs=(
            P("fsdp", "ctx", None),
            P("fsdp", "ctx", None),
            P("fsdp"),
            P("fsdp", None),
            P("fsdp", None),
            P("fsdp", None),
            P("fsdp", None),
            P("fsdp", None),
            P("fsdp", None),
            P("fsdp", None),
            P(None, "fsdp"),
            P("fsdp"),
            P("fsdp"),
            P("fsdp"),
            P("fsdp"),
            P("fsdp", None),
            P("fsdp"),
            P("fsdp", None),
            P("fsdp", None),
            P("fsdp", None),
        ),
        check_vma=False,
    )
```

```python
import jax
import jax.numpy as jnp
from jax import lax
from jax.experimental import pallas as pl
from jax.experimental.pallas import tpu as pltpu
from jax.sharding import PartitionSpec as P

HEADS = 8
KV_HEADS = 2
HEAD_DIM = 64
MIX_HEADS = 24
MIX_DIM = 64
STATE = 128
CONV = 4
QW = 512
KW = 128
MIX = 1536
CH = 1792
LB = 128
SMALL = 11
GROUPS = 8


EPSILON = 1e-05
ROPE_BASE = 100000000000.0
HIGHEST = lax.Precision.HIGHEST
NEG_LARGE = -1e30


def product(left, right):
    return jnp.dot(left, right, preferred_element_type=jnp.float32)


def left_product(left, right):
    return lax.dot_general(
        left, right, (((0,), (0,)), ((), ())), preferred_element_type=jnp.float32
    )


def right_product(left, right):
    return lax.dot_general(
        left, right, (((1,), (1,)), ((), ())), preferred_element_type=jnp.float32
    )


def rms_scale(values, gain_vector):
    return (
        values
        * lax.rsqrt(jnp.mean(values * values, axis=-1, keepdims=True) + EPSILON)
        * gain_vector
    )


def rope_tables(places):
    half_dim = HEAD_DIM // 2
    inverse = ROPE_BASE ** (-jnp.arange(half_dim, dtype=jnp.float32) / half_dim)
    angles = places.astype(jnp.float32)[:, None] * inverse[None, :]
    return (jnp.tile(jnp.cos(angles), (1, 4)), jnp.tile(jnp.sin(angles), (1, 4)))


def swap_matrix(width):
    row = lax.broadcasted_iota(jnp.int32, (width, width), 0)
    col = lax.broadcasted_iota(jnp.int32, (width, width), 1)
    half_dim = HEAD_DIM // 2
    lower = col % HEAD_DIM < half_dim
    return jnp.where(
        lower & (row == col + half_dim),
        -1.0,
        jnp.where(~lower & (row == col - half_dim), 1.0, 0.0),
    ).astype(jnp.float32)


def rotate(values, cosine, sine_part, sign):
    width = values.shape[1]
    swapped = jnp.dot(values, swap_matrix(width), precision=HIGHEST)
    repeats = width // cosine.shape[1]
    return values * jnp.tile(cosine, (1, repeats)) + sign * swapped * jnp.tile(
        sine_part, (1, repeats)
    )


WIDE = HEADS * LB


def split_heads(rows, target, half, stride=HEAD_DIM):
    turned = jnp.transpose(rows.astype(jnp.float32))
    zeros = jnp.zeros((HEAD_DIM, LB), target.dtype)
    for head in range(HEADS):
        group = head // (HEADS // KV_HEADS)
        cols = slice(head * LB, (head + 1) * LB)
        own = slice(group * HEAD_DIM, (group + 1) * HEAD_DIM)
        other = slice((1 - group) * HEAD_DIM, (2 - group) * HEAD_DIM)
        target[half, own, cols] = turned[head * stride : head * stride + HEAD_DIM].astype(
            target.dtype
        )
        target[half, other, cols] = zeros


def join_heads(wide):
    pieces = []
    for head in range(HEADS):
        group = head // (HEADS // KV_HEADS)
        pieces.append(
            wide[group * HEAD_DIM : (group + 1) * HEAD_DIM, head * LB : (head + 1) * LB]
        )
    return jnp.transpose(jnp.concatenate(pieces, axis=0))


def block_mask(rows_ref, block, half):
    base = jnp.where(half == 0, block, 31 - block) * LB
    key_at = lax.broadcasted_iota(jnp.int32, (LB, WIDE), 0) + base
    return (key_at <= rows_ref[half, 0:1, :]) & (key_at >= rows_ref[half, 1:2, :])


def pair_at(step, own):
    half = (step >= own).astype(jnp.int32)
    return step + half, half


def transposed_dot(left, right):
    return lax.dot_general(
        left, right, (((0,), (0,)), ((), ())), preferred_element_type=jnp.float32
    )


def attend_kernel(
    own_ref, rows_ref, query_ref, kv_ref, near_ref, out_ref, log_ref, turned, total, peak, mass
):
    own = own_ref[0]
    for half in range(2):
        scaled = query_ref[half * LB : (half + 1) * LB, :] * 0.125
        split_heads(scaled, turned, half)

    def scores(keys, values, block, half):
        found = product(keys, turned[half])
        return jnp.where(block_mask(rows_ref, block, half), found, NEG_LARGE), values

    for half in range(2):
        near = near_ref[half * LB : (half + 1) * LB, :]
        found, values = scores(near[:, 0:KW], near[:, KW:], own, half)
        top = jnp.max(found, axis=0, keepdims=True)
        weights = jnp.exp(found - top)
        peak[half] = top
        mass[half] = jnp.sum(weights, axis=0, keepdims=True)
        total[half] = transposed_dot(values, weights.astype(jnp.bfloat16))

    def one(step, carry):
        block, half = pair_at(step, own)
        found, values = scores(
            kv_ref[block, :, 0:KW], kv_ref[block, :, KW : 2 * KW], block, half
        )
        old = peak[half]
        top = jnp.maximum(old, jnp.max(found, axis=0, keepdims=True))
        fade = jnp.exp(old - top)
        weights = jnp.exp(found - top)
        peak[half] = top
        mass[half] = mass[half] * fade + jnp.sum(weights, axis=0, keepdims=True)
        total[half] = total[half] * fade + transposed_dot(values, weights.astype(jnp.bfloat16))
        return carry

    lax.fori_loop(0, kv_ref.shape[0] - 1, one, 0)
    for half in range(2):
        out_ref[half * LB : (half + 1) * LB, :] = join_heads(total[half] / mass[half]).astype(
            out_ref.dtype
        )
        log_ref[half] = peak[half] + jnp.log(mass[half])


def attend_back_kernel(
    own_ref,
    rows_ref,
    query_ref,
    kv_ref,
    near_ref,
    out_ref,
    log_ref,
    up_ref,
    d_query_ref,
    d_kv_ref,
    d_near_ref,
    turned,
    turned_up,
    inner,
    total,
):
    own = own_ref[0]
    d_kv_ref[own] = jnp.zeros((LB, 2 * KW), d_kv_ref.dtype)
    for half in range(2):
        rows = slice(half * LB, (half + 1) * LB)
        split_heads(query_ref[rows, :] * 0.125, turned, half)
        split_heads(up_ref[rows, :], turned_up, half, LB)
        seen = jnp.transpose(out_ref[rows, :].astype(jnp.float32))
        for head in range(HEADS):
            group = head // (HEADS // KV_HEADS)
            cols = slice(head * LB, (head + 1) * LB)
            up = turned_up[half, group * HEAD_DIM : (group + 1) * HEAD_DIM, cols]
            inner[half, :, cols] = jnp.sum(
                seen[head * HEAD_DIM : (head + 1) * HEAD_DIM] * up.astype(jnp.float32),
                axis=0,
                keepdims=True,
            )
        total[half] = jnp.zeros((KW, WIDE), jnp.float32)

    def visit(keys, values, block, half):
        found = product(keys, turned[half])
        weights = jnp.where(
            block_mask(rows_ref, block, half), jnp.exp(found - log_ref[half]), 0.0
        )
        d_weights = product(values, turned_up[half])
        d_scores = (weights * (d_weights - inner[half])).astype(jnp.bfloat16)
        total[half] += transposed_dot(keys, d_scores)
        d_keys = right_product(d_scores, turned[half])
        d_values = right_product(weights.astype(jnp.bfloat16), turned_up[half])
        return d_keys, d_values

    for half in range(2):
        rows = slice(half * LB, (half + 1) * LB)
        near = near_ref[rows, :]
        d_keys, d_values = visit(near[:, 0:KW], near[:, KW:], own, half)
        d_near_ref[rows, 0:KW] = d_keys
        d_near_ref[rows, KW:] = d_values

    def one(step, carry):
        block, half = pair_at(step, own)
        d_keys, d_values = visit(
            kv_ref[block, :, 0:KW], kv_ref[block, :, KW : 2 * KW], block, half
        )
        d_kv_ref[block, :, 0:KW] = d_keys.astype(d_kv_ref.dtype)
        d_kv_ref[block, :, KW : 2 * KW] = d_values.astype(d_kv_ref.dtype)
        return carry

    lax.fori_loop(0, kv_ref.shape[0] - 1, one, 0)
    for half in range(2):
        d_query_ref[half * LB : (half + 1) * LB, :] = join_heads(total[half]) * 0.125


VMEM_SPEC = pl.BlockSpec(memory_space=pltpu.VMEM)
SMEM_SPEC = pl.BlockSpec(memory_space=pltpu.SMEM)


def attend(own, rows, queries, kv_all, near):
    return pl.pallas_call(
        attend_kernel,
        out_shape=(
            jax.ShapeDtypeStruct((2 * LB, QW), jnp.bfloat16),
            jax.ShapeDtypeStruct((2, 1, WIDE), jnp.float32),
        ),
        in_specs=[SMEM_SPEC] + [VMEM_SPEC] * 4,
        out_specs=(VMEM_SPEC, VMEM_SPEC),
        scratch_shapes=[
            pltpu.VMEM((2, KW, WIDE), jnp.bfloat16),
            pltpu.VMEM((2, KW, WIDE), jnp.float32),
            pltpu.VMEM((2, 1, WIDE), jnp.float32),
            pltpu.VMEM((2, 1, WIDE), jnp.float32),
        ],
        compiler_params=pltpu.CompilerParams(vmem_limit_bytes=32 * 1024 * 1024),
        cost_estimate=pl.CostEstimate(
            flops=17 * 4 * LB * KW * WIDE, bytes_accessed=3 * 2**20, transcendentals=17 * LB * WIDE
        ),
        name="attend",
    )(own, rows, queries, kv_all, near)


def attend_back(own, rows, queries, kv_all, near, attended, logs, upstream):
    return pl.pallas_call(
        attend_back_kernel,
        out_shape=(
            jax.ShapeDtypeStruct((2 * LB, QW), jnp.float32),
            jax.ShapeDtypeStruct(kv_all.shape, jnp.bfloat16),
            jax.ShapeDtypeStruct(near.shape, jnp.float32),
        ),
        in_specs=[SMEM_SPEC] + [VMEM_SPEC] * 7,
        out_specs=(VMEM_SPEC, VMEM_SPEC, VMEM_SPEC),
        scratch_shapes=[
            pltpu.VMEM((2, KW, WIDE), jnp.bfloat16),
            pltpu.VMEM((2, KW, WIDE), jnp.bfloat16),
            pltpu.VMEM((2, 1, WIDE), jnp.float32),
            pltpu.VMEM((2, KW, WIDE), jnp.float32),
        ],
        compiler_params=pltpu.CompilerParams(vmem_limit_bytes=32 * 1024 * 1024),
        cost_estimate=pl.CostEstimate(
            flops=17 * 10 * LB * KW * WIDE, bytes_accessed=6 * 2**20, transcendentals=17 * LB * WIDE
        ),
        name="attend_back",
    )(own, rows, queries, kv_all, near, attended, logs, upstream)


SLICE = MIX // 16
EXTRA = 16


def row_pieces(pair):
    start = pair * PAIR
    pieces = []
    done = 0
    while done < PAIR:
        chunk, offset = divmod(start + done, SLICE)
        count = min(SLICE - offset, PAIR - done)
        pieces.append((chunk, offset, done, count))
        done += count
    return pieces


def put_rows(ref, half, pair, value):
    for chunk, offset, done, count in row_pieces(pair):
        ref[chunk, half, offset : offset + count, :] = value[done : done + count]


def take_rows(ref, half, pair):
    return jnp.concatenate(
        [
            ref[chunk, half, offset : offset + count, :]
            for chunk, offset, _, count in row_pieces(pair)
        ],
        axis=0,
    )


def put_decays(ref, half, decay):
    lane = lax.broadcasted_iota(jnp.int32, (1, 128), 1)
    level = lax.broadcasted_iota(jnp.int32, (EXTRA, 128), 0)
    for chunk in range(ref.shape[0]):
        first = chunk * SLICE // MIX_DIM
        last = ((chunk + 1) * SLICE - 1) // MIX_DIM
        row = jnp.zeros((1, 128), jnp.float32)
        for head in range(first, last + 1):
            row = jnp.where(lane >= head * MIX_DIM - chunk * SLICE, decay[:, head : head + 1], row)
        high = row.astype(jnp.bfloat16).astype(jnp.float32)
        ref[chunk, half, SLICE:, :] = jnp.where(
            level == 0, high, jnp.where(level == 1, row - high, 0.0)
        ).astype(jnp.bfloat16)


def scan_kernel(seen_ref, entry_ref, factor_ref, rows):
    count = seen_ref.shape[0]
    rows[...] = jnp.zeros(rows.shape, jnp.float32)
    for half in range(2):
        for place in range(count):
            extra = seen_ref[place, half, SLICE:, :].astype(jnp.float32)
            rows[place : place + 1, :] = extra[0:1, :] + extra[1:2, :]
        factors = jnp.transpose(rows[...])
        factor_ref[half] = factors
        state = jnp.zeros((SLICE, STATE), jnp.float32)
        for step in range(count):
            place = step if half == 0 else count - 1 - step
            entry_ref[place, half] = state.astype(jnp.bfloat16)
            state = factors[:SLICE, place : place + 1] * state + seen_ref[
                place, half, 0:SLICE, :
            ].astype(jnp.float32)


def scan_back_kernel(seen_ref, factor_ref, after_ref):
    count = seen_ref.shape[0]
    for half in range(2):
        factors = factor_ref[half]
        state = jnp.zeros((SLICE, STATE), jnp.float32)
        for step in range(count):
            place = count - 1 - step if half == 0 else step
            after_ref[place, half] = state.astype(jnp.bfloat16)
            state = factors[:SLICE, place : place + 1] * state + seen_ref[place, half].astype(
                jnp.float32
            )


PAIRS = MIX_HEADS // 2
PAIR = 2 * MIX_DIM


def lane_is_low():
    return lax.broadcasted_iota(jnp.int32, (LB, PAIR), 1) < MIX_DIM


def spread_pair(columns, pair, low_lanes):
    return jnp.where(
        low_lanes, columns[:, 2 * pair : 2 * pair + 1], columns[:, 2 * pair + 1 : 2 * pair + 2]
    )


def low_dot(left, right, left_dim, right_dim):
    return lax.dot_general(
        left.astype(jnp.bfloat16),
        right.astype(jnp.bfloat16),
        (((left_dim,), (right_dim,)), ((), ())),
        preferred_element_type=jnp.float32,
    )


def exact_dot(left, right):
    return jnp.dot(left, right, precision=HIGHEST, preferred_element_type=jnp.float32)


def triangle(lower):
    row = lax.broadcasted_iota(jnp.int32, (LB, LB), 0)
    col = lax.broadcasted_iota(jnp.int32, (LB, LB), 1)
    return jnp.where(col <= row if lower else col >= row, 1.0, 0.0).astype(jnp.float32)


def softplus(values):
    return jnp.maximum(values, 0.0) + jnp.log1p(jnp.exp(-jnp.abs(values)))


def sigmoid(values):
    return 1.0 / (1.0 + jnp.exp(-values))


def block_base(own, half):
    return (own if half == 0 else 31 - own) * LB


def stage_rows(pre_ref, stage, half):
    edge = 2 * LB + 8 * half
    cols = slice(2 * KW, 2 * KW + CH)
    stage[0:8, :] = pre_ref[edge : edge + 8, cols].astype(jnp.bfloat16).astype(jnp.float32)
    stage[8 : 8 + LB, :] = (
        pre_ref[half * LB : (half + 1) * LB, cols].astype(jnp.bfloat16).astype(jnp.float32)
    )


def window(stage, starts, base, offset):
    back = CONV - 1 - offset
    at = lax.broadcasted_iota(jnp.int32, (LB, 1), 0) + base - back
    keep = jnp.where(at >= starts, 1.0, 0.0)
    return stage[8 - back : 8 - back + LB, :] * keep


def mix_in_kernel(
    own_ref, pre_ref, starts_ref, taps_ref, shift_ref, heads_ref, conv_ref, step_ref, sum_ref,
    state_ref, decay_ref, stage
):
    own = own_ref[0]
    low_lanes = lane_is_low()
    lower = triangle(True)
    for half in range(2):
        rows = slice(half * LB, (half + 1) * LB)
        base = block_base(own, half)
        starts = starts_ref[rows, 0:1]
        stage_rows(pre_ref, stage, half)
        total = jnp.zeros((LB, CH), jnp.float32) + shift_ref[0:1, :]
        for offset in range(CONV):
            total = total + taps_ref[offset : offset + 1, :] * window(stage, starts, base, offset)
        conv_ref[rows, :] = (total * sigmoid(total)).astype(jnp.bfloat16)
        step = softplus(pre_ref[rows, 2 * KW + CH :] + heads_ref[0:1, :])
        summed = exact_dot(lower, -step * jnp.exp(heads_ref[1:2, :]))
        step_ref[rows, :] = step
        sum_ref[rows, :] = summed
        last = summed[LB - 1 : LB, :]
        same = starts == starts[LB - 1 : LB, :]
        weight = jnp.where(same, jnp.exp(last - summed), 0.0) * step
        decay = jnp.where(starts[LB - 1 : LB, :] < base, jnp.exp(last), 0.0)
        decay_ref[half : half + 1, :] = decay
        put_decays(state_ref, half, decay)
        write = conv_ref[rows, MIX : MIX + STATE]
        for pair in range(PAIRS):
            cols = slice(pair * PAIR, (pair + 1) * PAIR)
            driven = conv_ref[rows, cols].astype(jnp.float32) * spread_pair(weight, pair, low_lanes)
            put_rows(state_ref, half, pair, low_dot(driven, write, 0, 0).astype(jnp.bfloat16))


def block_terms(conv_ref, step_ref, sum_ref, starts_ref, rows, base):
    starts = starts_ref[rows, 0:1]
    summed = sum_ref[rows, :]
    step = step_ref[rows, :]
    summed_t = jnp.transpose(summed)
    step_t = jnp.transpose(step)
    row = lax.broadcasted_iota(jnp.int32, (LB, LB), 0)
    col = lax.broadcasted_iota(jnp.int32, (LB, LB), 1)
    allowed = (col <= row) & (col + base >= starts)
    write = conv_ref[rows, MIX : MIX + STATE]
    read = conv_ref[rows, MIX + STATE :]
    inner = low_dot(read, write, 1, 1)
    carried = jnp.where(starts < base, jnp.exp(summed), 0.0)
    return summed, step, summed_t, step_t, allowed, write, read, inner, carried


def head_decay(summed, summed_t, allowed, head):
    spread = summed[:, head : head + 1] - summed_t[head : head + 1, :]
    return jnp.exp(jnp.where(allowed, spread, NEG_LARGE))


def mix_out_kernel(
    own_ref, conv_ref, step_ref, sum_ref, starts_ref, skip_ref, entry_ref, gate_ref,
    scan_ref, gated_ref
):
    own = own_ref[0]
    low_lanes = lane_is_low()
    for half in range(2):
        rows = slice(half * LB, (half + 1) * LB)
        summed, step, summed_t, step_t, allowed, write, read, inner, carried = block_terms(
            conv_ref, step_ref, sum_ref, starts_ref, rows, block_base(own, half)
        )
        for pair in range(PAIRS):
            cols = slice(pair * PAIR, (pair + 1) * PAIR)
            values = conv_ref[rows, cols]
            found = []
            for head in (2 * pair, 2 * pair + 1):
                mixing = (
                    head_decay(summed, summed_t, allowed, head) * inner * step_t[head : head + 1, :]
                )
                found.append(low_dot(mixing, values, 1, 0))
            total = jnp.where(low_lanes, found[0], found[1])
            total = total + spread_pair(carried, pair, low_lanes) * low_dot(
                read, take_rows(entry_ref, half, pair), 1, 1
            )
            total = total + skip_ref[0:1, cols] * values.astype(jnp.float32)
            gate = gate_ref[rows, cols].astype(jnp.float32)
            scan_ref[rows, cols] = total
            gated_ref[rows, cols] = (total * gate * sigmoid(gate)).astype(jnp.bfloat16)


def branch_pair(low_ref, high_ref, rows, pair, low_lanes):
    found = []
    for place in range(2):
        group, turn = divmod(2 * pair + place, MIX_HEADS // GROUPS)
        source = low_ref if turn == 0 else high_ref
        block = source[rows, group * LB : (group + 1) * LB].astype(jnp.float32)
        if (turn != 1) != (place == 1):
            block = pltpu.roll(block, MIX_DIM, 1)
        found.append(block)
    return jnp.where(low_lanes, found[0], found[1])


def mix_back_kernel(
    own_ref, conv_ref, step_ref, sum_ref, starts_ref, skip_ref, entry_ref, gate_ref, scan_ref,
    up_low_ref, up_high_ref, d_gate_ref, d_values_ref, d_entry_ref, d_keys_ref, d_sum_ref, d_step_ref, d_skip_ref,
    row_a, row_b
):
    own = own_ref[0]
    low_lanes = lane_is_low()
    lane = lax.broadcasted_iota(jnp.int32, (LB, LB), 1)
    row_a[...] = jnp.zeros(row_a.shape, jnp.float32)
    row_b[...] = jnp.zeros(row_b.shape, jnp.float32)
    for half in range(2):
        rows = slice(half * LB, (half + 1) * LB)
        summed, step, summed_t, step_t, allowed, write, read, inner, carried = block_terms(
            conv_ref, step_ref, sum_ref, starts_ref, rows, block_base(own, half)
        )
        d_inner = jnp.zeros((LB, LB), jnp.float32)
        d_read = jnp.zeros((LB, STATE), jnp.float32)
        d_sum = jnp.zeros((LB, LB), jnp.float32)
        for pair in range(PAIRS):
            cols = slice(pair * PAIR, (pair + 1) * PAIR)
            values = conv_ref[rows, cols]
            values32 = values.astype(jnp.float32)
            gate = gate_ref[rows, cols].astype(jnp.float32)
            sig = sigmoid(gate)
            up = branch_pair(up_low_ref, up_high_ref, rows, pair, low_lanes)
            d_scan = up * gate * sig
            d_gate_ref[rows, cols] = (
                up * scan_ref[rows, cols] * sig * (1.0 + gate * (1.0 - sig))
            ).astype(jnp.bfloat16)
            d_skip_ref[half : half + 1, cols] = jnp.sum(d_scan * values32, axis=0, keepdims=True)
            d_values = skip_ref[0:1, cols] * d_scan
            entry = take_rows(entry_ref, half, pair)
            through = low_dot(read, entry, 1, 1) * d_scan
            for place in range(2):
                head = 2 * pair + place
                own_lanes = low_lanes if place == 0 else jnp.logical_not(low_lanes)
                d_own = jnp.where(own_lanes, d_scan, 0.0).astype(jnp.bfloat16)
                decay = head_decay(summed, summed_t, allowed, head)
                step_row = step_t[head : head + 1, :]
                raw = low_dot(d_own, values, 1, 1) * decay
                scaled = raw * step_row
                d_inner = d_inner + scaled
                mixed = decay * inner * step_row
                d_values = d_values + low_dot(mixed, d_own, 0, 0)
                kept = raw * inner
                by_key = jnp.sum(kept, axis=0, keepdims=True)
                row_a[head : head + 1, :] = by_key
                row_b[head : head + 1, :] = by_key * step_row
                by_row = jnp.sum(scaled * inner, axis=1, keepdims=True) + carried[
                    :, head : head + 1
                ] * jnp.sum(jnp.where(own_lanes, through, 0.0), axis=1, keepdims=True)
                d_sum = d_sum + jnp.where(lane == head, by_row, 0.0)
            d_values_ref[rows, cols] = d_values
            d_carry = (d_scan * spread_pair(carried, pair, low_lanes)).astype(jnp.bfloat16)
            d_read = d_read + low_dot(d_carry, entry, 1, 0)
            put_rows(d_entry_ref, half, pair, low_dot(d_carry, read, 0, 0).astype(jnp.bfloat16))
        d_keys_ref[rows, 0:STATE] = low_dot(d_inner, read, 0, 0)
        d_keys_ref[rows, STATE:] = d_read + low_dot(d_inner, write, 1, 0)
        d_sum_ref[rows, :] = d_sum - jnp.transpose(row_b[...])
        d_step_ref[rows, :] = jnp.transpose(row_a[...])


def mix_end_kernel(
    own_ref, conv_ref, step_ref, sum_ref, starts_ref, pre_ref, taps_ref, shift_ref, heads_ref,
    decay_ref, entry_ref, after_ref, d_values_ref, d_keys_ref, d_sum_ref, d_step_ref,
    d_pre_ref, d_taps_ref, d_heads_ref, stage, d_stage, d_conv, meet, edges
):
    own = own_ref[0]
    low_lanes = lane_is_low()
    lane = lax.broadcasted_iota(jnp.int32, (LB, LB), 1)
    upper = triangle(False)
    rate = jnp.exp(heads_ref[1:2, :])
    d_pre_ref[2 * LB :, CH:] = jnp.zeros((16, 128), d_pre_ref.dtype)
    meet[...] = jnp.zeros(meet.shape, jnp.float32)
    d_taps_ref[...] = jnp.zeros(d_taps_ref.shape, jnp.float32)
    d_heads_ref[...] = jnp.zeros(d_heads_ref.shape, jnp.float32)
    for half in range(2):
        rows = slice(half * LB, (half + 1) * LB)
        base = block_base(own, half)
        starts = starts_ref[rows, 0:1]
        summed = sum_ref[rows, :]
        step = step_ref[rows, :]
        last = summed[LB - 1 : LB, :]
        same = starts == starts[LB - 1 : LB, :]
        fade = jnp.where(same, jnp.exp(last - summed), 0.0)
        weight = fade * step
        write = conv_ref[rows, MIX : MIX + STATE]
        d_write = jnp.zeros((LB, STATE), jnp.float32)
        d_weight = jnp.zeros((LB, LB), jnp.float32)
        for pair in range(PAIRS):
            cols = slice(pair * PAIR, (pair + 1) * PAIR)
            values = conv_ref[rows, cols].astype(jnp.float32)
            after = take_rows(after_ref, half, pair)
            reach = low_dot(write, after, 1, 1)
            wide = spread_pair(weight, pair, low_lanes)
            d_conv[:, cols] = d_values_ref[rows, cols] + wide * reach
            d_write = d_write + low_dot(values * wide, after, 1, 0)
            both = values * reach
            overlap = after.astype(jnp.float32) * take_rows(
                entry_ref, half, pair
            ).astype(jnp.float32)
            for place in range(2):
                head = 2 * pair + place
                own_lanes = low_lanes if place == 0 else jnp.logical_not(low_lanes)
                column = jnp.sum(jnp.where(own_lanes, both, 0.0), axis=1, keepdims=True)
                d_weight = d_weight + jnp.where(lane == head, column, 0.0)
                meet[head : head + 1, :] = jnp.sum(
                    overlap[place * MIX_DIM : (place + 1) * MIX_DIM], axis=0, keepdims=True
                )
        d_conv[:, MIX : MIX + STATE] = d_keys_ref[rows, 0:STATE] + d_write
        d_conv[:, MIX + STATE :] = d_keys_ref[rows, STATE:]
        met = jnp.sum(jnp.transpose(meet[...]), axis=0, keepdims=True)
        moved = d_weight * weight
        d_last = (
            jnp.sum(moved, axis=0, keepdims=True) + decay_ref[half : half + 1, :] * met
        )
        at_last = lax.broadcasted_iota(jnp.int32, (LB, LB), 0) == LB - 1
        d_sum = d_sum_ref[rows, :] - moved + jnp.where(at_last, d_last, 0.0)
        d_rate = exact_dot(upper, d_sum)
        d_step = d_step_ref[rows, :] + d_weight * fade - d_rate * rate
        raw = pre_ref[rows, 2 * KW + CH :] + heads_ref[0:1, :]
        d_raw = jnp.where(lane < MIX_HEADS, d_step * sigmoid(raw), 0.0)
        d_heads_ref[0:1, :] += jnp.sum(d_raw, axis=0, keepdims=True)
        d_heads_ref[1:2, :] += jnp.sum(-d_rate * step * rate, axis=0, keepdims=True)
        d_pre_ref[rows, CH:] = d_raw.astype(d_pre_ref.dtype)
        stage_rows(pre_ref, stage, half)
        total = jnp.zeros((LB, CH), jnp.float32) + shift_ref[0:1, :]
        for offset in range(CONV):
            total = total + taps_ref[offset : offset + 1, :] * window(stage, starts, base, offset)
        sig = sigmoid(total)
        d_total = d_conv[...] * sig * (1.0 + total * (1.0 - sig))
        d_taps_ref[CONV : CONV + 1, :] += jnp.sum(d_total, axis=0, keepdims=True)
        d_stage[...] = jnp.zeros(d_stage.shape, jnp.float32)
        for offset in range(CONV):
            back = CONV - 1 - offset
            at = lax.broadcasted_iota(jnp.int32, (LB, 1), 0) + base - back
            keep = jnp.where(at >= starts, 1.0, 0.0)
            kept = d_total * keep
            seen = stage[8 - back : 8 - back + LB, :]
            d_taps_ref[offset : offset + 1, :] += jnp.sum(kept * seen, axis=0, keepdims=True)
            d_stage[8 - back : 8 - back + LB, :] += taps_ref[offset : offset + 1, :] * kept
        edges[8 * half : 8 * half + 8, :] = d_stage[0:8, :]
        d_pre_ref[rows, 0:CH] = d_stage[8 : 8 + LB, :].astype(d_pre_ref.dtype)
    d_pre_ref[2 * LB :, 0:CH] = edges[...].astype(d_pre_ref.dtype)


def whole_spec(shape):
    return pl.BlockSpec(shape, lambda step: (0,) * len(shape))


def streamed_call(kernel, name, shapes, scratch, inputs):
    outs = tuple(jax.ShapeDtypeStruct(shape, dtype) for shape, dtype in shapes)
    return pl.pallas_call(
        kernel,
        grid=(1,),
        out_shape=outs,
        in_specs=[SMEM_SPEC] + [whole_spec(value.shape) for value in inputs[1:]],
        out_specs=tuple(whole_spec(out.shape) for out in outs),
        scratch_shapes=[pltpu.VMEM(shape, dtype) for shape, dtype in scratch],
        compiler_params=pltpu.CompilerParams(vmem_limit_bytes=48 * 1024 * 1024),
        cost_estimate=pl.CostEstimate(
            flops=2 * 10**9, bytes_accessed=10**7, transcendentals=10**6
        ),
        name=name,
    )(*inputs)


def kernel_call(kernel, name, shapes, scratch, inputs):
    outs = tuple(jax.ShapeDtypeStruct(shape, dtype) for shape, dtype in shapes)
    moved = sum(value.size * value.dtype.itemsize for value in inputs) + sum(
        out.size * out.dtype.itemsize for out in outs
    )
    return pl.pallas_call(
        kernel,
        out_shape=outs,
        in_specs=[SMEM_SPEC] + [VMEM_SPEC] * (len(inputs) - 1),
        out_specs=tuple(VMEM_SPEC for _ in outs),
        scratch_shapes=[pltpu.VMEM(shape, dtype) for shape, dtype in scratch],
        compiler_params=pltpu.CompilerParams(vmem_limit_bytes=40 * 1024 * 1024),
        cost_estimate=pl.CostEstimate(
            flops=2 * 10**9, bytes_accessed=moved, transcendentals=10**6
        ),
        name=name,
    )(*inputs)


def finish_kernel(
    both_ref, query_ref, key_ref, value_ref, attn_ref, mixer_ref, state_ref, step_ref, out_ref,
    small_ref
):
    def part(start, count):
        return both_ref[:, start : start + count].astype(jnp.float32)

    first = 2 * KW + CH + 128
    key_ref[...] = part(0, KW)
    value_ref[...] = part(KW, KW)
    mixer_ref[:, MIX:] = part(2 * KW, MIX)
    state_ref[...] = part(2 * KW + MIX, 2 * STATE)
    tail = part(2 * KW + CH, 128)
    step_ref[...] = tail[:, :MIX_HEADS]
    small_ref[...] = jnp.transpose(tail)
    query_ref[...] = part(first, QW)
    mixer_ref[:, :MIX] = part(first + QW, MIX)
    start = first + QW + MIX
    width = out_ref.shape[1]
    attn_rows = QW // GROUPS
    mix_rows = MIX // GROUPS
    for group in range(both_ref.shape[0] // LB):
        low = both_ref[group * LB : (group + 1) * LB, start : start + width].astype(jnp.float32)
        high = both_ref[group * LB : (group + 1) * LB, start + width :].astype(jnp.float32)
        attn_ref[group * attn_rows : (group + 1) * attn_rows, :] = low[:attn_rows]
        at = group * mix_rows
        out_ref[at : at + LB - attn_rows, :] = low[attn_rows:]
        out_ref[at + LB - attn_rows : at + mix_rows, :] = high


def grad_kernel(counts, *refs):
    sides = len(counts)
    left_refs, right_refs = refs[:sides], refs[sides : 2 * sides]
    out_ref, turned = refs[2 * sides], refs[2 * sides + 1 :]
    step = pl.program_id(0)

    @pl.when(step == 0)
    def _():
        for left_ref, held in zip(left_refs, turned):
            held[...] = jnp.transpose(left_ref[...])

    start = 0
    for count, right_ref, held in zip(counts, right_refs, turned):

        @pl.when((step >= start) & (step < start + count))
        def _(right_ref=right_ref, held=held):
            out_ref[...] = product(held[...], right_ref[...]).astype(out_ref.dtype)

        start += count


def stacked_gradients(pairs, block, name):
    counts = tuple(right.shape[1] // block for _, right in pairs)
    starts = [sum(counts[:place]) for place in range(len(counts))]

    def right_spec(place):
        def at(step):
            return (0, jnp.clip(step - starts[place], 0, counts[place] - 1))

        return pl.BlockSpec((pairs[place][1].shape[0], block), at)

    lefts = [left for left, _ in pairs]
    rights = [right for _, right in pairs]
    height = lefts[0].shape[1]
    total = sum(counts) * block
    flops = sum(2 * left.shape[0] * height * right.shape[1] for left, right in pairs)
    return pl.pallas_call(
        lambda *refs: grad_kernel(counts, *refs),
        grid=(sum(counts),),
        out_shape=jax.ShapeDtypeStruct((height, total), jnp.bfloat16),
        in_specs=[pl.BlockSpec(left.shape, lambda step: (0, 0)) for left in lefts]
        + [right_spec(place) for place in range(len(pairs))],
        out_specs=pl.BlockSpec((height, block), lambda step: (0, step)),
        scratch_shapes=[pltpu.VMEM((height, left.shape[0]), jnp.bfloat16) for left in lefts],
        compiler_params=pltpu.CompilerParams(vmem_limit_bytes=40 * 1024 * 1024),
        cost_estimate=pl.CostEstimate(
            flops=flops, bytes_accessed=2 * height * total, transcendentals=0
        ),
        name=name,
    )(*lefts, *rights)


def plain_call(kernel, name, shapes, scratch, inputs):
    outs = tuple(jax.ShapeDtypeStruct(shape, dtype) for shape, dtype in shapes)
    return pl.pallas_call(
        kernel,
        out_shape=outs,
        in_specs=[VMEM_SPEC] * len(inputs),
        out_specs=tuple(VMEM_SPEC for _ in outs),
        scratch_shapes=[pltpu.VMEM(shape, dtype) for shape, dtype in scratch],
        compiler_params=pltpu.CompilerParams(vmem_limit_bytes=40 * 1024 * 1024),
        cost_estimate=pl.CostEstimate(flops=10**8, bytes_accessed=2**22, transcendentals=0),
        name=name,
    )(*inputs)


def ring_up(values):
    count = lax.axis_size("ctx")
    return lax.ppermute(values, "ctx", [(i, i + 1) for i in range(count - 1)])


def ring_down(values):
    count = lax.axis_size("ctx")
    return lax.ppermute(values, "ctx", [(i + 1, i) for i in range(count - 1)])


def gather(shard):
    return lax.all_gather(shard, "fsdp", axis=0, tiled=True)


def scatter(total):
    return lax.psum_scatter(total.astype(jnp.bfloat16), "fsdp", scatter_dimension=0, tiled=True)


def exchange(values):
    return lax.all_to_all(values, "ctx", 0, 0, tiled=True)


def spread(values, axis):
    count = lax.axis_size(axis)
    copies = jnp.broadcast_to(values[None], (count,) + values.shape)
    return lax.all_to_all(copies, axis, 0, 0, tiled=True)


def added(pieces):
    return jnp.sum(pieces.astype(jnp.float32), axis=0).astype(jnp.bfloat16)


def sum_pieces(shard):
    parts = lax.axis_size("ctx")
    return added(exchange(shard.reshape((parts, -1) + shard.shape[1:])))


def turn_gather(piece, stride, count):
    parts = lax.axis_size("ctx")
    place = lax.axis_index("ctx") // stride % count
    whole = jnp.zeros((count,) + piece.shape, piece.dtype)
    whole = lax.dynamic_update_slice_in_dim(whole, piece[None], place, 0)
    for hop in range(1, count):
        pairs = []
        for source in range(parts):
            spot = source // stride % count
            pairs.append((source, source + ((spot + hop) % count - spot) * stride))
        got = lax.ppermute(piece, "ctx", pairs)
        whole = lax.dynamic_update_slice_in_dim(whole, got[None], (place - hop) % count, 0)
    return whole


def ring_gather(piece):
    inner = turn_gather(piece, 1, 4)
    return turn_gather(inner, 4, 4).reshape((-1,) + piece.shape[1:])


def hidden_split(weight):
    shaped = weight.reshape(weight.shape[0], GROUPS, 2, LB)
    return shaped.transpose(0, 2, 1, 3).reshape(weight.shape)


def hidden_join(weight):
    shaped = weight.reshape(weight.shape[0], 2, GROUPS, LB)
    return shaped.transpose(0, 2, 1, 3).reshape(weight.shape)


def side_by_side(weight):
    return jnp.concatenate([weight[:, :LB], weight[:, LB:]], axis=2).reshape(
        weight.shape[0] * LB, -1
    )


def one_above(weight):
    shaped = weight.reshape(-1, LB, weight.shape[1])
    cols = weight.shape[1] // 2
    return jnp.concatenate([shaped[:, :, :cols], shaped[:, :, cols:]], axis=1)


def hidden_pieces(pieces, width):
    return jnp.concatenate(
        [
            hidden_join(pieces[:, :width]),
            hidden_join(pieces[:, width : 2 * width]),
            pieces[:, 2 * width :],
        ],
        axis=1,
    )


def pack_small(parts, rows):
    flat = jnp.concatenate([part.reshape(-1) for part in parts])
    flat = jnp.pad(flat, (0, rows * SMALL - flat.shape[0]))
    return flat.reshape(SMALL, rows).transpose()


def small_sizes(shards):
    return (1024 // shards, CONV * CH // shards, CH // shards) + (MIX_HEADS // shards,) * 3 + (
        1024 // shards,
    )


def split_small(flat, shards):
    pieces = []
    start = 0
    for size in small_sizes(shards):
        pieces.append(flat[..., start : start + size])
        start += size
    return pieces


def local(
    tokens,
    cotangent,
    lengths,
    input_gain,
    query_weight,
    key_weight,
    value_weight,
    attention_out,
    mixer_in,
    state_in,
    step_in,
    conv_weight,
    conv_bias,
    step_bias,
    decay_log,
    skip_gain,
    mixer_out,
    feed_gain,
    gate_weight,
    up_weight,
    down_weight,
):
    shards = lax.axis_size("fsdp")
    parts = lax.axis_size("ctx")
    ctx_index = lax.axis_index("ctx")
    rows = input_gain.shape[0]
    small = pack_small(
        (input_gain, conv_weight, conv_bias, step_bias, decay_log, skip_gain, feed_gain), rows
    )
    pad_cols = 128 - MIX_HEADS - SMALL
    held = rows // LB
    width = gate_weight.shape[1]
    attn_rows = QW // GROUPS
    mix_rows = MIX // GROUPS
    first_all = gather(
        jnp.concatenate(
            [
                key_weight,
                value_weight,
                mixer_in[:, MIX:],
                state_in,
                step_in,
                small,
                jnp.zeros((rows, pad_cols), jnp.bfloat16),
                query_weight,
                mixer_in[:, :MIX],
            ],
            axis=1,
        )
    )
    later = jnp.concatenate(
        [
            side_by_side(
                jnp.concatenate(
                    [
                        attention_out.reshape(held, attn_rows, -1),
                        mixer_out.reshape(held, mix_rows, -1),
                    ],
                    axis=1,
                )
            ),
            hidden_split(gate_weight),
            hidden_split(up_weight),
            side_by_side(down_weight.reshape(held, 2 * LB, -1)),
        ],
        axis=1,
    )
    later = lax.dynamic_slice_in_dim(later, ctx_index * (rows // parts), rows // parts, 0)
    later_all = lax.all_gather(later, ("fsdp", "ctx"), axis=0, tiled=True)
    first_width = 2 * KW + CH + 128
    first_proj = first_all[:, :first_width]
    second_proj = first_all[:, first_width:]
    out_low = later_all[:, :1024]
    out_high = later_all[:, 1024:2048]
    gate_up_proj = later_all[:, 2048 : 2048 + 2 * width]
    down_low = later_all[:, 2048 + 2 * width : 3072 + 2 * width]
    down_high = later_all[:, 3072 + 2 * width :]
    step_at = 2 * KW + CH
    small_at = step_at + MIX_HEADS
    small_all = first_all[:, small_at : small_at + SMALL].astype(jnp.float32)
    small_all = small_all.reshape(shards, rows, SMALL).transpose(0, 2, 1).reshape(shards, -1)
    gain_in32, taps32, shift32, step_shift32, decay32, skip32, feed32 = split_small(
        small_all, shards
    )
    gain_in32 = gain_in32.reshape(-1)
    taps32 = taps32.reshape(shards, CONV, -1).transpose(1, 0, 2).reshape(CONV, CH)
    shift32 = shift32.reshape(-1)
    step_shift32 = step_shift32.reshape(-1)
    decay32 = decay32.reshape(-1)
    skip32 = skip32.reshape(-1)
    feed32 = feed32.reshape(-1)

    row_count = tokens.shape[1]
    half_rows = row_count // 2
    first_start = ctx_index * half_rows
    second_start = (2 * parts - 1 - ctx_index) * half_rows
    offsets = jnp.arange(half_rows, dtype=jnp.int32)
    places = jnp.concatenate([first_start + offsets, second_start + offsets])
    bounds = jnp.cumsum(lengths[0])
    doc_starts = jnp.max(
        jnp.where(bounds[None, :-1] <= places[:, None], bounds[None, :-1], 0), axis=1
    )
    row_limits = jnp.tile(
        jnp.stack([places, doc_starts]).reshape(2, 2, half_rows).transpose(1, 0, 2), (1, 1, HEADS)
    )
    own = ctx_index.reshape(1).astype(jnp.int32)
    cosine, sine_part = rope_tables(places)

    x_own = tokens[0]
    x_ext = jnp.concatenate(
        [x_own, ring_up(x_own[half_rows - 8 : half_rows]), ring_down(x_own[row_count - 8 :])]
    ).astype(jnp.float32)
    normed_ext = rms_scale(x_ext, gain_in32).astype(jnp.bfloat16)
    normed = normed_ext[:row_count]
    first_pre = product(normed_ext, first_proj)
    keys_rot = rotate(first_pre[:row_count, :KW], cosine, sine_part, 1.0).astype(jnp.bfloat16)
    values_low = first_pre[:row_count, KW : 2 * KW].astype(jnp.bfloat16)
    kv_own = jnp.concatenate([keys_rot, values_low], axis=1)
    holders = jnp.arange(parts, dtype=jnp.int32)[:, None, None]
    kv_all = exchange(jnp.where(holders > ctx_index, kv_own[:half_rows], kv_own[half_rows:]))
    starts_col = jnp.broadcast_to(doc_starts[:, None], (row_count, 128)).astype(jnp.int32)
    pad_heads = 128 - MIX_HEADS
    head_terms = jnp.pad(jnp.stack([step_shift32, decay32]), ((0, 6), (0, pad_heads)))
    taps_pad = jnp.pad(taps32, ((0, 4), (0, 0)))
    shift_row = shift32[None]
    skip_row = jnp.repeat(skip32, MIX_DIM)[None]
    conv_out, steps, sums, states, block_decay = kernel_call(
        mix_in_kernel,
        "mix_in",
        (
            ((row_count, CH), jnp.bfloat16),
            ((row_count, 128), jnp.float32),
            ((row_count, 128), jnp.float32),
            ((parts, 2, SLICE + EXTRA, STATE), jnp.bfloat16),
            ((2, 128), jnp.float32),
        ),
        (((LB + 8, CH), jnp.float32),),
        (own, first_pre, starts_col, taps_pad, shift_row, head_terms),
    )

    entries, factors = plain_call(
        scan_kernel,
        "state_scan",
        (
            ((parts, 2, SLICE, STATE), jnp.bfloat16),
            ((2, 128, 128), jnp.float32),
        ),
        (((128, 128), jnp.float32),),
        (exchange(states),),
    )
    entries = exchange(entries)

    second_pre = product(normed, second_proj)
    queries = rotate(second_pre[:, :QW], cosine, sine_part, 1.0).astype(jnp.bfloat16)
    gate_z = second_pre[:, QW:].astype(jnp.bfloat16)
    attended_low, log_totals = attend(own, row_limits, queries, kv_all, kv_own)

    scanned, gated_low = kernel_call(
        mix_out_kernel,
        "mix_out",
        (((row_count, MIX), jnp.float32), ((row_count, MIX), jnp.bfloat16)),
        (),
        (own, conv_out, steps, sums, starts_col, skip_row, entries, gate_z),
    )
    x_rows = x_ext[:row_count]
    gated_groups = gated_low.reshape(row_count, GROUPS, mix_rows)
    branch_low = jnp.concatenate(
        [
            attended_low.reshape(row_count, GROUPS, attn_rows),
            gated_groups[:, :, : LB - attn_rows],
        ],
        axis=2,
    ).reshape(row_count, -1)
    branch_high = gated_groups[:, :, LB - attn_rows :].reshape(row_count, -1)
    middle = x_rows + product(branch_low, out_low) + product(branch_high, out_high)
    normed_ff = rms_scale(middle, feed32).astype(jnp.bfloat16)
    gate_up = product(normed_ff, gate_up_proj)
    gate_vals = gate_up[:, :width]
    up_vals = gate_up[:, width:]
    activ = (jax.nn.silu(gate_vals) * up_vals).astype(jnp.bfloat16)
    activ_low = activ[:, :1024]
    activ_high = activ[:, 1024:]
    output = (
        middle + product(activ_low, down_low) + product(activ_high, down_high)
    ).astype(jnp.bfloat16)

    upstream = cotangent[0]
    d_activ = jnp.concatenate(
        [right_product(upstream, down_low), right_product(upstream, down_high)], axis=1
    )
    sig_gate = jax.nn.sigmoid(gate_vals)
    d_gate = d_activ * up_vals * sig_gate * (1.0 + gate_vals * (1.0 - sig_gate))
    d_up = d_activ * gate_vals * sig_gate
    d_gate_up = jnp.concatenate([d_gate, d_up], axis=1).astype(jnp.bfloat16)
    third_shard = scatter(
        stacked_gradients(
            ((normed_ff, d_gate_up), (activ_low, upstream), (activ_high, upstream)),
            512,
            "third_gradients",
        )
    )
    d_normed_ff = right_product(d_gate_up, gate_up_proj)
    _, feed_pull = jax.vjp(rms_scale, middle, feed32)
    d_middle_norm, d_feed_gain = feed_pull(d_normed_ff)
    d_middle = upstream.astype(jnp.float32) + d_middle_norm
    d_middle_low = d_middle.astype(jnp.bfloat16)
    d_branch_low = right_product(d_middle_low, out_low).astype(jnp.bfloat16)
    d_branch_high = right_product(d_middle_low, out_high).astype(jnp.bfloat16)

    d_queries, d_kv, d_kv_near = attend_back(
        own, row_limits, queries, kv_all, kv_own, attended_low, log_totals, d_branch_low
    )
    d_query_pre = rotate(d_queries, cosine, sine_part, -1.0).astype(jnp.bfloat16)

    d_gate_z, d_values_part, d_entries, d_keys_part, d_sums, d_steps, d_skip_cols = streamed_call(
        mix_back_kernel,
        "mix_back",
        (
            ((row_count, MIX), jnp.bfloat16),
            ((row_count, MIX), jnp.float32),
            ((parts, 2, SLICE, STATE), jnp.bfloat16),
            ((row_count, 2 * STATE), jnp.float32),
            ((row_count, 128), jnp.float32),
            ((row_count, 128), jnp.float32),
            ((2, MIX), jnp.float32),
        ),
        (((128, 128), jnp.float32), ((128, 128), jnp.float32)),
        (own, conv_out, steps, sums, starts_col, skip_row, entries, gate_z, scanned, d_branch_low, d_branch_high),
    )
    d_second = jnp.concatenate([d_query_pre, d_gate_z], axis=1)
    seen_back = exchange(d_entries)
    second_total = stacked_gradients(
        ((normed, d_second), (branch_low, d_middle_low), (branch_high, d_middle_low)),
        512,
        "second_gradients",
    )
    second_total, seen_back = lax.optimization_barrier((second_total, seen_back))
    second_shard = scatter(second_total)
    (afters,) = plain_call(
        scan_back_kernel,
        "state_scan_back",
        (((parts, 2, SLICE, STATE), jnp.bfloat16),),
        (),
        (seen_back, factors),
    )
    afters = exchange(afters)
    d_kv, afters = lax.optimization_barrier((d_kv, afters))
    d_kv_seen = exchange(d_kv)
    third_shard, d_kv_seen = lax.optimization_barrier((third_shard, d_kv_seen))
    third_pieces = hidden_pieces(sum_pieces(third_shard), width)
    second_shard, third_pieces = lax.optimization_barrier((second_shard, third_pieces))
    second_pieces = sum_pieces(second_shard)
    d_kv_seen = d_kv_seen.astype(jnp.float32)
    d_kv_own = d_kv_near + jnp.concatenate(
        [
            jnp.sum(jnp.where(holders > ctx_index, d_kv_seen, 0.0), axis=0),
            jnp.sum(jnp.where(holders < ctx_index, d_kv_seen, 0.0), axis=0),
        ]
    )
    d_key_pre = rotate(d_kv_own[:, :KW], cosine, sine_part, -1.0)
    d_kv_pre = jnp.concatenate([d_key_pre, d_kv_own[:, KW:]], axis=1).astype(jnp.bfloat16)
    d_main, d_taps_all, d_heads = streamed_call(
        mix_end_kernel,
        "mix_end",
        (
            ((row_count + 16, CH + 128), jnp.bfloat16),
            ((8, CH), jnp.float32),
            ((8, 128), jnp.float32),
        ),
        (
            ((LB + 8, CH), jnp.float32),
            ((LB + 8, CH), jnp.float32),
            ((LB, CH), jnp.float32),
            ((128, 128), jnp.float32),
            ((16, CH), jnp.float32),
        ),
        (
            own,
            conv_out,
            steps,
            sums,
            starts_col,
            first_pre,
            taps_pad,
            shift_row,
            head_terms,
            block_decay,
            entries,
            afters,
            d_values_part,
            d_keys_part,
            d_sums,
            d_steps,
        ),
    )
    d_step_shift = d_heads[0, :MIX_HEADS]
    d_decay = d_heads[1, :MIX_HEADS]
    d_skip = d_skip_cols.sum(axis=0).reshape(MIX_HEADS, MIX_DIM).sum(axis=1)
    d_first = jnp.concatenate([jnp.pad(d_kv_pre, ((0, 16), (0, 0))), d_main], axis=1)
    d_normed = right_product(d_first, first_proj) + jnp.pad(
        right_product(d_second, second_proj), ((0, 16), (0, 0))
    )
    _, input_pull = jax.vjp(rms_scale, x_ext, gain_in32)
    d_input_gain = input_pull(d_normed)[1]

    d_taps = (
        d_taps_all[:CONV].reshape(CONV, shards, -1).transpose(1, 0, 2)
    )
    d_small = jnp.concatenate(
        [
            piece.reshape(shards, -1)
            for piece in (
                d_input_gain,
                d_taps,
                d_taps_all[CONV],
                d_step_shift,
                d_decay,
                d_skip,
                d_feed_gain,
            )
        ],
        axis=1,
    )
    d_small = jnp.pad(d_small, ((0, 0), (0, rows * SMALL - d_small.shape[1])))
    small_cols = jnp.pad(
        d_small.reshape(shards, SMALL, rows).transpose(0, 2, 1).reshape(shards * rows, SMALL),
        ((0, 0), (small_at, first_width - small_at - SMALL)),
    )
    first_total = left_product(normed_ext, d_first) + small_cols
    first_total, d_normed = lax.optimization_barrier((first_total.astype(jnp.bfloat16), d_normed))
    first_shard = scatter(first_total)
    d_rows_norm = input_pull(d_normed)[0]
    edge_low = ring_down(d_rows_norm[row_count : row_count + 8])
    edge_high = ring_up(d_rows_norm[row_count + 8 :])
    input_grad = d_middle + d_rows_norm[:row_count]
    input_grad = input_grad.at[half_rows - 8 : half_rows].add(edge_low)
    input_grad = input_grad.at[row_count - 8 :].add(edge_high)[None]
    third_own = ring_gather(third_pieces).astype(jnp.float32)
    first_shard, second_pieces = lax.optimization_barrier((first_shard, second_pieces))
    first_pieces = sum_pieces(first_shard)
    both = spread(jnp.concatenate([first_pieces, second_pieces], axis=1), "ctx")
    (
        grad_query,
        grad_key,
        grad_value,
        grad_attn,
        grad_mixer,
        grad_state,
        grad_step_in,
        grad_out,
        small_turned,
    ) = plain_call(
        finish_kernel,
        "finish",
        tuple(
            (shape, jnp.float32)
            for shape in (
                (rows, QW),
                (rows, KW),
                (rows, KW),
                attention_out.shape,
                (rows, 2 * MIX),
                (rows, 2 * STATE),
                (rows, MIX_HEADS),
                mixer_out.shape,
                (128, rows),
            )
        ),
        (),
        (both.reshape(rows, -1),),
    )
    grad_gain, grad_taps, grad_shift, grad_step, grad_decay, grad_skip, grad_feed = split_small(
        small_turned[MIX_HEADS : MIX_HEADS + SMALL].reshape(-1), shards
    )
    return (
        output[None],
        input_grad,
        grad_gain,
        grad_query,
        grad_key,
        grad_value,
        grad_attn,
        grad_mixer,
        grad_state,
        grad_step_in,
        grad_taps.reshape(CONV, -1),
        grad_shift,
        grad_step,
        grad_decay,
        grad_skip,
        grad_out,
        grad_feed,
        third_own[:, :width],
        third_own[:, width : 2 * width],
        one_above(third_own[:, 2 * width :]).reshape(-1, 1024),
    )


def solution(mesh):
    return jax.shard_map(
        local,
        mesh=mesh,
        in_specs=(
            P("fsdp", "ctx", None),
            P("fsdp", "ctx", None),
            P("fsdp", None),
            P("fsdp"),
            P("fsdp", None),
            P("fsdp", None),
            P("fsdp", None),
            P("fsdp", None),
            P("fsdp", None),
            P("fsdp", None),
            P("fsdp", None),
            P(None, "fsdp"),
            P("fsdp"),
            P("fsdp"),
            P("fsdp"),
            P("fsdp"),
            P("fsdp", None),
            P("fsdp"),
            P("fsdp", None),
            P("fsdp", None),
            P("fsdp", None),
        ),
        out_specs=(
            P("fsdp", "ctx", None),
            P("fsdp", "ctx", None),
            P("fsdp"),
            P("fsdp", None),
            P("fsdp", None),
            P("fsdp", None),
            P("fsdp", None),
            P("fsdp", None),
            P("fsdp", None),
            P("fsdp", None),
            P(None, "fsdp"),
            P("fsdp"),
            P("fsdp"),
            P("fsdp"),
            P("fsdp"),
            P("fsdp", None),
            P("fsdp"),
            P("fsdp", None),
            P("fsdp", None),
            P("fsdp", None),
        ),
        check_vma=False,
    )
```

```python
import jax
import jax.numpy as jnp
from jax import lax
from jax.experimental import pallas as pl
from jax.experimental.pallas import tpu as pltpu
from jax.sharding import PartitionSpec as P

HEADS = 8
KV_HEADS = 2
HEAD_DIM = 64
MIX_HEADS = 24
MIX_DIM = 64
STATE = 128
CONV = 4
QW = 512
KW = 128
MIX = 1536
CH = 1792
LB = 128
SMALL = 11
GROUPS = 8


EPSILON = 1e-05
ROPE_BASE = 100000000000.0
HIGHEST = lax.Precision.HIGHEST
NEG_LARGE = -1e30


def product(left, right):
    return jnp.dot(left, right, preferred_element_type=jnp.float32)


def left_product(left, right):
    return lax.dot_general(
        left, right, (((0,), (0,)), ((), ())), preferred_element_type=jnp.float32
    )


def right_product(left, right):
    return lax.dot_general(
        left, right, (((1,), (1,)), ((), ())), preferred_element_type=jnp.float32
    )


def rms_scale(values, gain_vector):
    return (
        values
        * lax.rsqrt(jnp.mean(values * values, axis=-1, keepdims=True) + EPSILON)
        * gain_vector
    )


def rope_tables(places):
    half_dim = HEAD_DIM // 2
    inverse = ROPE_BASE ** (-jnp.arange(half_dim, dtype=jnp.float32) / half_dim)
    angles = places.astype(jnp.float32)[:, None] * inverse[None, :]
    return (jnp.tile(jnp.cos(angles), (1, 4)), jnp.tile(jnp.sin(angles), (1, 4)))


def swap_matrix(width):
    row = lax.broadcasted_iota(jnp.int32, (width, width), 0)
    col = lax.broadcasted_iota(jnp.int32, (width, width), 1)
    half_dim = HEAD_DIM // 2
    lower = col % HEAD_DIM < half_dim
    return jnp.where(
        lower & (row == col + half_dim),
        -1.0,
        jnp.where(~lower & (row == col - half_dim), 1.0, 0.0),
    ).astype(jnp.float32)


def rotate(values, cosine, sine_part, sign):
    width = values.shape[1]
    swapped = jnp.dot(values, swap_matrix(width), precision=HIGHEST)
    repeats = width // cosine.shape[1]
    return values * jnp.tile(cosine, (1, repeats)) + sign * swapped * jnp.tile(
        sine_part, (1, repeats)
    )


WIDE = HEADS * LB


def split_heads(rows, target, half, stride=HEAD_DIM):
    turned = jnp.transpose(rows.astype(jnp.float32))
    zeros = jnp.zeros((HEAD_DIM, LB), target.dtype)
    for head in range(HEADS):
        group = head // (HEADS // KV_HEADS)
        cols = slice(head * LB, (head + 1) * LB)
        own = slice(group * HEAD_DIM, (group + 1) * HEAD_DIM)
        other = slice((1 - group) * HEAD_DIM, (2 - group) * HEAD_DIM)
        target[half, own, cols] = turned[head * stride : head * stride + HEAD_DIM].astype(
            target.dtype
        )
        target[half, other, cols] = zeros


def join_heads(wide):
    pieces = []
    for head in range(HEADS):
        group = head // (HEADS // KV_HEADS)
        pieces.append(
            wide[group * HEAD_DIM : (group + 1) * HEAD_DIM, head * LB : (head + 1) * LB]
        )
    return jnp.transpose(jnp.concatenate(pieces, axis=0))


def block_mask(rows_ref, block, half):
    base = jnp.where(half == 0, block, 31 - block) * LB
    key_at = lax.broadcasted_iota(jnp.int32, (LB, WIDE), 0) + base
    return (key_at <= rows_ref[half, 0:1, :]) & (key_at >= rows_ref[half, 1:2, :])


def pair_at(step, own):
    half = (step >= own).astype(jnp.int32)
    return step + half, half


def transposed_dot(left, right):
    return lax.dot_general(
        left, right, (((0,), (0,)), ((), ())), preferred_element_type=jnp.float32
    )


def attend_kernel(
    own_ref, rows_ref, query_ref, kv_ref, near_ref, out_ref, log_ref, turned, total, peak, mass
):
    own = own_ref[0]
    for half in range(2):
        scaled = query_ref[half * LB : (half + 1) * LB, :] * 0.125
        split_heads(scaled, turned, half)

    def scores(keys, values, block, half):
        found = product(keys, turned[half])
        return jnp.where(block_mask(rows_ref, block, half), found, NEG_LARGE), values

    for half in range(2):
        near = near_ref[half * LB : (half + 1) * LB, :]
        found, values = scores(near[:, 0:KW], near[:, KW:], own, half)
        top = jnp.max(found, axis=0, keepdims=True)
        weights = jnp.exp(found - top)
        peak[half] = top
        mass[half] = jnp.sum(weights, axis=0, keepdims=True)
        total[half] = transposed_dot(values, weights.astype(jnp.bfloat16))

    def one(step, carry):
        block, half = pair_at(step, own)
        found, values = scores(
            kv_ref[block, :, 0:KW], kv_ref[block, :, KW : 2 * KW], block, half
        )
        old = peak[half]
        top = jnp.maximum(old, jnp.max(found, axis=0, keepdims=True))
        fade = jnp.exp(old - top)
        weights = jnp.exp(found - top)
        peak[half] = top
        mass[half] = mass[half] * fade + jnp.sum(weights, axis=0, keepdims=True)
        total[half] = total[half] * fade + transposed_dot(values, weights.astype(jnp.bfloat16))
        return carry

    lax.fori_loop(0, kv_ref.shape[0] - 1, one, 0)
    for half in range(2):
        out_ref[half * LB : (half + 1) * LB, :] = join_heads(total[half] / mass[half]).astype(
            out_ref.dtype
        )
        log_ref[half] = peak[half] + jnp.log(mass[half])


def attend_back_kernel(
    own_ref,
    rows_ref,
    query_ref,
    kv_ref,
    near_ref,
    out_ref,
    log_ref,
    up_ref,
    d_query_ref,
    d_kv_ref,
    d_near_ref,
    turned,
    turned_up,
    inner,
    total,
):
    own = own_ref[0]
    d_kv_ref[own] = jnp.zeros((LB, 2 * KW), d_kv_ref.dtype)
    for half in range(2):
        rows = slice(half * LB, (half + 1) * LB)
        split_heads(query_ref[rows, :] * 0.125, turned, half)
        split_heads(up_ref[rows, :], turned_up, half, LB)
        seen = jnp.transpose(out_ref[rows, :].astype(jnp.float32))
        for head in range(HEADS):
            group = head // (HEADS // KV_HEADS)
            cols = slice(head * LB, (head + 1) * LB)
            up = turned_up[half, group * HEAD_DIM : (group + 1) * HEAD_DIM, cols]
            inner[half, :, cols] = jnp.sum(
                seen[head * HEAD_DIM : (head + 1) * HEAD_DIM] * up.astype(jnp.float32),
                axis=0,
                keepdims=True,
            )
        total[half] = jnp.zeros((KW, WIDE), jnp.float32)

    def visit(keys, values, block, half):
        found = product(keys, turned[half])
        weights = jnp.where(
            block_mask(rows_ref, block, half), jnp.exp(found - log_ref[half]), 0.0
        )
        d_weights = product(values, turned_up[half])
        d_scores = (weights * (d_weights - inner[half])).astype(jnp.bfloat16)
        total[half] += transposed_dot(keys, d_scores)
        d_keys = right_product(d_scores, turned[half])
        d_values = right_product(weights.astype(jnp.bfloat16), turned_up[half])
        return d_keys, d_values

    for half in range(2):
        rows = slice(half * LB, (half + 1) * LB)
        near = near_ref[rows, :]
        d_keys, d_values = visit(near[:, 0:KW], near[:, KW:], own, half)
        d_near_ref[rows, 0:KW] = d_keys
        d_near_ref[rows, KW:] = d_values

    def one(step, carry):
        block, half = pair_at(step, own)
        d_keys, d_values = visit(
            kv_ref[block, :, 0:KW], kv_ref[block, :, KW : 2 * KW], block, half
        )
        d_kv_ref[block, :, 0:KW] = d_keys.astype(d_kv_ref.dtype)
        d_kv_ref[block, :, KW : 2 * KW] = d_values.astype(d_kv_ref.dtype)
        return carry

    lax.fori_loop(0, kv_ref.shape[0] - 1, one, 0)
    for half in range(2):
        d_query_ref[half * LB : (half + 1) * LB, :] = join_heads(total[half]) * 0.125


VMEM_SPEC = pl.BlockSpec(memory_space=pltpu.VMEM)
SMEM_SPEC = pl.BlockSpec(memory_space=pltpu.SMEM)


def attend(own, rows, queries, kv_all, near):
    return pl.pallas_call(
        attend_kernel,
        out_shape=(
            jax.ShapeDtypeStruct((2 * LB, QW), jnp.bfloat16),
            jax.ShapeDtypeStruct((2, 1, WIDE), jnp.float32),
        ),
        in_specs=[SMEM_SPEC] + [VMEM_SPEC] * 4,
        out_specs=(VMEM_SPEC, VMEM_SPEC),
        scratch_shapes=[
            pltpu.VMEM((2, KW, WIDE), jnp.bfloat16),
            pltpu.VMEM((2, KW, WIDE), jnp.float32),
            pltpu.VMEM((2, 1, WIDE), jnp.float32),
            pltpu.VMEM((2, 1, WIDE), jnp.float32),
        ],
        compiler_params=pltpu.CompilerParams(vmem_limit_bytes=32 * 1024 * 1024),
        cost_estimate=pl.CostEstimate(
            flops=17 * 4 * LB * KW * WIDE, bytes_accessed=3 * 2**20, transcendentals=17 * LB * WIDE
        ),
        name="attend",
    )(own, rows, queries, kv_all, near)


def attend_back(own, rows, queries, kv_all, near, attended, logs, upstream):
    return streamed_call(
        attend_back_kernel,
        "attend_back",
        (
            ((2 * LB, QW), jnp.float32),
            (kv_all.shape, jnp.bfloat16),
            (near.shape, jnp.float32),
        ),
        (
            ((2, KW, WIDE), jnp.bfloat16),
            ((2, KW, WIDE), jnp.bfloat16),
            ((2, 1, WIDE), jnp.float32),
            ((2, KW, WIDE), jnp.float32),
        ),
        (own, rows, queries, kv_all, near, attended, logs, upstream),
    )


SLICE = MIX // 16
EXTRA = 16


def row_pieces(pair):
    start = pair * PAIR
    pieces = []
    done = 0
    while done < PAIR:
        chunk, offset = divmod(start + done, SLICE)
        count = min(SLICE - offset, PAIR - done)
        pieces.append((chunk, offset, done, count))
        done += count
    return pieces


def put_rows(ref, half, pair, value):
    for chunk, offset, done, count in row_pieces(pair):
        ref[chunk, half, offset : offset + count, :] = value[done : done + count]


def take_rows(ref, half, pair):
    return jnp.concatenate(
        [
            ref[chunk, half, offset : offset + count, :]
            for chunk, offset, _, count in row_pieces(pair)
        ],
        axis=0,
    )


def put_decays(ref, half, decay):
    lane = lax.broadcasted_iota(jnp.int32, (1, 128), 1)
    level = lax.broadcasted_iota(jnp.int32, (EXTRA, 128), 0)
    for chunk in range(ref.shape[0]):
        first = chunk * SLICE // MIX_DIM
        last = ((chunk + 1) * SLICE - 1) // MIX_DIM
        row = jnp.zeros((1, 128), jnp.float32)
        for head in range(first, last + 1):
            row = jnp.where(lane >= head * MIX_DIM - chunk * SLICE, decay[:, head : head + 1], row)
        high = row.astype(jnp.bfloat16).astype(jnp.float32)
        ref[chunk, half, SLICE:, :] = jnp.where(
            level == 0, high, jnp.where(level == 1, row - high, 0.0)
        ).astype(jnp.bfloat16)


def scan_kernel(seen_ref, entry_ref, factor_ref, rows):
    count = seen_ref.shape[0]
    rows[...] = jnp.zeros(rows.shape, jnp.float32)
    for half in range(2):
        for place in range(count):
            extra = seen_ref[place, half, SLICE:, :].astype(jnp.float32)
            rows[place : place + 1, :] = extra[0:1, :] + extra[1:2, :]
        factors = jnp.transpose(rows[...])
        factor_ref[half] = factors
        state = jnp.zeros((SLICE, STATE), jnp.float32)
        for step in range(count):
            place = step if half == 0 else count - 1 - step
            entry_ref[place, half] = state.astype(jnp.bfloat16)
            state = factors[:SLICE, place : place + 1] * state + seen_ref[
                place, half, 0:SLICE, :
            ].astype(jnp.float32)


def scan_back_kernel(seen_ref, factor_ref, after_ref):
    count = seen_ref.shape[0]
    for half in range(2):
        factors = factor_ref[half]
        state = jnp.zeros((SLICE, STATE), jnp.float32)
        for step in range(count):
            place = count - 1 - step if half == 0 else step
            after_ref[place, half] = state.astype(jnp.bfloat16)
            state = factors[:SLICE, place : place + 1] * state + seen_ref[place, half].astype(
                jnp.float32
            )


PAIRS = MIX_HEADS // 2
PAIR = 2 * MIX_DIM


def lane_is_low():
    return lax.broadcasted_iota(jnp.int32, (LB, PAIR), 1) < MIX_DIM


def spread_pair(columns, pair, low_lanes):
    return jnp.where(
        low_lanes, columns[:, 2 * pair : 2 * pair + 1], columns[:, 2 * pair + 1 : 2 * pair + 2]
    )


def low_dot(left, right, left_dim, right_dim):
    return lax.dot_general(
        left.astype(jnp.bfloat16),
        right.astype(jnp.bfloat16),
        (((left_dim,), (right_dim,)), ((), ())),
        preferred_element_type=jnp.float32,
    )


def exact_dot(left, right):
    return jnp.dot(left, right, precision=HIGHEST, preferred_element_type=jnp.float32)


def triangle(lower):
    row = lax.broadcasted_iota(jnp.int32, (LB, LB), 0)
    col = lax.broadcasted_iota(jnp.int32, (LB, LB), 1)
    return jnp.where(col <= row if lower else col >= row, 1.0, 0.0).astype(jnp.float32)


def softplus(values):
    return jnp.maximum(values, 0.0) + jnp.log1p(jnp.exp(-jnp.abs(values)))


def sigmoid(values):
    return 1.0 / (1.0 + jnp.exp(-values))


def block_base(own, half):
    return (own if half == 0 else 31 - own) * LB


def stage_rows(pre_ref, stage, half):
    edge = 2 * LB + 8 * half
    cols = slice(2 * KW, 2 * KW + CH)
    stage[0:8, :] = pre_ref[edge : edge + 8, cols].astype(jnp.bfloat16).astype(jnp.float32)
    stage[8 : 8 + LB, :] = (
        pre_ref[half * LB : (half + 1) * LB, cols].astype(jnp.bfloat16).astype(jnp.float32)
    )


def window(stage, starts, base, offset):
    back = CONV - 1 - offset
    at = lax.broadcasted_iota(jnp.int32, (LB, 1), 0) + base - back
    keep = jnp.where(at >= starts, 1.0, 0.0)
    return stage[8 - back : 8 - back + LB, :] * keep


def mix_in_kernel(
    own_ref, pre_ref, starts_ref, taps_ref, shift_ref, heads_ref, conv_ref, step_ref, sum_ref,
    state_ref, decay_ref, stage
):
    own = own_ref[0]
    low_lanes = lane_is_low()
    lower = triangle(True)
    for half in range(2):
        rows = slice(half * LB, (half + 1) * LB)
        base = block_base(own, half)
        starts = starts_ref[rows, 0:1]
        stage_rows(pre_ref, stage, half)
        total = jnp.zeros((LB, CH), jnp.float32) + shift_ref[0:1, :]
        for offset in range(CONV):
            total = total + taps_ref[offset : offset + 1, :] * window(stage, starts, base, offset)
        conv_ref[rows, :] = (total * sigmoid(total)).astype(jnp.bfloat16)
        step = softplus(pre_ref[rows, 2 * KW + CH :] + heads_ref[0:1, :])
        summed = exact_dot(lower, -step * jnp.exp(heads_ref[1:2, :]))
        step_ref[rows, :] = step
        sum_ref[rows, :] = summed
        last = summed[LB - 1 : LB, :]
        same = starts == starts[LB - 1 : LB, :]
        weight = jnp.where(same, jnp.exp(last - summed), 0.0) * step
        decay = jnp.where(starts[LB - 1 : LB, :] < base, jnp.exp(last), 0.0)
        decay_ref[half : half + 1, :] = decay
        put_decays(state_ref, half, decay)
        write = conv_ref[rows, MIX : MIX + STATE]
        for pair in range(PAIRS):
            cols = slice(pair * PAIR, (pair + 1) * PAIR)
            driven = conv_ref[rows, cols].astype(jnp.float32) * spread_pair(weight, pair, low_lanes)
            put_rows(state_ref, half, pair, low_dot(driven, write, 0, 0).astype(jnp.bfloat16))


def block_terms(conv_ref, step_ref, sum_ref, starts_ref, rows, base):
    starts = starts_ref[rows, 0:1]
    summed = sum_ref[rows, :]
    step = step_ref[rows, :]
    summed_t = jnp.transpose(summed)
    step_t = jnp.transpose(step)
    row = lax.broadcasted_iota(jnp.int32, (LB, LB), 0)
    col = lax.broadcasted_iota(jnp.int32, (LB, LB), 1)
    allowed = (col <= row) & (col + base >= starts)
    write = conv_ref[rows, MIX : MIX + STATE]
    read = conv_ref[rows, MIX + STATE :]
    inner = low_dot(read, write, 1, 1)
    carried = jnp.where(starts < base, jnp.exp(summed), 0.0)
    return summed, step, summed_t, step_t, allowed, write, read, inner, carried


def head_decay(summed, summed_t, allowed, head):
    spread = summed[:, head : head + 1] - summed_t[head : head + 1, :]
    return jnp.exp(jnp.where(allowed, spread, NEG_LARGE))


def mix_out_kernel(
    own_ref, conv_ref, step_ref, sum_ref, starts_ref, skip_ref, entry_ref, gate_ref, attended_ref,
    scan_ref, low_ref, high_ref
):
    own = own_ref[0]
    low_lanes = lane_is_low()
    for half in range(2):
        rows = slice(half * LB, (half + 1) * LB)
        summed, step, summed_t, step_t, allowed, write, read, inner, carried = block_terms(
            conv_ref, step_ref, sum_ref, starts_ref, rows, block_base(own, half)
        )
        heads = []
        for pair in range(PAIRS):
            cols = slice(pair * PAIR, (pair + 1) * PAIR)
            values = conv_ref[rows, cols]
            found = []
            for head in (2 * pair, 2 * pair + 1):
                mixing = (
                    head_decay(summed, summed_t, allowed, head) * inner * step_t[head : head + 1, :]
                )
                found.append(low_dot(mixing, values, 1, 0))
            total = jnp.where(low_lanes, found[0], found[1])
            total = total + spread_pair(carried, pair, low_lanes) * low_dot(
                read, take_rows(entry_ref, half, pair), 1, 1
            )
            total = total + skip_ref[0:1, cols] * values.astype(jnp.float32)
            gate = gate_ref[rows, cols].astype(jnp.float32)
            scan_ref[rows, cols] = total
            gated = total * gate * sigmoid(gate)
            turned = pltpu.roll(gated, MIX_DIM, 1)
            for place in range(2):
                turn = (2 * pair + place) % (MIX_HEADS // GROUPS)
                heads.append(gated if (turn != 1) == (place == 1) else turned)
        for group in range(GROUPS):
            attended = attended_ref[
                rows, group // 2 * LB : (group // 2 + 1) * LB
            ].astype(jnp.float32)
            if group % 2 == 1:
                attended = pltpu.roll(attended, MIX_DIM, 1)
            cols = slice(group * LB, (group + 1) * LB)
            low_ref[rows, cols] = jnp.where(low_lanes, attended, heads[3 * group]).astype(
                jnp.bfloat16
            )
            high_ref[rows, cols] = jnp.where(
                low_lanes, heads[3 * group + 1], heads[3 * group + 2]
            ).astype(jnp.bfloat16)


def branch_pair(low_ref, high_ref, rows, pair, low_lanes):
    found = []
    for place in range(2):
        group, turn = divmod(2 * pair + place, MIX_HEADS // GROUPS)
        source = low_ref if turn == 0 else high_ref
        block = source[rows, group * LB : (group + 1) * LB].astype(jnp.float32)
        if (turn != 1) != (place == 1):
            block = pltpu.roll(block, MIX_DIM, 1)
        found.append(block)
    return jnp.where(low_lanes, found[0], found[1])


def mix_back_kernel(
    own_ref, conv_ref, step_ref, sum_ref, starts_ref, skip_ref, entry_ref, gate_ref, scan_ref,
    up_low_ref, up_high_ref, d_gate_ref, d_values_ref, d_entry_ref, d_keys_ref, d_sum_ref, d_step_ref, d_skip_ref,
    row_a, row_b
):
    own = own_ref[0]
    low_lanes = lane_is_low()
    lane = lax.broadcasted_iota(jnp.int32, (LB, LB), 1)
    row_a[...] = jnp.zeros(row_a.shape, jnp.float32)
    row_b[...] = jnp.zeros(row_b.shape, jnp.float32)
    for half in range(2):
        rows = slice(half * LB, (half + 1) * LB)
        summed, step, summed_t, step_t, allowed, write, read, inner, carried = block_terms(
            conv_ref, step_ref, sum_ref, starts_ref, rows, block_base(own, half)
        )
        d_inner = jnp.zeros((LB, LB), jnp.float32)
        d_read = jnp.zeros((LB, STATE), jnp.float32)
        d_sum = jnp.zeros((LB, LB), jnp.float32)
        for pair in range(PAIRS):
            cols = slice(pair * PAIR, (pair + 1) * PAIR)
            values = conv_ref[rows, cols]
            values32 = values.astype(jnp.float32)
            gate = gate_ref[rows, cols].astype(jnp.float32)
            sig = sigmoid(gate)
            up = branch_pair(up_low_ref, up_high_ref, rows, pair, low_lanes)
            d_scan = up * gate * sig
            d_gate_ref[rows, cols] = (
                up * scan_ref[rows, cols] * sig * (1.0 + gate * (1.0 - sig))
            ).astype(jnp.bfloat16)
            d_skip_ref[half : half + 1, cols] = jnp.sum(d_scan * values32, axis=0, keepdims=True)
            d_values = skip_ref[0:1, cols] * d_scan
            entry = take_rows(entry_ref, half, pair)
            through = low_dot(read, entry, 1, 1) * d_scan
            for place in range(2):
                head = 2 * pair + place
                own_lanes = low_lanes if place == 0 else jnp.logical_not(low_lanes)
                d_own = jnp.where(own_lanes, d_scan, 0.0).astype(jnp.bfloat16)
                decay = head_decay(summed, summed_t, allowed, head)
                step_row = step_t[head : head + 1, :]
                raw = low_dot(d_own, values, 1, 1) * decay
                scaled = raw * step_row
                d_inner = d_inner + scaled
                mixed = decay * inner * step_row
                d_values = d_values + low_dot(mixed, d_own, 0, 0)
                kept = raw * inner
                by_key = jnp.sum(kept, axis=0, keepdims=True)
                row_a[head : head + 1, :] = by_key
                row_b[head : head + 1, :] = by_key * step_row
                by_row = jnp.sum(scaled * inner, axis=1, keepdims=True) + carried[
                    :, head : head + 1
                ] * jnp.sum(jnp.where(own_lanes, through, 0.0), axis=1, keepdims=True)
                d_sum = d_sum + jnp.where(lane == head, by_row, 0.0)
            d_values_ref[rows, cols] = d_values
            d_carry = (d_scan * spread_pair(carried, pair, low_lanes)).astype(jnp.bfloat16)
            d_read = d_read + low_dot(d_carry, entry, 1, 0)
            put_rows(d_entry_ref, half, pair, low_dot(d_carry, read, 0, 0).astype(jnp.bfloat16))
        d_keys_ref[rows, 0:STATE] = low_dot(d_inner, read, 0, 0)
        d_keys_ref[rows, STATE:] = d_read + low_dot(d_inner, write, 1, 0)
        d_sum_ref[rows, :] = d_sum - jnp.transpose(row_b[...])
        d_step_ref[rows, :] = jnp.transpose(row_a[...])


def mix_end_kernel(
    own_ref, conv_ref, step_ref, sum_ref, starts_ref, pre_ref, taps_ref, shift_ref, heads_ref,
    decay_ref, entry_ref, after_ref, d_values_ref, d_keys_ref, d_sum_ref, d_step_ref,
    d_pre_ref, d_taps_ref, d_heads_ref, stage, d_stage, d_conv, meet, edges
):
    own = own_ref[0]
    low_lanes = lane_is_low()
    lane = lax.broadcasted_iota(jnp.int32, (LB, LB), 1)
    upper = triangle(False)
    rate = jnp.exp(heads_ref[1:2, :])
    d_pre_ref[2 * LB :, CH:] = jnp.zeros((16, 128), d_pre_ref.dtype)
    meet[...] = jnp.zeros(meet.shape, jnp.float32)
    d_taps_ref[...] = jnp.zeros(d_taps_ref.shape, jnp.float32)
    d_heads_ref[...] = jnp.zeros(d_heads_ref.shape, jnp.float32)
    for half in range(2):
        rows = slice(half * LB, (half + 1) * LB)
        base = block_base(own, half)
        starts = starts_ref[rows, 0:1]
        summed = sum_ref[rows, :]
        step = step_ref[rows, :]
        last = summed[LB - 1 : LB, :]
        same = starts == starts[LB - 1 : LB, :]
        fade = jnp.where(same, jnp.exp(last - summed), 0.0)
        weight = fade * step
        write = conv_ref[rows, MIX : MIX + STATE]
        d_write = jnp.zeros((LB, STATE), jnp.float32)
        d_weight = jnp.zeros((LB, LB), jnp.float32)
        for pair in range(PAIRS):
            cols = slice(pair * PAIR, (pair + 1) * PAIR)
            values = conv_ref[rows, cols].astype(jnp.float32)
            after = take_rows(after_ref, half, pair)
            reach = low_dot(write, after, 1, 1)
            wide = spread_pair(weight, pair, low_lanes)
            d_conv[:, cols] = d_values_ref[rows, cols] + wide * reach
            d_write = d_write + low_dot(values * wide, after, 1, 0)
            both = values * reach
            overlap = after.astype(jnp.float32) * take_rows(
                entry_ref, half, pair
            ).astype(jnp.float32)
            for place in range(2):
                head = 2 * pair + place
                own_lanes = low_lanes if place == 0 else jnp.logical_not(low_lanes)
                column = jnp.sum(jnp.where(own_lanes, both, 0.0), axis=1, keepdims=True)
                d_weight = d_weight + jnp.where(lane == head, column, 0.0)
                meet[head : head + 1, :] = jnp.sum(
                    overlap[place * MIX_DIM : (place + 1) * MIX_DIM], axis=0, keepdims=True
                )
        d_conv[:, MIX : MIX + STATE] = d_keys_ref[rows, 0:STATE] + d_write
        d_conv[:, MIX + STATE :] = d_keys_ref[rows, STATE:]
        met = jnp.sum(jnp.transpose(meet[...]), axis=0, keepdims=True)
        moved = d_weight * weight
        d_last = (
            jnp.sum(moved, axis=0, keepdims=True) + decay_ref[half : half + 1, :] * met
        )
        at_last = lax.broadcasted_iota(jnp.int32, (LB, LB), 0) == LB - 1
        d_sum = d_sum_ref[rows, :] - moved + jnp.where(at_last, d_last, 0.0)
        d_rate = exact_dot(upper, d_sum)
        d_step = d_step_ref[rows, :] + d_weight * fade - d_rate * rate
        raw = pre_ref[rows, 2 * KW + CH :] + heads_ref[0:1, :]
        d_raw = jnp.where(lane < MIX_HEADS, d_step * sigmoid(raw), 0.0)
        d_heads_ref[0:1, :] += jnp.sum(d_raw, axis=0, keepdims=True)
        d_heads_ref[1:2, :] += jnp.sum(-d_rate * step * rate, axis=0, keepdims=True)
        d_pre_ref[rows, CH:] = d_raw.astype(d_pre_ref.dtype)
        stage_rows(pre_ref, stage, half)
        total = jnp.zeros((LB, CH), jnp.float32) + shift_ref[0:1, :]
        for offset in range(CONV):
            total = total + taps_ref[offset : offset + 1, :] * window(stage, starts, base, offset)
        sig = sigmoid(total)
        d_total = d_conv[...] * sig * (1.0 + total * (1.0 - sig))
        d_taps_ref[CONV : CONV + 1, :] += jnp.sum(d_total, axis=0, keepdims=True)
        d_stage[...] = jnp.zeros(d_stage.shape, jnp.float32)
        for offset in range(CONV):
            back = CONV - 1 - offset
            at = lax.broadcasted_iota(jnp.int32, (LB, 1), 0) + base - back
            keep = jnp.where(at >= starts, 1.0, 0.0)
            kept = d_total * keep
            seen = stage[8 - back : 8 - back + LB, :]
            d_taps_ref[offset : offset + 1, :] += jnp.sum(kept * seen, axis=0, keepdims=True)
            d_stage[8 - back : 8 - back + LB, :] += taps_ref[offset : offset + 1, :] * kept
        edges[8 * half : 8 * half + 8, :] = d_stage[0:8, :]
        d_pre_ref[rows, 0:CH] = d_stage[8 : 8 + LB, :].astype(d_pre_ref.dtype)
    d_pre_ref[2 * LB :, 0:CH] = edges[...].astype(d_pre_ref.dtype)


def whole_spec(shape):
    return pl.BlockSpec(shape, lambda step: (0,) * len(shape))


def streamed_call(kernel, name, shapes, scratch, inputs):
    outs = tuple(jax.ShapeDtypeStruct(shape, dtype) for shape, dtype in shapes)
    return pl.pallas_call(
        kernel,
        grid=(1,),
        out_shape=outs,
        in_specs=[SMEM_SPEC] + [whole_spec(value.shape) for value in inputs[1:]],
        out_specs=tuple(whole_spec(out.shape) for out in outs),
        scratch_shapes=[pltpu.VMEM(shape, dtype) for shape, dtype in scratch],
        compiler_params=pltpu.CompilerParams(vmem_limit_bytes=48 * 1024 * 1024),
        cost_estimate=pl.CostEstimate(
            flops=2 * 10**9, bytes_accessed=10**7, transcendentals=10**6
        ),
        name=name,
    )(*inputs)


def kernel_call(kernel, name, shapes, scratch, inputs):
    outs = tuple(jax.ShapeDtypeStruct(shape, dtype) for shape, dtype in shapes)
    moved = sum(value.size * value.dtype.itemsize for value in inputs) + sum(
        out.size * out.dtype.itemsize for out in outs
    )
    return pl.pallas_call(
        kernel,
        out_shape=outs,
        in_specs=[SMEM_SPEC] + [VMEM_SPEC] * (len(inputs) - 1),
        out_specs=tuple(VMEM_SPEC for _ in outs),
        scratch_shapes=[pltpu.VMEM(shape, dtype) for shape, dtype in scratch],
        compiler_params=pltpu.CompilerParams(vmem_limit_bytes=40 * 1024 * 1024),
        cost_estimate=pl.CostEstimate(
            flops=2 * 10**9, bytes_accessed=moved, transcendentals=10**6
        ),
        name=name,
    )(*inputs)


def finish_kernel(
    first_ref, second_ref, query_ref, key_ref, value_ref, attn_ref, mixer_ref, state_ref, step_ref, out_ref,
    small_ref
):
    def part(start, count):
        return first_ref[:, start : start + count].astype(jnp.float32)

    key_ref[...] = part(0, KW)
    value_ref[...] = part(KW, KW)
    mixer_ref[:, MIX:] = part(2 * KW, MIX)
    state_ref[...] = part(2 * KW + MIX, 2 * STATE)
    tail = part(2 * KW + CH, 128)
    step_ref[...] = tail[:, :MIX_HEADS]
    small_ref[...] = jnp.transpose(tail)
    query_ref[...] = second_ref[:, :QW].astype(jnp.float32)
    mixer_ref[:, :MIX] = second_ref[:, QW : QW + MIX].astype(jnp.float32)
    start = QW + MIX
    width = out_ref.shape[1]
    attn_rows = QW // GROUPS
    mix_rows = MIX // GROUPS
    for group in range(second_ref.shape[0] // LB):
        low = second_ref[group * LB : (group + 1) * LB, start : start + width].astype(jnp.float32)
        high = second_ref[group * LB : (group + 1) * LB, start + width :].astype(jnp.float32)
        attn_ref[group * attn_rows : (group + 1) * attn_rows, :] = low[:attn_rows]
        at = group * mix_rows
        out_ref[at : at + LB - attn_rows, :] = low[attn_rows:]
        out_ref[at + LB - attn_rows : at + mix_rows, :] = high


def grad_kernel(counts, *refs):
    sides = len(counts)
    left_refs, right_refs = refs[:sides], refs[sides : 2 * sides]
    out_ref, turned = refs[2 * sides], refs[2 * sides + 1 :]
    step = pl.program_id(0)

    @pl.when(step == 0)
    def _():
        for left_ref, held in zip(left_refs, turned):
            held[...] = jnp.transpose(left_ref[0 : held.shape[1], :])

    start = 0
    for count, right_ref, held in zip(counts, right_refs, turned):

        @pl.when((step >= start) & (step < start + count))
        def _(right_ref=right_ref, held=held):
            out_ref[...] = product(held[...], right_ref[...]).astype(out_ref.dtype)

        start += count


def stacked_gradients(pairs, block, name):
    counts = tuple(right.shape[1] // block for _, right in pairs)
    starts = [sum(counts[:place]) for place in range(len(counts))]

    def right_spec(place):
        def at(step):
            return (0, jnp.clip(step - starts[place], 0, counts[place] - 1))

        return pl.BlockSpec((pairs[place][1].shape[0], block), at)

    lefts = [left for left, _ in pairs]
    rights = [right for _, right in pairs]
    height = lefts[0].shape[1]
    total = sum(counts) * block
    flops = sum(2 * left.shape[0] * height * right.shape[1] for left, right in pairs)
    return pl.pallas_call(
        lambda *refs: grad_kernel(counts, *refs),
        grid=(sum(counts),),
        out_shape=jax.ShapeDtypeStruct((height, total), jnp.bfloat16),
        in_specs=[pl.BlockSpec(left.shape, lambda step: (0, 0)) for left in lefts]
        + [right_spec(place) for place in range(len(pairs))],
        out_specs=pl.BlockSpec((height, block), lambda step: (0, step)),
        scratch_shapes=[
            pltpu.VMEM((height, right.shape[0]), jnp.bfloat16) for right in rights
        ],
        compiler_params=pltpu.CompilerParams(vmem_limit_bytes=40 * 1024 * 1024),
        cost_estimate=pl.CostEstimate(
            flops=flops, bytes_accessed=2 * height * total, transcendentals=0
        ),
        name=name,
    )(*lefts, *rights)


def plain_call(kernel, name, shapes, scratch, inputs):
    outs = tuple(jax.ShapeDtypeStruct(shape, dtype) for shape, dtype in shapes)
    return pl.pallas_call(
        kernel,
        out_shape=outs,
        in_specs=[VMEM_SPEC] * len(inputs),
        out_specs=tuple(VMEM_SPEC for _ in outs),
        scratch_shapes=[pltpu.VMEM(shape, dtype) for shape, dtype in scratch],
        compiler_params=pltpu.CompilerParams(vmem_limit_bytes=40 * 1024 * 1024),
        cost_estimate=pl.CostEstimate(flops=10**8, bytes_accessed=2**22, transcendentals=0),
        name=name,
    )(*inputs)


def ring_up(values):
    count = lax.axis_size("ctx")
    return lax.ppermute(values, "ctx", [(i, i + 1) for i in range(count - 1)])


def ring_down(values):
    count = lax.axis_size("ctx")
    return lax.ppermute(values, "ctx", [(i + 1, i) for i in range(count - 1)])


def gather(shard):
    return lax.all_gather(shard, "fsdp", axis=0, tiled=True)


def scatter(total):
    return lax.psum_scatter(total.astype(jnp.bfloat16), "fsdp", scatter_dimension=0, tiled=True)


def exchange(values):
    return lax.all_to_all(values, "ctx", 0, 0, tiled=True)


def spread(values, axis):
    count = lax.axis_size(axis)
    copies = jnp.broadcast_to(values[None], (count,) + values.shape)
    return lax.all_to_all(copies, axis, 0, 0, tiled=True)


def added(pieces):
    return jnp.sum(pieces.astype(jnp.float32), axis=0).astype(jnp.bfloat16)


def sum_pieces(shard):
    parts = lax.axis_size("ctx")
    return added(exchange(shard.reshape((parts, -1) + shard.shape[1:])))


def turn_moves(piece, stride, count):
    parts = lax.axis_size("ctx")
    moved = []
    for hop in range(1, count):
        pairs = []
        for source in range(parts):
            spot = source // stride % count
            pairs.append((source, source + ((spot + hop) % count - spot) * stride))
        moved.append(lax.ppermute(piece, "ctx", pairs))
    return moved


def turn_place(piece, moved, stride, count):
    place = lax.axis_index("ctx") // stride % count
    whole = jnp.zeros((count,) + piece.shape, piece.dtype)
    whole = lax.dynamic_update_slice_in_dim(whole, piece[None], place, 0)
    for hop, got in enumerate(moved, 1):
        whole = lax.dynamic_update_slice_in_dim(whole, got[None], (place - hop) % count, 0)
    return whole


def turn_gather(piece, stride, count):
    return turn_place(piece, turn_moves(piece, stride, count), stride, count)


def hidden_split(weight):
    shaped = weight.reshape(weight.shape[0], GROUPS, 2, LB)
    return shaped.transpose(0, 2, 1, 3).reshape(weight.shape)


def hidden_join(weight):
    shaped = weight.reshape(weight.shape[0], 2, GROUPS, LB)
    return shaped.transpose(0, 2, 1, 3).reshape(weight.shape)


def side_by_side(weight):
    return jnp.concatenate([weight[:, :LB], weight[:, LB:]], axis=2).reshape(
        weight.shape[0] * LB, -1
    )


def one_above(weight):
    shaped = weight.reshape(-1, LB, weight.shape[1])
    cols = weight.shape[1] // 2
    return jnp.concatenate([shaped[:, :, :cols], shaped[:, :, cols:]], axis=1)


def hidden_pieces(pieces, width):
    return jnp.concatenate(
        [
            hidden_join(pieces[:, :width]),
            hidden_join(pieces[:, width : 2 * width]),
            pieces[:, 2 * width :],
        ],
        axis=1,
    )


def pack_small(parts, rows):
    flat = jnp.concatenate([part.reshape(-1) for part in parts])
    flat = jnp.pad(flat, (0, rows * SMALL - flat.shape[0]))
    return flat.reshape(SMALL, rows).transpose()


def small_sizes(shards):
    return (1024 // shards, CONV * CH // shards, CH // shards) + (MIX_HEADS // shards,) * 3 + (
        1024 // shards,
    )


def split_small(flat, shards):
    pieces = []
    start = 0
    for size in small_sizes(shards):
        pieces.append(flat[..., start : start + size])
        start += size
    return pieces


def local(
    tokens,
    cotangent,
    lengths,
    input_gain,
    query_weight,
    key_weight,
    value_weight,
    attention_out,
    mixer_in,
    state_in,
    step_in,
    conv_weight,
    conv_bias,
    step_bias,
    decay_log,
    skip_gain,
    mixer_out,
    feed_gain,
    gate_weight,
    up_weight,
    down_weight,
):
    shards = lax.axis_size("fsdp")
    parts = lax.axis_size("ctx")
    ctx_index = lax.axis_index("ctx")
    rows = input_gain.shape[0]
    small = pack_small(
        (input_gain, conv_weight, conv_bias, step_bias, decay_log, skip_gain, feed_gain), rows
    )
    pad_cols = 128 - MIX_HEADS - SMALL
    held = rows // LB
    width = gate_weight.shape[1]
    attn_rows = QW // GROUPS
    mix_rows = MIX // GROUPS
    first_all = gather(
        jnp.concatenate(
            [
                key_weight,
                value_weight,
                mixer_in[:, MIX:],
                state_in,
                step_in,
                small,
                jnp.zeros((rows, pad_cols), jnp.bfloat16),
                query_weight,
                mixer_in[:, :MIX],
            ],
            axis=1,
        )
    )
    later = jnp.concatenate(
        [
            side_by_side(
                jnp.concatenate(
                    [
                        attention_out.reshape(held, attn_rows, -1),
                        mixer_out.reshape(held, mix_rows, -1),
                    ],
                    axis=1,
                )
            ),
            hidden_split(gate_weight),
            hidden_split(up_weight),
            side_by_side(down_weight.reshape(held, 2 * LB, -1)),
        ],
        axis=1,
    )
    later = lax.dynamic_slice_in_dim(later, ctx_index * (rows // parts), rows // parts, 0)
    later_all = lax.all_gather(later, ("fsdp", "ctx"), axis=0, tiled=True)
    first_width = 2 * KW + CH + 128
    first_proj = first_all[:, :first_width]
    second_proj = first_all[:, first_width:]
    out_low = later_all[:, :1024]
    out_high = later_all[:, 1024:2048]
    gate_up_proj = later_all[:, 2048 : 2048 + 2 * width]
    down_low = later_all[:, 2048 + 2 * width : 3072 + 2 * width]
    down_high = later_all[:, 3072 + 2 * width :]
    step_at = 2 * KW + CH
    small_at = step_at + MIX_HEADS
    small_all = first_all[:, small_at : small_at + SMALL].astype(jnp.float32)
    small_all = small_all.reshape(shards, rows, SMALL).transpose(0, 2, 1).reshape(shards, -1)
    gain_in32, taps32, shift32, step_shift32, decay32, skip32, feed32 = split_small(
        small_all, shards
    )
    gain_in32 = gain_in32.reshape(-1)
    taps32 = taps32.reshape(shards, CONV, -1).transpose(1, 0, 2).reshape(CONV, CH)
    shift32 = shift32.reshape(-1)
    step_shift32 = step_shift32.reshape(-1)
    decay32 = decay32.reshape(-1)
    skip32 = skip32.reshape(-1)
    feed32 = feed32.reshape(-1)

    row_count = tokens.shape[1]
    half_rows = row_count // 2
    first_start = ctx_index * half_rows
    second_start = (2 * parts - 1 - ctx_index) * half_rows
    offsets = jnp.arange(half_rows, dtype=jnp.int32)
    places = jnp.concatenate([first_start + offsets, second_start + offsets])
    bounds = jnp.cumsum(lengths[0])
    doc_starts = jnp.max(
        jnp.where(bounds[None, :-1] <= places[:, None], bounds[None, :-1], 0), axis=1
    )
    row_limits = jnp.tile(
        jnp.stack([places, doc_starts]).reshape(2, 2, half_rows).transpose(1, 0, 2), (1, 1, HEADS)
    )
    own = ctx_index.reshape(1).astype(jnp.int32)
    cosine, sine_part = rope_tables(places)

    x_own = tokens[0]
    x_ext = jnp.concatenate(
        [x_own, ring_up(x_own[half_rows - 8 : half_rows]), ring_down(x_own[row_count - 8 :])]
    ).astype(jnp.float32)
    normed_ext = rms_scale(x_ext, gain_in32).astype(jnp.bfloat16)
    normed = normed_ext[:row_count]
    first_pre = product(normed_ext, first_proj)
    keys_rot = rotate(first_pre[:row_count, :KW], cosine, sine_part, 1.0).astype(jnp.bfloat16)
    values_low = first_pre[:row_count, KW : 2 * KW].astype(jnp.bfloat16)
    kv_own = jnp.concatenate([keys_rot, values_low], axis=1)
    holders = jnp.arange(parts, dtype=jnp.int32)[:, None, None]
    kv_all = exchange(jnp.where(holders > ctx_index, kv_own[:half_rows], kv_own[half_rows:]))
    starts_col = jnp.broadcast_to(doc_starts[:, None], (row_count, 128)).astype(jnp.int32)
    pad_heads = 128 - MIX_HEADS
    head_terms = jnp.pad(jnp.stack([step_shift32, decay32]), ((0, 6), (0, pad_heads)))
    taps_pad = jnp.pad(taps32, ((0, 4), (0, 0)))
    shift_row = shift32[None]
    skip_row = jnp.repeat(skip32, MIX_DIM)[None]
    conv_out, steps, sums, states, block_decay = kernel_call(
        mix_in_kernel,
        "mix_in",
        (
            ((row_count, CH), jnp.bfloat16),
            ((row_count, 128), jnp.float32),
            ((row_count, 128), jnp.float32),
            ((parts, 2, SLICE + EXTRA, STATE), jnp.bfloat16),
            ((2, 128), jnp.float32),
        ),
        (((LB + 8, CH), jnp.float32),),
        (own, first_pre, starts_col, taps_pad, shift_row, head_terms),
    )

    entries, factors = plain_call(
        scan_kernel,
        "state_scan",
        (
            ((parts, 2, SLICE, STATE), jnp.bfloat16),
            ((2, 128, 128), jnp.float32),
        ),
        (((128, 128), jnp.float32),),
        (exchange(states),),
    )
    entries = exchange(entries)

    second_pre = product(normed, second_proj)
    queries = rotate(second_pre[:, :QW], cosine, sine_part, 1.0).astype(jnp.bfloat16)
    gate_z = second_pre[:, QW:].astype(jnp.bfloat16)
    attended_low, log_totals = attend(own, row_limits, queries, kv_all, kv_own)

    scanned, branch_low, branch_high = kernel_call(
        mix_out_kernel,
        "mix_out",
        (
            ((row_count, MIX), jnp.float32),
            ((row_count, GROUPS * LB), jnp.bfloat16),
            ((row_count, GROUPS * LB), jnp.bfloat16),
        ),
        (),
        (own, conv_out, steps, sums, starts_col, skip_row, entries, gate_z, attended_low),
    )
    x_rows = x_ext[:row_count]
    middle = x_rows + product(branch_low, out_low) + product(branch_high, out_high)
    normed_ff = rms_scale(middle, feed32).astype(jnp.bfloat16)
    gate_up = product(normed_ff, gate_up_proj)
    gate_vals = gate_up[:, :width]
    up_vals = gate_up[:, width:]
    activ = (jax.nn.silu(gate_vals) * up_vals).astype(jnp.bfloat16)
    activ_low = activ[:, :1024]
    activ_high = activ[:, 1024:]
    output = (
        middle + product(activ_low, down_low) + product(activ_high, down_high)
    ).astype(jnp.bfloat16)

    upstream = cotangent[0]
    d_activ = jnp.concatenate(
        [right_product(upstream, down_low), right_product(upstream, down_high)], axis=1
    )
    sig_gate = jax.nn.sigmoid(gate_vals)
    d_gate = d_activ * up_vals * sig_gate * (1.0 + gate_vals * (1.0 - sig_gate))
    d_up = d_activ * gate_vals * sig_gate
    d_gate_up = jnp.concatenate([d_gate, d_up], axis=1).astype(jnp.bfloat16)
    third_shard = scatter(
        stacked_gradients(
            ((normed_ff, d_gate_up), (activ_low, upstream), (activ_high, upstream)),
            512,
            "third_gradients",
        )
    )
    d_normed_ff = right_product(d_gate_up, gate_up_proj)
    _, feed_pull = jax.vjp(rms_scale, middle, feed32)
    d_middle_norm, d_feed_gain = feed_pull(d_normed_ff)
    d_middle = upstream.astype(jnp.float32) + d_middle_norm
    d_middle_low = d_middle.astype(jnp.bfloat16)
    d_branch_low = right_product(d_middle_low, out_low).astype(jnp.bfloat16)
    d_branch_high = right_product(d_middle_low, out_high).astype(jnp.bfloat16)

    d_queries, d_kv, d_kv_near = attend_back(
        own, row_limits, queries, kv_all, kv_own, attended_low, log_totals, d_branch_low
    )
    d_query_pre = rotate(d_queries, cosine, sine_part, -1.0).astype(jnp.bfloat16)

    d_gate_z, d_values_part, d_entries, d_keys_part, d_sums, d_steps, d_skip_cols = streamed_call(
        mix_back_kernel,
        "mix_back",
        (
            ((row_count, MIX), jnp.bfloat16),
            ((row_count, MIX), jnp.float32),
            ((parts, 2, SLICE, STATE), jnp.bfloat16),
            ((row_count, 2 * STATE), jnp.float32),
            ((row_count, 128), jnp.float32),
            ((row_count, 128), jnp.float32),
            ((2, MIX), jnp.float32),
        ),
        (((128, 128), jnp.float32), ((128, 128), jnp.float32)),
        (own, conv_out, steps, sums, starts_col, skip_row, entries, gate_z, scanned, d_branch_low, d_branch_high),
    )
    d_second = jnp.concatenate([d_query_pre, d_gate_z], axis=1)
    seen_back = exchange(d_entries)
    second_total = stacked_gradients(
        ((normed_ext, d_second), (branch_low, d_middle_low), (branch_high, d_middle_low)),
        512,
        "second_gradients",
    )
    second_total, seen_back = lax.optimization_barrier((second_total, seen_back))
    second_shard = scatter(second_total)
    (afters,) = plain_call(
        scan_back_kernel,
        "state_scan_back",
        (((parts, 2, SLICE, STATE), jnp.bfloat16),),
        (),
        (seen_back, factors),
    )
    afters = exchange(afters)
    d_kv, afters = lax.optimization_barrier((d_kv, afters))
    d_kv_seen = exchange(d_kv)
    third_shard, d_kv_seen = lax.optimization_barrier((third_shard, d_kv_seen))
    early_pieces = sum_pieces(jnp.concatenate([third_shard, second_shard], axis=1))
    early_pieces = hidden_pieces(early_pieces, width)
    d_kv_seen = d_kv_seen.astype(jnp.float32)
    d_kv_own = d_kv_near + jnp.concatenate(
        [
            jnp.sum(jnp.where(holders > ctx_index, d_kv_seen, 0.0), axis=0),
            jnp.sum(jnp.where(holders < ctx_index, d_kv_seen, 0.0), axis=0),
        ]
    )
    d_key_pre = rotate(d_kv_own[:, :KW], cosine, sine_part, -1.0)
    d_kv_pre = jnp.concatenate([d_key_pre, d_kv_own[:, KW:]], axis=1).astype(jnp.bfloat16)
    d_main, d_taps_all, d_heads = streamed_call(
        mix_end_kernel,
        "mix_end",
        (
            ((row_count + 16, CH + 128), jnp.bfloat16),
            ((8, CH), jnp.float32),
            ((8, 128), jnp.float32),
        ),
        (
            ((LB + 8, CH), jnp.float32),
            ((LB + 8, CH), jnp.float32),
            ((LB, CH), jnp.float32),
            ((128, 128), jnp.float32),
            ((16, CH), jnp.float32),
        ),
        (
            own,
            conv_out,
            steps,
            sums,
            starts_col,
            first_pre,
            taps_pad,
            shift_row,
            head_terms,
            block_decay,
            entries,
            afters,
            d_values_part,
            d_keys_part,
            d_sums,
            d_steps,
        ),
    )
    d_step_shift = d_heads[0, :MIX_HEADS]
    d_decay = d_heads[1, :MIX_HEADS]
    d_skip = d_skip_cols.sum(axis=0).reshape(MIX_HEADS, MIX_DIM).sum(axis=1)
    d_first = jnp.concatenate([jnp.pad(d_kv_pre, ((0, 16), (0, 0))), d_main], axis=1)
    d_normed = right_product(d_first, first_proj) + jnp.pad(
        right_product(d_second, second_proj), ((0, 16), (0, 0))
    )
    _, input_pull = jax.vjp(rms_scale, x_ext, gain_in32)
    d_input_gain = input_pull(d_normed)[1]

    d_taps = (
        d_taps_all[:CONV].reshape(CONV, shards, -1).transpose(1, 0, 2)
    )
    d_small = jnp.concatenate(
        [
            piece.reshape(shards, -1)
            for piece in (
                d_input_gain,
                d_taps,
                d_taps_all[CONV],
                d_step_shift,
                d_decay,
                d_skip,
                d_feed_gain,
            )
        ],
        axis=1,
    )
    d_small = jnp.pad(d_small, ((0, 0), (0, rows * SMALL - d_small.shape[1])))
    small_cols = jnp.pad(
        d_small.reshape(shards, SMALL, rows).transpose(0, 2, 1).reshape(shards * rows, SMALL),
        ((0, 0), (small_at, first_width - small_at - SMALL)),
    )
    first_total = left_product(normed_ext, d_first) + small_cols
    first_total, d_normed = lax.optimization_barrier((first_total.astype(jnp.bfloat16), d_normed))
    first_shard = scatter(first_total)
    d_rows_norm = input_pull(d_normed)[0]
    edge_low = ring_down(d_rows_norm[row_count : row_count + 8])
    edge_high = ring_up(d_rows_norm[row_count + 8 :])
    input_grad = d_middle + d_rows_norm[:row_count]
    input_grad = input_grad.at[half_rows - 8 : half_rows].add(edge_low)
    input_grad = input_grad.at[row_count - 8 :].add(edge_high)[None]
    inner = turn_gather(early_pieces, 1, 4)
    moved = turn_moves(inner, 4, 4)
    first_shard, early_pieces = lax.optimization_barrier((first_shard, early_pieces))
    first_pieces = sum_pieces(first_shard)
    moved, first_pieces = lax.optimization_barrier((moved, first_pieces))
    early_own = turn_place(inner, moved, 4, 4).reshape(rows, -1)
    third_own = early_own[:, : 2 * width + 2048].astype(jnp.float32)
    second_own = early_own[:, 2 * width + 2048 :]
    first_own = spread(first_pieces, "ctx")
    (
        grad_query,
        grad_key,
        grad_value,
        grad_attn,
        grad_mixer,
        grad_state,
        grad_step_in,
        grad_out,
        small_turned,
    ) = plain_call(
        finish_kernel,
        "finish",
        tuple(
            (shape, jnp.float32)
            for shape in (
                (rows, QW),
                (rows, KW),
                (rows, KW),
                attention_out.shape,
                (rows, 2 * MIX),
                (rows, 2 * STATE),
                (rows, MIX_HEADS),
                mixer_out.shape,
                (128, rows),
            )
        ),
        (),
        (first_own.reshape(rows, -1), second_own),
    )
    grad_gain, grad_taps, grad_shift, grad_step, grad_decay, grad_skip, grad_feed = split_small(
        small_turned[MIX_HEADS : MIX_HEADS + SMALL].reshape(-1), shards
    )
    return (
        output[None],
        input_grad,
        grad_gain,
        grad_query,
        grad_key,
        grad_value,
        grad_attn,
        grad_mixer,
        grad_state,
        grad_step_in,
        grad_taps.reshape(CONV, -1),
        grad_shift,
        grad_step,
        grad_decay,
        grad_skip,
        grad_out,
        grad_feed,
        third_own[:, :width],
        third_own[:, width : 2 * width],
        one_above(third_own[:, 2 * width :]).reshape(-1, 1024),
    )


def solution(mesh):
    return jax.shard_map(
        local,
        mesh=mesh,
        in_specs=(
            P("fsdp", "ctx", None),
            P("fsdp", "ctx", None),
            P("fsdp", None),
            P("fsdp"),
            P("fsdp", None),
            P("fsdp", None),
            P("fsdp", None),
            P("fsdp", None),
            P("fsdp", None),
            P("fsdp", None),
            P("fsdp", None),
            P(None, "fsdp"),
            P("fsdp"),
            P("fsdp"),
            P("fsdp"),
            P("fsdp"),
            P("fsdp", None),
            P("fsdp"),
            P("fsdp", None),
            P("fsdp", None),
            P("fsdp", None),
        ),
        out_specs=(
            P("fsdp", "ctx", None),
            P("fsdp", "ctx", None),
            P("fsdp"),
            P("fsdp", None),
            P("fsdp", None),
            P("fsdp", None),
            P("fsdp", None),
            P("fsdp", None),
            P("fsdp", None),
            P("fsdp", None),
            P(None, "fsdp"),
            P("fsdp"),
            P("fsdp"),
            P("fsdp"),
            P("fsdp"),
            P("fsdp", None),
            P("fsdp"),
            P("fsdp", None),
            P("fsdp", None),
            P("fsdp", None),
        ),
        check_vma=False,
    )
```
